128 devices in a mesh: seq: 4 (over x), shard: 32 (over z, y, core).
Axes of the slice: x: 4, y: 4, z: 4, core: 2. Of those that a mesh axis runs over, the one named last changes fastest.
Arguments:
- inputs: bfloat16 [32, 2048, 768], P('shard', 'seq'), may hold values from -6 to 6
- positions: int32 [32, 2048], P('shard', 'seq'), may hold values from 0 to 2045, as said below
- first_gain: bfloat16 [768], P('shard'), may hold values from 0.5 to 1.5
- first_shift: bfloat16 [768], P('shard'), may hold values from -1 to 1
- second_gain: bfloat16 [768], P('shard'), may hold values from 0.5 to 1.5
- second_shift: bfloat16 [768], P('shard'), may hold values from -1 to 1
- mix_weight: bfloat16 [768, 2304], P('shard'), may hold values from -0.21875 to 0.21875
- mix_bias: bfloat16 [2304], P('shard'), may hold values from -1 to 1
- out_weight: bfloat16 [768, 768], P('shard'), may hold values from -0.875 to 0.875
- out_bias: bfloat16 [768], P('shard'), may hold values from -1 to 1
- up_weight: bfloat16 [768, 3072], P('shard'), may hold values from -0.21875 to 0.21875
- up_bias: bfloat16 [3072], P('shard'), may hold values from -1 to 1
- down_weight: bfloat16 [3072, 768], P('shard'), may hold values from -0.109375 to 0.109375
- down_bias: bfloat16 [768], P('shard'), may hold values from -1 to 1
- cotangent: bfloat16 [32, 2048, 768], P('shard', 'seq'), may hold values from -6 to 6
Outputs:
- outputs: bfloat16 [32, 2048, 768], P('shard', 'seq')
- input_grad: bfloat16 [32, 2048, 768], P('shard', 'seq')
- grad_first_gain: float32 [768], P('shard')
- grad_first_shift: float32 [768], P('shard')
- grad_second_gain: float32 [768], P('shard')
- grad_second_shift: float32 [768], P('shard')
- grad_mix_weight: float32 [768, 2304], P('shard')
- grad_mix_bias: float32 [2304], P('shard')
- grad_out_weight: float32 [768, 768], P('shard')
- grad_out_bias: float32 [768], P('shard')
- grad_up_weight: float32 [768, 3072], P('shard')
- grad_up_bias: float32 [3072], P('shard')
- grad_down_weight: float32 [3072, 768], P('shard')
- grad_down_bias: float32 [768], P('shard')
The draws below stay inside these ranges and needn't reach their ends.
Inputs may be any that keep to these rules, and one draw needn't show every extreme that they name: Each sequence is three documents laid end to end, positions counting 0, 1, 2, ... from each document's start; the middle document starts within the first 512 tokens, after the first token, and ends within the last 512, before the last token. In one sequence, drawn from the seed, the middle document runs from token 1 to token 2046.
All inputs are finite; a program needn't handle non-finite values.
Results may differ from the reference program's by a relative error of at most 0.02.
Values may be sent and summed in bfloat16 or wider, within the bound.
A program may use at most 192 MiB of HBM per device.

```python
import math
import jax
import jax.numpy as jnp
from jax import lax

D = 768
FF = 3072
H = 12
HD = 64
ROT = 16
TOK_DEV = 512
LEN = 2048
NSEQ = 32


def draw_positions(key, part):
    key = jax.random.fold_in(key, 7)
    first_key, second_key, third_key = jax.random.split(key, 3)
    start = jax.random.randint(first_key, (NSEQ, 1), 1, TOK_DEV)
    finish = LEN - jax.random.randint(second_key, (NSEQ, 1), 1, TOK_DEV)
    chosen = jax.random.randint(third_key, (), 0, NSEQ)
    which = jnp.arange(NSEQ, dtype=jnp.int32)[:, None] == chosen
    start = jnp.where(which, 1, start)
    finish = jnp.where(which, LEN - 1, finish)
    index = jnp.arange(LEN, dtype=jnp.int32)[None, :]
    placed = jnp.where(index < start, index, jnp.where(index < finish, index - start, index - finish))
    return placed.astype(jnp.int32)


def level_of(key, dims, shards, low, top_value):
    factor_of = 1.0
    for position, blocks in shards:
        draws = jax.random.uniform(jax.random.fold_in(jax.random.fold_in(key, 6), position), (blocks,), jnp.float32, low / len(shards), top_value / len(shards))
        factor_of = factor_of * jnp.repeat(jnp.exp(draws), dims[position] // blocks).reshape((-1,) + (1,) * (len(dims) - 1 - position))
    return factor_of


def centred(stream_key, dims, spread, limit, cuts=(), kind=jnp.bfloat16):
    level = level_of(stream_key, dims, cuts, -0.22, 0.18) if cuts else 1.0
    values = jax.random.normal(stream_key, dims, jnp.float32) * spread * level
    return jnp.minimum(jnp.maximum(values, -limit), limit).astype(kind)


def setup_inputs(seed: int = 0) -> dict:
    streams_of = jax.random.split(jax.random.key(seed), 16)
    inputs = centred(streams_of[0], (NSEQ, LEN, D), 1.0, 6.0, ((0, 32), (1, 4)))
    positions = draw_positions(jax.random.fold_in(streams_of[15], 71), 0)
    first_gain = jnp.clip(1.0 + 0.1 * jax.random.normal(streams_of[2], (D,), jnp.float32), 0.5, 1.5).astype(jnp.bfloat16)
    first_shift = centred(streams_of[3], (D,), 0.2, 1.0, ((0, 32),))
    second_gain = jnp.clip(1.0 + 0.1 * jax.random.normal(streams_of[4], (D,), jnp.float32), 0.5, 1.5).astype(jnp.bfloat16)
    second_shift = centred(streams_of[5], (D,), 0.2, 1.0, ((0, 32),))
    mix_weight = centred(streams_of[6], (D, 3 * D), D ** -0.5, 0.21875, ((0, 32),))
    mix_bias = centred(streams_of[7], (3 * D,), 0.2, 1.0, ((0, 32),))
    out_weight = centred(streams_of[8], (D, D), (D // 16) ** -0.5, 0.875, ((0, 32),))
    out_bias = centred(streams_of[9], (D,), 0.2, 1.0, ((0, 32),))
    up_weight = centred(streams_of[10], (D, FF), D ** -0.5, 0.21875, ((0, 32),))
    up_bias = centred(streams_of[11], (FF,), 0.2, 1.0, ((0, 32),))
    down_weight = centred(streams_of[12], (FF, D), FF ** -0.5, 0.109375, ((0, 32),))
    down_bias = centred(streams_of[13], (D,), 0.2, 1.0, ((0, 32),))
    cotangent = centred(streams_of[14], (NSEQ, LEN, D), 1.0, 6.0, ((0, 32), (1, 4)))
    return dict(inputs=inputs, positions=positions, first_gain=first_gain, first_shift=first_shift, second_gain=second_gain, second_shift=second_shift, mix_weight=mix_weight, mix_bias=mix_bias, out_weight=out_weight, out_bias=out_bias, up_weight=up_weight, up_bias=up_bias, down_weight=down_weight, down_bias=down_bias, cotangent=cotangent)


@jax.custom_vjp
def low(v):
    return lax.optimization_barrier(v.astype(jnp.bfloat16)).astype(jnp.float32)

@jax.custom_vjp
def low_back(v):
    return v

def low_keep(v):
    return (low(v), None)

def low_pass(kept, grad):
    return (grad,)

def back_keep(v):
    return (v, None)

def back_low(kept, grad):
    return (low(grad),)
low.defvjp(low_keep, low_pass)
low_back.defvjp(back_keep, back_low)
precise = lax.Precision.HIGHEST

def norm_layer(rows, gain, shift):
    centered = rows - lax.optimization_barrier(jnp.mean(rows, axis=-1, keepdims=True))
    inverse = lax.rsqrt(lax.optimization_barrier(jnp.mean(centered * centered, axis=-1, keepdims=True)) + 1e-05)
    return centered * inverse * gain + shift

def rotary_tables(places):
    freqs = 10000.0 ** (-jnp.arange(0, ROT, 2, dtype=jnp.float32) / ROT)
    angles = places.astype(jnp.float32)[:, None] * freqs[None, :]
    angles = jnp.concatenate([angles, angles], axis=-1)
    return (jnp.cos(angles), jnp.sin(angles))

def rotate(values, cosine, sine):
    half = ROT // 2
    turned = values[..., :ROT]
    swapped = jnp.concatenate([-turned[..., half:], turned[..., :half]], axis=-1)
    turned = turned * cosine[:, None, :] + swapped * sine[:, None, :]
    return jnp.concatenate([turned, values[..., ROT:]], axis=-1)

def visible(places):
    index = jnp.arange(places.shape[0], dtype=jnp.int32)
    later = index[:, None] >= index[None, :]
    same = places[:, None] - places[None, :] == index[:, None] - index[None, :]
    return later & same

def layer(params, rows, places):
    first_gain, first_shift, second_gain, second_shift, mix_weight, mix_bias, out_weight, out_bias, up_weight, up_bias, down_weight, down_bias = params
    length = rows.shape[0]
    first = low(norm_layer(rows, first_gain, first_shift))
    mixed = low_back(low(jnp.dot(first, mix_weight, precision=precise) + mix_bias))
    mixed = mixed.reshape(length, H, 3, HD)
    cosine, sine = rotary_tables(places)
    queries = low(rotate(mixed[:, :, 0], cosine, sine))
    keys = low(rotate(mixed[:, :, 1], cosine, sine))
    values = mixed[:, :, 2]
    scale = 1.0 / math.sqrt(HD)
    scores = low_back(jnp.einsum('qhd,khd->hqk', queries, keys, precision=precise)) * scale
    scores = jnp.where(visible(places)[None], scores, -1e+30)
    probs = low(jax.nn.softmax(scores, axis=-1))
    context = jnp.einsum('hqk,khd->qhd', probs, values, precision=precise)
    context = low_back(low(context)).reshape(length, D)
    attended = jnp.dot(context, out_weight, precision=precise) + out_bias
    second = low(norm_layer(rows, second_gain, second_shift))
    hidden = low_back(jnp.dot(second, up_weight, precision=precise) + up_bias)
    active = low(jax.nn.gelu(hidden, approximate=False))
    fed = jnp.dot(active, down_weight, precision=precise) + down_bias
    return rows + attended + fed

def reference(inputs, positions, first_gain, first_shift, second_gain, second_shift, mix_weight, mix_bias, out_weight, out_bias, up_weight, up_bias, down_weight, down_bias, cotangent):
    params = tuple((p.astype(jnp.float32) for p in (first_gain, first_shift, second_gain, second_shift, mix_weight, mix_bias, out_weight, out_bias, up_weight, up_bias, down_weight, down_bias)))

    def one_sequence(totals, item):
        rows, places, grad_rows = item
        result, pull = jax.vjp(lambda prm, given: layer(prm, given, places), params, rows.astype(jnp.float32))
        param_grads, row_grads = pull(grad_rows.astype(jnp.float32))
        totals = jax.tree.map(jnp.add, totals, param_grads)
        return (totals, (result.astype(jnp.bfloat16), row_grads.astype(jnp.bfloat16)))
    zeros = jax.tree.map(jnp.zeros_like, params)
    totals, (outputs, input_grad) = lax.scan(one_sequence, zeros, (inputs, positions, cotangent))
    return (outputs, input_grad, totals[0], totals[1], totals[2], totals[3], totals[4], totals[5], totals[6], totals[7], totals[8], totals[9], totals[10], totals[11])
```

```python
import functools

import jax
import jax.numpy as jnp
from jax import lax
from jax.experimental import pallas as pl
from jax.experimental.pallas import tpu as pltpu
from jax.sharding import PartitionSpec as P

HD = 64
ROT = 16
NX = 4
BF = jnp.bfloat16
F32 = jnp.float32
MESH = pl.DeviceIdType.MESH
NT = (((1,), (1,)), ((), ()))
VMEM_LIMIT = 56 * 1024 * 1024
WIDE = 1536
PAIR = 48


def dot(a, b):
    return jnp.dot(a, b, preferred_element_type=F32)


def dot_nt(a, b):
    return lax.dot_general(a, b, NT, preferred_element_type=F32)


def dot_tn(a, b):
    return lax.dot_general(a, b, (((0,), (0,)), ((), ())), preferred_element_type=F32)


def places():
    x = lax.axis_index("seq")
    s = lax.axis_index("shard")
    return x, s // 8, (s // 2) % 4, s % 2


def at(x, z, y, c):
    return (x, (z * 4 + y) * 2 + c)


def gather_kernel(
    rows_ref, pair_ref, pos_ref, all_ref, mine_ref, other_ref, posall_ref, s1, r1, s2, r2, s3, r3, sx, rx, sf, rf, sp, rp, loc
):
    x, z, y, c = places()
    is0 = c == 0
    right, left, far = lax.rem(x + 1, 4), lax.rem(x + 3, 4), lax.rem(x + 2, 4)
    me = lax.axis_index("shard")

    def first(k):
        return at(x, jnp.where(is0, z, lax.rem(z + k, 4)), jnp.where(is0, lax.rem(y + k, 4), y), c)

    def second(k):
        return at(x, jnp.where(is0, lax.rem(z + k, 4), z), jnp.where(is0, y, lax.rem(y + k, 4)), c)

    def block(dz, dy):
        return lax.rem(z + dz, 4) * 4 + lax.rem(y + dy, 4)

    def held(a, b):
        da, db = (4 - a) % 4, (4 - b) % 4
        return jnp.where(is0, block(db, da), block(da, db))

    def rows_of(ref, b):
        return ref.at[pl.ds(pl.multiple_of(b * PAIR, 16), PAIR)]

    sibling = (x, me + 1 - 2 * c)
    barrier = pltpu.get_barrier_semaphore()
    peers = [first(k) for k in (1, 2, 3)] + [second(k) for k in (1, 2, 3)]
    peers += [sibling, (right, me), (left, me), (far, me)]
    for peer in peers:
        pl.semaphore_signal(barrier, inc=1, device_id=peer, device_id_type=MESH)
    pl.semaphore_wait(barrier, len(peers))

    def remote(src, dst, ss, rs, dev):
        return pltpu.make_async_remote_copy(
            src_ref=src, dst_ref=dst, send_sem=ss, recv_sem=rs, device_id=dev, device_id_type=MESH
        )

    def quarter(ref, who, q):
        return ref.at[pl.ds(pl.multiple_of(who * 512 + q * 128, 128), 128)]

    own = [rows_ref.at[pl.ds(q * 128, 128)] for q in range(4)]
    sends = []
    recvs_r, recvs_l = {}, {}
    for i in range(4):
        q = i
        a = remote(own[q], quarter(all_ref, x, q), sx.at[0, q], rx.at[0, q], (right, me))
        a.start()
        q = 3 - i
        b = remote(own[q], quarter(all_ref, x, q), sx.at[1, q], rx.at[1, q], (left, me))
        b.start()
        sends += [a, b]
    first_copies = []
    own_block = z * 4 + y
    started = []
    order = (1, 3, 2)
    for k in order:
        cp = remote(pair_ref, rows_of(mine_ref, own_block), s1.at[k - 1], r1.at[k - 1], first(k))
        cp.start()
        started.append(cp)
    for k in order:
        cp = remote(pair_ref, rows_of(mine_ref, own_block), s2.at[0, k - 1], r2.at[0, k - 1], second(k))
        cp.start()
        started.append(cp)
    for k in order:
        dev = (lax.rem(x + k, 4), me)
        cp = remote(pos_ref, posall_ref.at[pl.ds(pl.multiple_of(x * 8, 8), 8)], sp.at[k - 1], rp.at[k - 1], dev)
        cp.start()
        started.append(cp)
    cp = remote(pair_ref, rows_of(other_ref, own_block), s3.at[0, 0], r3.at[0, 0], sibling)
    cp.start()
    started.append(cp)
    l0 = pltpu.make_async_copy(rows_ref, all_ref.at[pl.ds(pl.multiple_of(x * 512, 512), 512)], loc.at[0])
    l1 = pltpu.make_async_copy(pair_ref, rows_of(mine_ref, own_block), loc.at[1])
    l2 = pltpu.make_async_copy(pos_ref, posall_ref.at[pl.ds(pl.multiple_of(x * 8, 8), 8)], loc.at[2])
    for cp in (l0, l1, l2):
        cp.start()

    def landed(dst, sem):
        remote(dst, dst, sem, sem, sibling).wait_recv()

    for k in order:
        b = held(k, 0)
        landed(rows_of(mine_ref, b), r1.at[k - 1])
        for j in order:
            cp = remote(rows_of(mine_ref, b), rows_of(mine_ref, b), s2.at[k, j - 1], r2.at[k, j - 1], second(j))
            cp.start()
            started.append(cp)
        cp = remote(rows_of(mine_ref, b), rows_of(other_ref, b), s3.at[k, 0], r3.at[k, 0], sibling)
        cp.start()
        started.append(cp)
    for i in range(2):
        q = i
        landed(quarter(all_ref, left, q), rx.at[0, q])
        a = remote(quarter(all_ref, left, q), quarter(all_ref, left, q), sf.at[0, i], rf.at[0, i], (right, me))
        a.start()
        q = 3 - i
        landed(quarter(all_ref, right, q), rx.at[1, q])
        b = remote(quarter(all_ref, right, q), quarter(all_ref, right, q), sf.at[1, i], rf.at[1, i], (left, me))
        b.start()
        started += [a, b]
    for j in order:
        for k in (0,) + order:
            b = held(k, j)
            landed(rows_of(mine_ref, b), r2.at[k, j - 1])
            cp = remote(rows_of(mine_ref, b), rows_of(other_ref, b), s3.at[k, j], r3.at[k, j], sibling)
            cp.start()
            started.append(cp)
    for a in range(4):
        for b in range(4):
            da, db = (4 - a) % 4, (4 - b) % 4
            blk = jnp.where(is0, block(da, db), block(db, da))
            landed(rows_of(other_ref, blk), r3.at[a, b])
    for i in range(2):
        landed(quarter(all_ref, left, 2 + i), rx.at[0, 2 + i])
        landed(quarter(all_ref, right, i), rx.at[1, i])
    for i in range(2):
        landed(quarter(all_ref, far, i), rf.at[0, i])
        landed(quarter(all_ref, far, 3 - i), rf.at[1, i])
    for k in order:
        src = lax.rem(x + 4 - k, 4)
        landed(posall_ref.at[pl.ds(pl.multiple_of(src * 8, 8), 8)], rp.at[k - 1])
    for cp in (l0, l1, l2):
        cp.wait()
    for cp in sends + started:
        cp.wait_send()


def gather(rows, pair, pos):
    any_spec = pl.BlockSpec(memory_space=pl.ANY)
    dma = pltpu.SemaphoreType.DMA
    return pl.pallas_call(
        gather_kernel,
        out_shape=(
            jax.ShapeDtypeStruct((2048, 768), BF),
            jax.ShapeDtypeStruct((768, WIDE), BF),
            jax.ShapeDtypeStruct((768, WIDE), BF),
            jax.ShapeDtypeStruct((32, 128), jnp.int32),
        ),
        in_specs=[any_spec] * 3,
        out_specs=[any_spec] * 4,
        scratch_shapes=[
            dma((3,)), dma((3,)), dma((4, 3)), dma((4, 3)), dma((4, 4)), dma((4, 4)),
            dma((2, 4)), dma((2, 4)), dma((2, 2)), dma((2, 2)), dma((3,)), dma((3,)), dma((3,)),
        ],
        compiler_params=pltpu.CompilerParams(
            collective_id=0, has_side_effects=True, vmem_limit_bytes=VMEM_LIMIT
        ),
        name="gather_all",
    )(rows, pair, pos)


def scatter_kernel(mine_ref, other_ref, out_ref, first_in, total, second_in, part, third_in, s0, r0, s1, r1, s2, r2):
    x, z, y, c = places()
    is0 = c == 0
    me = lax.axis_index("shard")
    sibling = (x, me + 1 - 2 * c)

    def first(k):
        return at(x, jnp.where(is0, lax.rem(z + k, 4), z), jnp.where(is0, y, lax.rem(y + k, 4)), c)

    def second(k):
        return at(x, jnp.where(is0, z, lax.rem(z + k, 4)), jnp.where(is0, lax.rem(y + k, 4), y), c)

    here1 = jnp.where(is0, z, y)
    here2 = jnp.where(is0, y, z)

    def rows(a, b, flip):
        blk = jnp.where(is0 != flip, a * 4 + b, b * 4 + a)
        return pl.ds(pl.multiple_of(blk * PAIR, 16), PAIR)

    barrier = pltpu.get_barrier_semaphore()
    peers = [first(k) for k in (1, 2, 3)] + [second(k) for k in (1, 2, 3)] + [sibling]
    for peer in peers:
        pl.semaphore_signal(barrier, inc=1, device_id=peer, device_id_type=MESH)
    pl.semaphore_wait(barrier, len(peers))

    def remote(src, dst, ss, rs, dev):
        return pltpu.make_async_remote_copy(
            src_ref=src, dst_ref=dst, send_sem=ss, recv_sem=rs, device_id=dev, device_id_type=MESH
        )

    started = []
    order = (1, 3, 2, 0)
    sib1, sib2 = here2, here1
    for k in order:
        for b in range(4):
            r = rows(lax.rem(sib1 + k, 4), b, True)
            cp = remote(other_ref.at[r], first_in.at[r], s0.at[k, b], r0.at[k, b], sibling)
            cp.start()
            started.append(cp)
    for k in order:
        place = lax.rem(here1 + k, 4)
        for b in range(4):
            r = rows(place, b, False)
            remote(first_in.at[r], first_in.at[r], s0.at[k, b], r0.at[k, b], sibling).wait_recv()
            total[r] = (mine_ref[r].astype(F32) + first_in[r].astype(F32)).astype(BF)
            if k:
                cp = remote(total.at[r], second_in.at[k - 1, b], s1.at[k - 1, b], r1.at[k - 1, b], first(k))
                cp.start()
                started.append(cp)
    for j in order:
        b = lax.rem(here2 + j, 4)
        r = rows(here1, b, False)
        acc = total[r].astype(F32)
        for k in (1, 3, 2):
            slot = second_in.at[k - 1, b]
            remote(slot, slot, s1.at[k - 1, b], r1.at[k - 1, b], sibling).wait_recv()
            acc = acc + second_in[k - 1, b].astype(F32)
        part[j] = acc.astype(BF)
        if j:
            cp = remote(part.at[j], third_in.at[j - 1], s2.at[j - 1], r2.at[j - 1], second(j))
            cp.start()
            started.append(cp)
    acc = part[0].astype(F32)
    for j in (1, 3, 2):
        remote(third_in.at[j - 1], third_in.at[j - 1], s2.at[j - 1], r2.at[j - 1], sibling).wait_recv()
        acc = acc + third_in[j - 1].astype(F32)
    out_ref[...] = acc.astype(BF)
    for cp in started:
        cp.wait_send()


def scatter(mine, other):
    vm = pl.BlockSpec(memory_space=pltpu.VMEM)
    dma = pltpu.SemaphoreType.DMA
    return pl.pallas_call(
        scatter_kernel,
        out_shape=jax.ShapeDtypeStruct((PAIR, WIDE), BF),
        in_specs=[vm, vm],
        out_specs=vm,
        scratch_shapes=[
            pltpu.VMEM((768, WIDE), BF),
            pltpu.VMEM((768, WIDE), BF),
            pltpu.VMEM((3, 4, PAIR, WIDE), BF),
            pltpu.VMEM((4, PAIR, WIDE), BF),
            pltpu.VMEM((3, PAIR, WIDE), BF),
            dma((4, 4)), dma((4, 4)), dma((3, 4)), dma((3, 4)), dma((3,)), dma((3,)),
        ],
        compiler_params=pltpu.CompilerParams(
            collective_id=1, has_side_effects=True, vmem_limit_bytes=VMEM_LIMIT
        ),
        cost_estimate=pl.CostEstimate(flops=0, bytes_accessed=80_000_000, transcendentals=0),
        name="scatter_all",
    )(mine, other)


BQ = 512
NB = 2048 // BQ


def attention_kernel(
    mixed_ref, cos_ref, sin_ref, start_ref, grad_ref, turn_ref, ctx_ref, out_ref,
    qs, ks, vs, qt, es, ss, dkt, dvt, dqs, os, gs,
):
    turn = turn_ref[...]

    @pl.loop(0, NB)
    def _(i):
        r = pl.ds(pl.multiple_of(i * BQ, BQ), BQ)
        cosine, sine = cos_ref[r], sin_ref[r]
        lane = lax.broadcasted_iota(jnp.int32, (BQ, 128), 1)
        for h in range(3):
            q = mixed_ref[r, h * 192 : h * 192 + 64]
            k = mixed_ref[r, h * 192 + 64 : h * 192 + 128]
            v = mixed_ref[r, h * 192 + 128 : h * 192 + 192]
            q = q.astype(F32) * cosine + dot(q, turn) * sine
            k = k.astype(F32) * cosine + dot(k, turn) * sine
            q = q.astype(BF) * 0.125
            qs[h, r] = q
            qt[h, i] = q.astype(F32).T.astype(BF)
            ks[h, r] = k.astype(BF)
            wide = jnp.concatenate([v.astype(F32), jnp.zeros((BQ, 64), F32)], axis=1)
            vs[h, r] = jnp.where((lane == 64) | (lane == 65), 1.0, wide).astype(BF)
            gs[h, r] = grad_ref[r, h * 64 : h * 64 + 64]

    @pl.loop(0, 3)
    def _(h):
        dkt[h] = jnp.zeros((64, 2048), F32)
        dvt[h] = jnp.zeros((64, 2048), F32)
        for i in range(NB):
            r = pl.ds(i * BQ, BQ)
            q = qs[h, r]
            start = start_ref[r]
            top = None
            for b in range(i + 1):
                col = pl.ds(b * BQ, BQ)
                s = dot_nt(q, ks[h, col])
                cols = lax.broadcasted_iota(jnp.int32, (BQ, BQ), 1)
                keep = cols >= start - b * BQ
                if b == i:
                    keep &= cols <= lax.broadcasted_iota(jnp.int32, (BQ, BQ), 0)
                s = jnp.where(keep, s, -1e30)
                ss[:, col] = s
                m = jnp.max(s, axis=-1, keepdims=True)
                top = m if top is None else jnp.maximum(top, m)
            acc = None
            for b in range(i + 1):
                col = pl.ds(b * BQ, BQ)
                e = jnp.exp(ss[:, col] - top).astype(BF)
                es[:, col] = e
                o = dot(e, vs[h, col])
                acc = o if acc is None else acc + o
            inverse = 1.0 / acc[:, 64:65]
            o = acc[:, :64] * inverse
            os[h, r] = o.astype(BF)
            g = gs[h, r].astype(F32) * inverse
            delta = -jnp.sum(g * o, axis=-1, keepdims=True)
            high = delta.astype(BF).astype(F32)
            lane = lax.broadcasted_iota(jnp.int32, (BQ, 128), 1)
            wide = jnp.concatenate([g, jnp.zeros((BQ, 64), F32)], axis=1)
            wide = jnp.where(lane == 64, high, jnp.where(lane == 65, delta - high, wide)).astype(BF)
            gt = g.T.astype(BF)
            dq = None
            for b in range(i + 1):
                col = pl.ds(b * BQ, BQ)
                dp = dot_nt(wide, vs[h, col])
                e = es[:, col]
                ds = (e.astype(F32) * dp).astype(BF)
                part = dot(ds, ks[h, col])
                dq = part if dq is None else dq + part
                dkt[h, :, col] += dot(qt[h, i], ds)
                dvt[h, :, col] += dot(gt, e)
            dqs[h, r] = dq * 0.125

    @pl.loop(0, NB)
    def _(i):
        r = pl.ds(pl.multiple_of(i * BQ, BQ), BQ)
        cosine, sine = cos_ref[r], sin_ref[r]

        def back(g):
            return g * cosine + dot_nt((g * sine).astype(BF), turn)

        parts = []
        for h in range(3):
            parts.append(back(dqs[h, r]))
            parts.append(back(dkt[h, :, r].T))
            parts.append(dvt[h, :, r].T)
        out_ref[r] = jnp.concatenate(parts, axis=1).astype(BF)
        ctx_ref[r] = jnp.concatenate([os[h, r].astype(F32) for h in range(3)], axis=1).astype(BF)


def attention(mixed, cosine, sine, start, grads, turn):
    vm = pl.BlockSpec(memory_space=pltpu.VMEM)
    return pl.pallas_call(
        attention_kernel,
        out_shape=(jax.ShapeDtypeStruct((2048, 192), BF), jax.ShapeDtypeStruct((2048, 576), BF)),
        in_specs=[vm] * 6,
        out_specs=[vm, vm],
        scratch_shapes=[
            pltpu.VMEM((3, 2048, 64), BF),
            pltpu.VMEM((3, 2048, 64), BF),
            pltpu.VMEM((3, 2048, 128), BF),
            pltpu.VMEM((3, NB, 64, BQ), BF),
            pltpu.VMEM((BQ, 2048), BF),
            pltpu.VMEM((BQ, 2048), F32),
            pltpu.VMEM((3, 64, 2048), F32),
            pltpu.VMEM((3, 64, 2048), F32),
            pltpu.VMEM((3, 2048, 64), F32),
            pltpu.VMEM((3, 2048, 64), BF),
            pltpu.VMEM((3, 2048, 64), BF),
        ],
        compiler_params=pltpu.CompilerParams(vmem_limit_bytes=VMEM_LIMIT),
        cost_estimate=pl.CostEstimate(
            flops=30_000_000_000, bytes_accessed=10_000_000, transcendentals=8_000_000
        ),
        name="attention_both",
    )(mixed, cosine, sine, start, grads, turn)


def shift_x(v, k):
    return lax.ppermute(v, "seq", [(i, (i + k) % NX) for i in range(NX)])


def gather_x(v, x):
    got = [(0, v)] + [(k, shift_x(v, k)) for k in (1, 3, 2)]
    full = jnp.zeros((NX,) + v.shape, v.dtype)
    for k, block in got:
        full = lax.dynamic_update_slice(full, block[None], (lax.rem(x + NX - k, NX),) + (0,) * v.ndim)
    return full


def scatter_x(v, x):
    def block(k):
        return lax.dynamic_slice_in_dim(v, lax.rem(x + k, NX) * 512, 512, 0)

    got = [shift_x(block(k), k) for k in (1, 3, 2)]
    total = block(0).astype(F32)
    for part in got:
        total = total + part.astype(F32)
    return total


def swap_core(v):
    return lax.ppermute(v, "shard", [(i, i ^ 1) for i in range(32)])


def local(
    inputs, positions, first_gain, first_shift, second_gain, second_shift, mix_weight, mix_bias,
    out_weight, out_bias, up_weight, up_bias, down_weight, down_bias, cotangent,
):
    x, _, _, c = places()
    is0 = c == 0
    small = jnp.concatenate(
        [
            jnp.stack([first_gain, first_shift, second_gain, second_shift, out_bias, down_bias], 1),
            mix_bias.reshape(24, 3),
            up_bias.reshape(24, 4),
        ],
        axis=1,
    )
    half_a = jnp.concatenate(
        [
            out_weight,
            lax.dynamic_slice_in_dim(mix_weight, x * 576, 576, 1),
            small,
            jnp.zeros((24, WIDE - 768 - 576 - 13), BF),
        ],
        axis=1,
    )
    up_part = lax.dynamic_index_in_dim(up_weight.reshape(24, 32, 4, 24), x, 2, keepdims=False)
    half_b = jnp.concatenate(
        [up_part.reshape(24, 768), lax.dynamic_slice_in_dim(down_weight, x * 24, 24, 0)], axis=1
    )
    kept = jnp.where(is0, half_a, half_b)
    came = swap_core(jnp.where(is0, half_b, half_a))
    pair = jnp.where(is0, jnp.concatenate([kept, came], 0), jnp.concatenate([came, kept], 0))
    pos_own = jnp.concatenate([positions.reshape(4, 128)] * 2, axis=0)
    rows_all, mine, other, pos_all = gather(inputs[0], pair, pos_own)
    grad_low = cotangent[0]
    grads_all = gather_x(grad_low, x).reshape(2048, 768)

    w_a = jnp.where(is0, mine, other)
    w_b = jnp.where(is0, other, mine)
    out_rows = lax.dynamic_slice(w_a, (x * 192, 0), (192, 768))
    mix_w = w_a[:, 768:1344]
    extra = w_a[:, 1344:1408]
    vectors = extra.astype(F32).T
    g1, b1, g2, b2, out_b, down_b = (vectors[i] for i in range(6))
    mixb = lax.dynamic_slice_in_dim(extra[:, 6:9].astype(F32).reshape(2304), x * 576, 576, 0)
    upb = lax.dynamic_index_in_dim(
        extra[:, 9:13].astype(F32).reshape(32, 4, 24), x, 1, keepdims=False
    ).reshape(768)
    up_w, down_w = w_b[:, :768], w_b[:, 768:]

    place = pos_all.reshape(4, 2, 512)[:, 0].reshape(2048)
    freqs = 10000.0 ** (-jnp.arange(0, ROT, 2, dtype=F32) / ROT)
    angles = freqs[:, None] * place.astype(F32)[None, :]
    cos8, sin8 = jnp.cos(angles), jnp.sin(angles)
    cosine = jnp.concatenate([cos8, cos8, jnp.ones((48, 2048), F32)], 0).T
    sine = jnp.concatenate([sin8, sin8, jnp.zeros((48, 2048), F32)], 0).T
    start = (jnp.arange(2048, dtype=jnp.int32) - place)[:, None]
    turn = (jnp.eye(64, k=8) * (jnp.arange(64) >= 8) * (jnp.arange(64) < 16)).astype(BF) - (
        jnp.eye(64, k=-8) * (jnp.arange(64) < 8)
    ).astype(BF)

    rows = rows_all.astype(F32)
    centered = rows - jnp.mean(rows, axis=-1, keepdims=True)
    inverse = lax.rsqrt(jnp.mean(centered * centered, axis=-1, keepdims=True) + 1e-05)
    unit = centered * inverse
    first_low = (unit * g1 + b1).astype(BF)
    second_low = (unit * g2 + b2).astype(BF)
    mixed = (dot(first_low, mix_w) + mixb).astype(BF)
    hidden = dot(second_low, up_w) + upb
    active = jax.nn.gelu(hidden, approximate=False).astype(BF)
    context_grad = dot_nt(grads_all, out_rows).astype(BF)
    context, mix_grad = attention(mixed, cosine, sine, start, context_grad, turn)

    outputs_part = (dot(context, out_rows) + dot(active, down_w)).astype(BF)
    outputs_sum = scatter_x(outputs_part, x)

    active_grad = dot_nt(grads_all, down_w)
    hidden_low = jax.vjp(lambda t: jax.nn.gelu(t, approximate=False), hidden)[1](active_grad)[0].astype(BF)
    second_pull = dot_nt(hidden_low, up_w)
    first_pull = dot_nt(mix_grad, mix_w)
    pulls = (first_pull * g1 + second_pull * g2).astype(BF)
    pulls_sum = scatter_x(pulls, x)

    down_grad = dot_tn(active, grads_all)
    up_grad = dot_tn(second_low, hidden_low)
    out_grad = dot_tn(context, grads_all)
    mix_wgrad = dot_tn(first_low, mix_grad)
    bias_grad = jnp.sum(grad_low.astype(F32), axis=0)
    upb_grad = jnp.sum(hidden_low.astype(F32), axis=0)
    mixb_grad = jnp.sum(mix_grad.astype(F32), axis=0)
    sums = [
        jnp.sum(first_pull * unit, axis=0),
        jnp.sum(first_pull, axis=0),
        jnp.sum(second_pull * unit, axis=0),
        jnp.sum(second_pull, axis=0),
        bias_grad,
    ]
    upb_full = lax.dynamic_update_slice(
        jnp.zeros((32, 4, 24), F32), upb_grad.reshape(32, 1, 24), (0, x, 0)
    ).reshape(768, 4)
    mixb_full = lax.dynamic_update_slice(jnp.zeros((2304,), F32), mixb_grad, (x * 576,)).reshape(768, 3)
    small_grad = jnp.concatenate(
        [jnp.stack(sums, 1), mixb_full, upb_full, jnp.zeros((768, WIDE - 1344 - 12), F32)], axis=1
    )
    out_full = lax.dynamic_update_slice(jnp.zeros((768, 768), BF), out_grad.astype(BF), (x * 192, 0))
    grad_a = jnp.concatenate([out_full, mix_wgrad.astype(BF), small_grad.astype(BF)], axis=1)
    grad_b = jnp.concatenate([up_grad.astype(BF), down_grad.astype(BF)], axis=1)
    reduced = scatter(jnp.where(is0, grad_a, grad_b), jnp.where(is0, grad_b, grad_a))
    low, high = reduced[:24], reduced[24:]
    kept = jnp.where(is0, low, high)
    came = swap_core(jnp.where(is0, high, low))
    shares = jnp.concatenate([jnp.where(is0, kept, came), jnp.where(is0, came, kept)], axis=1)
    shares = gather_x(shares, x).astype(F32)
    got_out = jnp.sum(shares[:, :, :768], axis=0)
    got_mix = shares[:, :, 768:1344].transpose(1, 0, 2).reshape(24, 2304)
    got_small = jnp.sum(shares[:, :, 1344:1356], axis=0)
    got_up = shares[:, :, 1536:2304].reshape(4, 24, 32, 24).transpose(1, 2, 0, 3).reshape(24, 3072)
    got_down = shares[:, :, 2304:].reshape(96, 768)

    outputs = (inputs[0].astype(F32) + outputs_sum + (out_b + down_b)).astype(BF)[None]
    own = inputs[0].astype(F32)
    centered = own - jnp.mean(own, axis=-1, keepdims=True)
    inverse = lax.rsqrt(jnp.mean(centered * centered, axis=-1, keepdims=True) + 1e-05)
    unit = centered * inverse
    back = inverse * (
        pulls_sum
        - jnp.mean(pulls_sum, axis=-1, keepdims=True)
        - unit * jnp.mean(pulls_sum * unit, axis=-1, keepdims=True)
    )
    input_grad = (grad_low.astype(F32) + back).astype(BF)[None]
    return (
        outputs,
        input_grad,
        got_small[:, 0],
        got_small[:, 1],
        got_small[:, 2],
        got_small[:, 3],
        got_mix,
        got_small[:, 5:8].reshape(72),
        got_out,
        got_small[:, 4],
        got_up,
        got_small[:, 8:12].reshape(96),
        got_down,
        got_small[:, 4],
    )


def solution(mesh):
    vec, mat, tok = P("shard"), P("shard", None), P("shard", "seq", None)
    return jax.shard_map(
        local,
        mesh=mesh,
        in_specs=(tok, P("shard", "seq"), vec, vec, vec, vec, mat, vec, mat, vec, mat, vec, mat, vec, tok),
        out_specs=(tok, tok, vec, vec, vec, vec, mat, vec, mat, vec, mat, vec, mat, vec),
        check_vma=False,
    )
```

```python
import functools

import jax
import jax.numpy as jnp
from jax import lax
from jax.experimental import pallas as pl
from jax.experimental.pallas import tpu as pltpu
from jax.sharding import PartitionSpec as P

HD = 64
ROT = 16
NX = 4
BF = jnp.bfloat16
F32 = jnp.float32
MESH = pl.DeviceIdType.MESH
NT = (((1,), (1,)), ((), ()))
VMEM_LIMIT = 56 * 1024 * 1024
WIDE = 1536
PAIR = 48


def dot(a, b):
    return jnp.dot(a, b, preferred_element_type=F32)


def dot_nt(a, b):
    return lax.dot_general(a, b, NT, preferred_element_type=F32)


def dot_tn(a, b):
    return lax.dot_general(a, b, (((0,), (0,)), ((), ())), preferred_element_type=F32)


def places():
    x = lax.axis_index("seq")
    s = lax.axis_index("shard")
    return x, s // 8, (s // 2) % 4, s % 2


def at(x, z, y, c):
    return (x, (z * 4 + y) * 2 + c)


def gather_kernel(
    rows_ref, pair_ref, pos_ref, all_ref, mine_ref, other_ref, posall_ref, s1, r1, s2, r2, s3, r3, sx, rx, sf, rf, sp, rp, loc
):
    x, z, y, c = places()
    is0 = c == 0
    right, left, far = lax.rem(x + 1, 4), lax.rem(x + 3, 4), lax.rem(x + 2, 4)
    me = lax.axis_index("shard")

    def first(k):
        return at(x, jnp.where(is0, z, lax.rem(z + k, 4)), jnp.where(is0, lax.rem(y + k, 4), y), c)

    def second(k):
        return at(x, jnp.where(is0, lax.rem(z + k, 4), z), jnp.where(is0, y, lax.rem(y + k, 4)), c)

    def block(dz, dy):
        return lax.rem(z + dz, 4) * 4 + lax.rem(y + dy, 4)

    def held(a, b):
        da, db = (4 - a) % 4, (4 - b) % 4
        return jnp.where(is0, block(db, da), block(da, db))

    def rows_of(ref, b):
        return ref.at[pl.ds(pl.multiple_of(b * PAIR, 16), PAIR)]

    sibling = (x, me + 1 - 2 * c)
    barrier = pltpu.get_barrier_semaphore()
    peers = [first(k) for k in (1, 2, 3)] + [second(k) for k in (1, 2, 3)]
    peers += [sibling, (right, me), (left, me), (far, me)]
    for peer in peers:
        pl.semaphore_signal(barrier, inc=1, device_id=peer, device_id_type=MESH)
    pl.semaphore_wait(barrier, len(peers))

    def remote(src, dst, ss, rs, dev):
        return pltpu.make_async_remote_copy(
            src_ref=src, dst_ref=dst, send_sem=ss, recv_sem=rs, device_id=dev, device_id_type=MESH
        )

    def quarter(ref, who, q):
        return ref.at[pl.ds(pl.multiple_of(who * 512 + q * 128, 128), 128)]

    own = [rows_ref.at[pl.ds(q * 128, 128)] for q in range(4)]
    sends = []
    recvs_r, recvs_l = {}, {}
    for i in range(4):
        q = i
        a = remote(own[q], quarter(all_ref, x, q), sx.at[0, q], rx.at[0, q], (right, me))
        a.start()
        q = 3 - i
        b = remote(own[q], quarter(all_ref, x, q), sx.at[1, q], rx.at[1, q], (left, me))
        b.start()
        sends += [a, b]
    first_copies = []
    own_block = z * 4 + y
    started = []
    order = (1, 3, 2)
    for k in order:
        cp = remote(pair_ref, rows_of(mine_ref, own_block), s1.at[k - 1], r1.at[k - 1], first(k))
        cp.start()
        started.append(cp)
    for k in order:
        cp = remote(pair_ref, rows_of(mine_ref, own_block), s2.at[0, k - 1], r2.at[0, k - 1], second(k))
        cp.start()
        started.append(cp)
    for k in order:
        dev = (lax.rem(x + k, 4), me)
        cp = remote(pos_ref, posall_ref.at[pl.ds(pl.multiple_of(x * 8, 8), 8)], sp.at[k - 1], rp.at[k - 1], dev)
        cp.start()
        started.append(cp)
    cp = remote(pair_ref, rows_of(other_ref, own_block), s3.at[0, 0], r3.at[0, 0], sibling)
    cp.start()
    started.append(cp)
    l0 = pltpu.make_async_copy(rows_ref, all_ref.at[pl.ds(pl.multiple_of(x * 512, 512), 512)], loc.at[0])
    l1 = pltpu.make_async_copy(pair_ref, rows_of(mine_ref, own_block), loc.at[1])
    l2 = pltpu.make_async_copy(pos_ref, posall_ref.at[pl.ds(pl.multiple_of(x * 8, 8), 8)], loc.at[2])
    for cp in (l0, l1, l2):
        cp.start()

    def landed(dst, sem):
        remote(dst, dst, sem, sem, sibling).wait_recv()

    for k in order:
        b = held(k, 0)
        landed(rows_of(mine_ref, b), r1.at[k - 1])
        for j in order:
            cp = remote(rows_of(mine_ref, b), rows_of(mine_ref, b), s2.at[k, j - 1], r2.at[k, j - 1], second(j))
            cp.start()
            started.append(cp)
        cp = remote(rows_of(mine_ref, b), rows_of(other_ref, b), s3.at[k, 0], r3.at[k, 0], sibling)
        cp.start()
        started.append(cp)
    for i in range(2):
        q = i
        landed(quarter(all_ref, left, q), rx.at[0, q])
        a = remote(quarter(all_ref, left, q), quarter(all_ref, left, q), sf.at[0, i], rf.at[0, i], (right, me))
        a.start()
        q = 3 - i
        landed(quarter(all_ref, right, q), rx.at[1, q])
        b = remote(quarter(all_ref, right, q), quarter(all_ref, right, q), sf.at[1, i], rf.at[1, i], (left, me))
        b.start()
        started += [a, b]
    for j in order:
        for k in (0,) + order:
            b = held(k, j)
            landed(rows_of(mine_ref, b), r2.at[k, j - 1])
            cp = remote(rows_of(mine_ref, b), rows_of(other_ref, b), s3.at[k, j], r3.at[k, j], sibling)
            cp.start()
            started.append(cp)
    for a in range(4):
        for b in range(4):
            da, db = (4 - a) % 4, (4 - b) % 4
            blk = jnp.where(is0, block(da, db), block(db, da))
            landed(rows_of(other_ref, blk), r3.at[a, b])
    for i in range(2):
        landed(quarter(all_ref, left, 2 + i), rx.at[0, 2 + i])
        landed(quarter(all_ref, right, i), rx.at[1, i])
    for i in range(2):
        landed(quarter(all_ref, far, i), rf.at[0, i])
        landed(quarter(all_ref, far, 3 - i), rf.at[1, i])
    for k in order:
        src = lax.rem(x + 4 - k, 4)
        landed(posall_ref.at[pl.ds(pl.multiple_of(src * 8, 8), 8)], rp.at[k - 1])
    for cp in (l0, l1, l2):
        cp.wait()
    for cp in sends + started:
        cp.wait_send()


def gather(rows, pair, pos):
    any_spec = pl.BlockSpec(memory_space=pl.ANY)
    dma = pltpu.SemaphoreType.DMA
    return pl.pallas_call(
        gather_kernel,
        out_shape=(
            jax.ShapeDtypeStruct((2048, 768), BF),
            jax.ShapeDtypeStruct((768, WIDE), BF),
            jax.ShapeDtypeStruct((768, WIDE), BF),
            jax.ShapeDtypeStruct((32, 128), jnp.int32),
        ),
        in_specs=[any_spec] * 3,
        out_specs=[any_spec] * 4,
        scratch_shapes=[
            dma((3,)), dma((3,)), dma((4, 3)), dma((4, 3)), dma((4, 4)), dma((4, 4)),
            dma((2, 4)), dma((2, 4)), dma((2, 2)), dma((2, 2)), dma((3,)), dma((3,)), dma((3,)),
        ],
        compiler_params=pltpu.CompilerParams(
            collective_id=0, has_side_effects=True, vmem_limit_bytes=VMEM_LIMIT
        ),
        name="gather_all",
    )(rows, pair, pos)


BQ = 512
NB = 2048 // BQ


def attention_kernel(
    mixed_ref, cos_ref, sin_ref, start_ref, grad_ref, turn_ref, ctx_ref, out_ref,
    qs, ks, vs, qt, es, ss, dkt, dvt, dqs, os, gs,
):
    turn = turn_ref[...]

    @pl.loop(0, NB)
    def _(i):
        r = pl.ds(pl.multiple_of(i * BQ, BQ), BQ)
        cosine, sine = cos_ref[r], sin_ref[r]
        lane = lax.broadcasted_iota(jnp.int32, (BQ, 128), 1)
        for h in range(3):
            q = mixed_ref[r, h * 192 : h * 192 + 64]
            k = mixed_ref[r, h * 192 + 64 : h * 192 + 128]
            v = mixed_ref[r, h * 192 + 128 : h * 192 + 192]
            q = q.astype(F32) * cosine + dot(q, turn) * sine
            k = k.astype(F32) * cosine + dot(k, turn) * sine
            q = q.astype(BF) * 0.125
            qs[h, r] = q
            qt[h, i] = q.astype(F32).T.astype(BF)
            ks[h, r] = k.astype(BF)
            wide = jnp.concatenate([v.astype(F32), jnp.zeros((BQ, 64), F32)], axis=1)
            vs[h, r] = jnp.where((lane == 64) | (lane == 65), 1.0, wide).astype(BF)
            gs[h, r] = grad_ref[r, h * 64 : h * 64 + 64]

    @pl.loop(0, 3)
    def _(h):
        dkt[h] = jnp.zeros((64, 2048), F32)
        dvt[h] = jnp.zeros((64, 2048), F32)
        for i in range(NB):
            r = pl.ds(i * BQ, BQ)
            q = qs[h, r]
            start = start_ref[r]
            top = None
            for b in range(i + 1):
                col = pl.ds(b * BQ, BQ)
                s = dot_nt(q, ks[h, col])
                cols = lax.broadcasted_iota(jnp.int32, (BQ, BQ), 1)
                keep = cols >= start - b * BQ
                if b == i:
                    keep &= cols <= lax.broadcasted_iota(jnp.int32, (BQ, BQ), 0)
                s = jnp.where(keep, s, -1e30)
                ss[:, col] = s
                m = jnp.max(s, axis=-1, keepdims=True)
                top = m if top is None else jnp.maximum(top, m)
            acc = None
            for b in range(i + 1):
                col = pl.ds(b * BQ, BQ)
                e = jnp.exp(ss[:, col] - top).astype(BF)
                es[:, col] = e
                o = dot(e, vs[h, col])
                acc = o if acc is None else acc + o
            inverse = 1.0 / acc[:, 64:65]
            o = acc[:, :64] * inverse
            os[h, r] = o.astype(BF)
            g = gs[h, r].astype(F32) * inverse
            delta = -jnp.sum(g * o, axis=-1, keepdims=True)
            high = delta.astype(BF).astype(F32)
            lane = lax.broadcasted_iota(jnp.int32, (BQ, 128), 1)
            wide = jnp.concatenate([g, jnp.zeros((BQ, 64), F32)], axis=1)
            wide = jnp.where(lane == 64, high, jnp.where(lane == 65, delta - high, wide)).astype(BF)
            gt = g.T.astype(BF)
            dq = None
            for b in range(i + 1):
                col = pl.ds(b * BQ, BQ)
                dp = dot_nt(wide, vs[h, col])
                e = es[:, col]
                ds = (e.astype(F32) * dp).astype(BF)
                part = dot(ds, ks[h, col])
                dq = part if dq is None else dq + part
                dkt[h, :, col] += dot(qt[h, i], ds)
                dvt[h, :, col] += dot(gt, e)
            dqs[h, r] = dq * 0.125

    @pl.loop(0, NB)
    def _(i):
        r = pl.ds(pl.multiple_of(i * BQ, BQ), BQ)
        cosine, sine = cos_ref[r], sin_ref[r]

        def back(g):
            return g * cosine + dot_nt((g * sine).astype(BF), turn)

        parts = []
        for h in range(3):
            parts.append(back(dqs[h, r]))
            parts.append(back(dkt[h, :, r].T))
            parts.append(dvt[h, :, r].T)
        out_ref[r] = jnp.concatenate(parts, axis=1).astype(BF)
        ctx_ref[r] = jnp.concatenate([os[h, r].astype(F32) for h in range(3)], axis=1).astype(BF)


def attention(mixed, cosine, sine, start, grads, turn):
    vm = pl.BlockSpec(memory_space=pltpu.VMEM)
    return pl.pallas_call(
        attention_kernel,
        out_shape=(jax.ShapeDtypeStruct((2048, 192), BF), jax.ShapeDtypeStruct((2048, 576), BF)),
        in_specs=[vm] * 6,
        out_specs=[vm, vm],
        scratch_shapes=[
            pltpu.VMEM((3, 2048, 64), BF),
            pltpu.VMEM((3, 2048, 64), BF),
            pltpu.VMEM((3, 2048, 128), BF),
            pltpu.VMEM((3, NB, 64, BQ), BF),
            pltpu.VMEM((BQ, 2048), BF),
            pltpu.VMEM((BQ, 2048), F32),
            pltpu.VMEM((3, 64, 2048), F32),
            pltpu.VMEM((3, 64, 2048), F32),
            pltpu.VMEM((3, 2048, 64), F32),
            pltpu.VMEM((3, 2048, 64), BF),
            pltpu.VMEM((3, 2048, 64), BF),
        ],
        compiler_params=pltpu.CompilerParams(vmem_limit_bytes=VMEM_LIMIT),
        cost_estimate=pl.CostEstimate(
            flops=30_000_000_000, bytes_accessed=10_000_000, transcendentals=8_000_000
        ),
        name="attention_both",
    )(mixed, cosine, sine, start, grads, turn)


def tail_kernel(
    ctx_h, ctxt_h, mg_h, act_h, actt_h, dg_h, unitt_h, w_h, vec_ref, ga_h, gb_h, gc_h, gd_h, rows_ref,
    out_ref, back_ref, fin_ref,
    ctx, ctxt, mg, act, actt, hl, unitt, w, g, buf, passed, got, grads, first_in, second_in, part, third_in, col,
    ld, sa, ra, sb, rb, s0, r0, s1, r1, s2, r2, s3, r3, s4, r4,
):
    x, z, y, c = places()
    is0 = c == 0
    me = lax.axis_index("shard")
    right, left = lax.rem(x + 1, 4), lax.rem(x + 3, 4)
    sibling = (x, me + 1 - 2 * c)

    def tok(k):
        return pl.ds(pl.multiple_of(lax.rem(x + 4 - k, 4) * 512, 512), 512)

    loads = []

    def load(src, dst):
        cp = pltpu.make_async_copy(src, dst, ld.at[len(loads)])
        cp.start()
        loads.append(cp)
        return cp

    l_ctx = load(ctx_h, ctx)
    l_w = load(w_h, w)
    l_act = load(act_h, act)
    l_g = [load(s, g.at[tok(k)]) for k, s in enumerate((ga_h, gb_h, gc_h, gd_h))]
    l_dg = load(dg_h, hl)
    l_mg = load(mg_h, mg)
    l_unitt = load(unitt_h, unitt)
    l_actt = load(actt_h, actt)
    l_ctxt = load(ctxt_h, ctxt)

    def first(k):
        return at(x, jnp.where(is0, lax.rem(z + k, 4), z), jnp.where(is0, y, lax.rem(y + k, 4)), c)

    def second(k):
        return at(x, jnp.where(is0, z, lax.rem(z + k, 4)), jnp.where(is0, lax.rem(y + k, 4), y), c)

    here1 = jnp.where(is0, z, y)
    here2 = jnp.where(is0, y, z)

    def rows(a, b, flip):
        blk = jnp.where(is0 != flip, a * 4 + b, b * 4 + a)
        return pl.ds(pl.multiple_of(blk * PAIR, 16), PAIR)

    barrier = pltpu.get_barrier_semaphore()
    peers = [first(k) for k in (1, 2, 3)] + [second(k) for k in (1, 2, 3)] + [sibling]
    peers += [(lax.rem(x + k, 4), me) for k in (1, 2, 3)]
    for peer in peers:
        pl.semaphore_signal(barrier, inc=1, device_id=peer, device_id_type=MESH)
    pl.semaphore_wait(barrier, len(peers))
    started = []

    def remote(src, dst, ss, rs, dev):
        cp = pltpu.make_async_remote_copy(
            src_ref=src, dst_ref=dst, send_sem=ss, recv_sem=rs, device_id=dev, device_id_type=MESH
        )
        return cp

    def send(*args):
        cp = remote(*args)
        cp.start()
        started.append(cp)

    def landed(dst, sem):
        remote(dst, dst, sem, sem, sibling).wait_recv()

    half = [pl.ds(0, 256), pl.ds(256, 256)]
    dev_x = [(right, me), (left, me)]

    def far_send(n):
        for d in range(2):
            send(buf.at[n, 2, half[d]], passed.at[n, d], sa.at[n, d], ra.at[n, d], dev_x[d])

    def near_send(n, d, h):
        send(buf.at[n, 3 - 2 * d, half[h]], got.at[n, d, half[h]], sb.at[n, d, h], rb.at[n, d, h], dev_x[d])

    def pass_on(n):
        for d in range(2):
            landed(passed.at[n, d], ra.at[n, d])
            k = 3 - 2 * d
            buf[n, k, half[d]] = (buf[n, k, half[d]].astype(F32) + passed[n, d].astype(F32)).astype(BF)
            near_send(n, d, d)

    def total(n, h):
        for d in range(2):
            landed(got.at[n, d, half[h]], rb.at[n, d, h])
        return buf[n, 0, half[h]].astype(F32) + got[n, 0, half[h]].astype(F32) + got[n, 1, half[h]].astype(F32)

    out_rows = pl.ds(pl.multiple_of(x * 192, 64), 192)

    def outputs_of(k):
        base = lax.rem(x + 4 - k, 4) * 512

        @pl.loop(0, 2)
        def _(i):
            r = pl.ds(pl.multiple_of(base + i * 256, 256), 256)
            o = dot(ctx[r], w[0, out_rows, 0:768]) + dot(act[r], w[1, :, 768:])
            buf[0, k, pl.ds(pl.multiple_of(i * 256, 256), 256)] = o.astype(BF)

    def pulls_of(k):
        base = lax.rem(x + 4 - k, 4) * 512

        @pl.loop(0, 2)
        def _(i):
            r = pl.ds(pl.multiple_of(base + i * 256, 256), 256)
            ag = dot_nt(g[r], w[1, :, 768:])
            low = (ag * hl[r].astype(F32)).astype(BF)
            hl[r] = low
            s = dot_nt(low, w[1, :, 0:768]) * vec_ref[2:3] + dot_nt(mg[r], w[0, :, 768:1344]) * vec_ref[0:1]
            buf[1, k, pl.ds(pl.multiple_of(i * 256, 256), 256)] = s.astype(BF)

    l_ctx.wait()
    l_w.wait()
    l_act.wait()
    for k in (2, 3, 1, 0):
        outputs_of(k)
        if k == 2:
            far_send(0)
        elif k == 3:
            near_send(0, 0, 1)
        elif k == 1:
            near_send(0, 1, 0)
    for cp in l_g:
        cp.wait()
    l_dg.wait()
    l_mg.wait()
    for k in (2, 3, 1, 0):
        pulls_of(k)
        if k == 2:
            far_send(1)
            pass_on(0)
        elif k == 3:
            near_send(1, 0, 1)
        elif k == 1:
            near_send(1, 1, 0)
    l_unitt.wait()
    l_actt.wait()
    l_ctxt.wait()
    ones = jnp.ones((16, 2048), BF)
    sum_mix = dot(ones, mg[...])[0:8]
    sum_up = dot(ones, hl[...])[0:8]
    sum_g = dot(ones, g[...])[0:8]
    gains = jnp.concatenate([vec_ref[...], sum_up, sum_g], axis=0)
    col[...] = jnp.concatenate([gains, jnp.zeros((104, 768), F32)], axis=0).T

    grads[0, :, 0:768] = jnp.zeros((768, 768), BF)
    grads[0, out_rows, 0:768] = dot(ctxt[...], g[...]).astype(BF)

    @pl.loop(0, 3)
    def _(i):
        r = pl.ds(pl.multiple_of(i * 256, 256), 256)
        cols = col[r]
        u = unitt[r]
        u1 = dot(u, mg[...])
        wm = w[0, r, 768:1344].astype(F32)
        gain1 = jnp.sum(wm * u1, axis=-1, keepdims=True)
        shift1 = jnp.sum(wm * sum_mix[0:1], axis=-1, keepdims=True)
        dmix = u1 * cols[:, 0:1] + cols[:, 1:2] * sum_mix[0:1]
        u2 = dot(u, hl[...])
        wu = w[1, r, 0:768].astype(F32)
        gain2 = jnp.sum(wu * u2, axis=-1, keepdims=True)
        shift2 = jnp.sum(wu * sum_up[0:1], axis=-1, keepdims=True)
        grads[1, r, 0:768] = (u2 * cols[:, 2:3] + cols[:, 3:4] * sum_up[0:1]).astype(BF)
        grads[1, r, 768:] = dot(actt[r], g[...]).astype(BF)
        lane = lax.broadcasted_iota(jnp.int32, (256, 192), 1)
        small = jnp.zeros((256, 192), F32)
        for n, v in enumerate((gain1, shift1, gain2, shift2, cols[:, 16:17], cols[:, 8:9])):
            small = jnp.where(lane == n, v, small)
        grads[0, r, 768:1536] = jnp.concatenate([dmix, small], axis=1).astype(BF)

    mixcol = jnp.concatenate([sum_mix, jnp.zeros((120, 576), F32)], axis=0).T
    col[pl.ds(0, 576)] = mixcol
    lane = lax.broadcasted_iota(jnp.int32, (192, 192), 1)
    more = jnp.zeros((192, 192), F32)
    for n in range(3):
        more = jnp.where(lane == 6 + n, col[pl.ds(n, 192, stride=3), 0:1], more)
    old = grads[0, out_rows, 768:1536].astype(F32)
    grads[0, out_rows, 768:1536] = (
        old + jnp.concatenate([jnp.zeros((192, 576), F32), more], axis=1)
    ).astype(BF)

    order = (1, 3, 2, 0)
    for k in order:
        for b in range(4):
            r = rows(lax.rem(here2 + k, 4), b, True)
            send(grads.at[1 - c, r], first_in.at[r], s0.at[k, b], r0.at[k, b], sibling)
    pass_on(1)
    for k in order:
        place = lax.rem(here1 + k, 4)
        for b in range(4):
            r = rows(place, b, False)
            landed(first_in.at[r], r0.at[k, b])
            grads[c, r] = (grads[c, r].astype(F32) + first_in[r].astype(F32)).astype(BF)
            if k:
                send(grads.at[c, r], second_in.at[k - 1, b], s1.at[k - 1, b], r1.at[k - 1, b], first(k))
    for h in range(2):
        o = total(0, h) + rows_ref[half[h]].astype(F32) + vec_ref[4:5]
        out_ref[half[h]] = o.astype(BF)
    for j in order:
        b = lax.rem(here2 + j, 4)
        r = rows(here1, b, False)
        acc = grads[c, r].astype(F32)
        for k in (1, 3, 2):
            landed(second_in.at[k - 1, b], r1.at[k - 1, b])
            acc = acc + second_in[k - 1, b].astype(F32)
        part[j] = acc.astype(BF)
        if j:
            send(part.at[j], third_in.at[j - 1], s2.at[j - 1], r2.at[j - 1], second(j))
    acc = part[0].astype(F32)
    for j in (1, 3, 2):
        landed(third_in.at[j - 1], r2.at[j - 1])
        acc = acc + third_in[j - 1].astype(F32)
    fin_ref[c, x] = acc.astype(BF)
    for k in (1, 3, 2):
        slot = fin_ref.at[c, x]
        send(slot, slot, s3.at[k - 1], r3.at[k - 1], (lax.rem(x + k, 4), me))
    slot = fin_ref.at[c, x]
    send(slot, slot, s4.at[0], r4.at[0], sibling)
    for h in range(2):
        s = total(1, h)
        v = rows_ref[half[h]].astype(F32)
        v = v - jnp.mean(v, axis=-1, keepdims=True)
        inverse = lax.rsqrt(jnp.mean(v * v, axis=-1, keepdims=True) + 1e-05)
        unit = v * inverse
        s = s - jnp.mean(s, axis=-1, keepdims=True) - unit * jnp.mean(s * unit, axis=-1, keepdims=True)
        own = pl.ds(pl.multiple_of(x * 512 + h * 256, 256), 256)
        back_ref[half[h]] = (g[own].astype(F32) + inverse * s).astype(BF)
    for k in (1, 3, 2):
        slot = fin_ref.at[c, lax.rem(x + 4 - k, 4)]
        landed(slot, r3.at[k - 1])
        send(slot, slot, s4.at[k], r4.at[k], sibling)
    for k in range(4):
        landed(fin_ref.at[1 - c, lax.rem(x + 4 - k, 4)], r4.at[k])
    for cp in started:
        cp.wait_send()


def tail(ctx, ctxt, mg, act, actt, dg, unitt, w, vec, g, rows):
    vm = pl.BlockSpec(memory_space=pltpu.VMEM)
    hbm = pl.BlockSpec(memory_space=pl.ANY)
    dma = pltpu.SemaphoreType.DMA
    return pl.pallas_call(
        tail_kernel,
        out_shape=(
            jax.ShapeDtypeStruct((512, 768), BF),
            jax.ShapeDtypeStruct((512, 768), BF),
            jax.ShapeDtypeStruct((2, 4, PAIR, WIDE), BF),
        ),
        in_specs=[hbm] * 8 + [vm] + [hbm] * 4 + [vm],
        out_specs=[vm, vm, vm],
        scratch_shapes=[
            pltpu.VMEM((2048, 192), BF),
            pltpu.VMEM((192, 2048), BF),
            pltpu.VMEM((2048, 576), BF),
            pltpu.VMEM((2048, 768), BF),
            pltpu.VMEM((768, 2048), BF),
            pltpu.VMEM((2048, 768), BF),
            pltpu.VMEM((768, 2048), BF),
            pltpu.VMEM((2, 768, WIDE), BF),
            pltpu.VMEM((2048, 768), BF),
            pltpu.VMEM((2, 4, 512, 768), BF),
            pltpu.VMEM((2, 2, 256, 768), BF),
            pltpu.VMEM((2, 2, 512, 768), BF),
            pltpu.VMEM((2, 768, WIDE), BF),
            pltpu.VMEM((768, WIDE), BF),
            pltpu.VMEM((3, 4, PAIR, WIDE), BF),
            pltpu.VMEM((4, PAIR, WIDE), BF),
            pltpu.VMEM((3, PAIR, WIDE), BF),
            pltpu.VMEM((768, 128), F32),
            dma((12,)),
            dma((2, 2)), dma((2, 2)), dma((2, 2, 2)), dma((2, 2, 2)),
            dma((4, 4)), dma((4, 4)), dma((3, 4)), dma((3, 4)), dma((3,)), dma((3,)),
            dma((3,)), dma((3,)), dma((4,)), dma((4,)),
        ],
        compiler_params=pltpu.CompilerParams(
            collective_id=1, has_side_effects=True, vmem_limit_bytes=60 * 1024 * 1024
        ),
        name="tail_all",
    )(ctx, ctxt, mg, act, actt, dg, unitt, w, vec, *g, rows)


def shift_x(v, k):
    return lax.ppermute(v, "seq", [(i, (i + k) % NX) for i in range(NX)])


def swap_core(v):
    return lax.ppermute(v, "shard", [(i, i ^ 1) for i in range(32)])


def local(
    inputs, positions, first_gain, first_shift, second_gain, second_shift, mix_weight, mix_bias,
    out_weight, out_bias, up_weight, up_bias, down_weight, down_bias, cotangent,
):
    x, _, _, c = places()
    is0 = c == 0
    small = jnp.concatenate(
        [
            jnp.stack([first_gain, first_shift, second_gain, second_shift, out_bias, down_bias], 1),
            mix_bias.reshape(24, 3),
            up_bias.reshape(24, 4),
        ],
        axis=1,
    )
    half_a = jnp.concatenate(
        [
            out_weight,
            lax.dynamic_slice_in_dim(mix_weight, x * 576, 576, 1),
            small,
            jnp.zeros((24, WIDE - 768 - 576 - 13), BF),
        ],
        axis=1,
    )
    up_part = lax.dynamic_index_in_dim(up_weight.reshape(24, 32, 4, 24), x, 2, keepdims=False)
    half_b = jnp.concatenate(
        [up_part.reshape(24, 768), lax.dynamic_slice_in_dim(down_weight, x * 24, 24, 0)], axis=1
    )
    kept = jnp.where(is0, half_a, half_b)
    came = swap_core(jnp.where(is0, half_b, half_a))
    pair = jnp.where(is0, jnp.concatenate([kept, came], 0), jnp.concatenate([came, kept], 0))
    pos_own = jnp.concatenate([positions.reshape(4, 128)] * 2, axis=0)
    rows_all, mine, other, pos_all = gather(inputs[0], pair, pos_own)
    grad_low = cotangent[0]
    grads = [grad_low] + [shift_x(grad_low, k) for k in (1, 2, 3)]
    grads_all = jnp.zeros((4, 512, 768), BF)
    for k in range(4):
        grads_all = lax.dynamic_update_slice(grads_all, grads[k][None], (lax.rem(x + 4 - k, 4), 0, 0))
    grads_all = grads_all.reshape(2048, 768)

    w_a = jnp.where(is0, mine, other)
    w_b = jnp.where(is0, other, mine)
    out_rows = lax.dynamic_slice(w_a, (x * 192, 0), (192, 768))
    mix_w = w_a[:, 768:1344]
    extra = w_a[:, 1344:1408]
    vectors = extra.astype(F32).T
    g1, b1, g2, b2, out_b, down_b = (vectors[i] for i in range(6))
    mixb = lax.dynamic_slice_in_dim(extra[:, 6:9].astype(F32).reshape(2304), x * 576, 576, 0)
    upb = lax.dynamic_index_in_dim(
        extra[:, 9:13].astype(F32).reshape(32, 4, 24), x, 1, keepdims=False
    ).reshape(768)
    up_w, down_w = w_b[:, :768], w_b[:, 768:]

    place = pos_all.reshape(4, 2, 512)[:, 0].reshape(2048)
    freqs = 10000.0 ** (-jnp.arange(0, ROT, 2, dtype=F32) / ROT)
    angles = freqs[:, None] * place.astype(F32)[None, :]
    cos8, sin8 = jnp.cos(angles), jnp.sin(angles)
    cosine = jnp.concatenate([cos8, cos8, jnp.ones((48, 2048), F32)], 0).T
    sine = jnp.concatenate([sin8, sin8, jnp.zeros((48, 2048), F32)], 0).T
    start = (jnp.arange(2048, dtype=jnp.int32) - place)[:, None]
    turn = (jnp.eye(64, k=8) * (jnp.arange(64) >= 8) * (jnp.arange(64) < 16)).astype(BF) - (
        jnp.eye(64, k=-8) * (jnp.arange(64) < 8)
    ).astype(BF)

    rows = rows_all.astype(F32)
    centered = rows - jnp.mean(rows, axis=-1, keepdims=True)
    inverse = lax.rsqrt(jnp.mean(centered * centered, axis=-1, keepdims=True) + 1e-05)
    unit = centered * inverse
    first_low = (unit * g1 + b1).astype(BF)
    second_low = (unit * g2 + b2).astype(BF)
    mixed = (dot(first_low, mix_w) + mixb).astype(BF)
    hidden = dot(second_low, up_w) + upb
    active = jax.nn.gelu(hidden, approximate=False).astype(BF)
    context_grad = dot_nt(grads_all, out_rows).astype(BF)
    context, mix_grad = attention(mixed, cosine, sine, start, context_grad, turn)

    phi = jnp.exp(hidden * hidden * -0.5) * (2.0 * jnp.pi) ** -0.5
    slope = (0.5 * (1.0 + lax.erf(hidden * 2.0**-0.5)) + hidden * phi).astype(BF)
    unit_t = unit.astype(BF).T
    vec = jnp.concatenate([jnp.stack([g1, b1, g2, b2, out_b + down_b]), jnp.zeros((3, 768), F32)], 0)
    outputs, input_grad, shares = tail(
        context, context.T, mix_grad, active, active.T, slope, unit_t, jnp.stack([w_a, w_b]), vec, grads, inputs[0]
    )
    shares = lax.dynamic_slice_in_dim(shares, c * 24, 24, 2).astype(F32)
    half_a, half_b = shares[0], shares[1]
    got_out = jnp.sum(half_a[:, :, :768], axis=0)
    got_mix = half_a[:, :, 768:1344].transpose(1, 0, 2).reshape(24, 2304)
    got_small = jnp.sum(half_a[:, :, 1344:1353], axis=0)
    got_bias = half_a[0, :, 1348]
    got_up = half_b[:, :, :768].reshape(4, 24, 32, 24).transpose(1, 2, 0, 3).reshape(24, 3072)
    got_down = half_b[:, :, 768:].reshape(96, 768)
    return (
        outputs[None],
        input_grad[None],
        got_small[:, 0],
        got_small[:, 1],
        got_small[:, 2],
        got_small[:, 3],
        got_mix,
        got_small[:, 6:9].reshape(72),
        got_out,
        got_bias,
        got_up,
        half_a[:, :, 1349].reshape(96),
        got_down,
        got_bias,
    )


def solution(mesh):
    vec, mat, tok = P("shard"), P("shard", None), P("shard", "seq", None)
    return jax.shard_map(
        local,
        mesh=mesh,
        in_specs=(tok, P("shard", "seq"), vec, vec, vec, vec, mat, vec, mat, vec, mat, vec, mat, vec, tok),
        out_specs=(tok, tok, vec, vec, vec, vec, mat, vec, mat, vec, mat, vec, mat, vec),
        check_vma=False,
    )
```

```python
import functools

import jax
import jax.numpy as jnp
from jax import lax
from jax.experimental import pallas as pl
from jax.experimental.pallas import tpu as pltpu
from jax.sharding import PartitionSpec as P

HD = 64
ROT = 16
NX = 4
BF = jnp.bfloat16
F32 = jnp.float32
MESH = pl.DeviceIdType.MESH
NT = (((1,), (1,)), ((), ()))
VMEM_LIMIT = 56 * 1024 * 1024
WIDE = 1536
PAIR = 48


def dot(a, b):
    return jnp.dot(a, b, preferred_element_type=F32)


def dot_nt(a, b):
    return lax.dot_general(a, b, NT, preferred_element_type=F32)


def dot_tn(a, b):
    return lax.dot_general(a, b, (((0,), (0,)), ((), ())), preferred_element_type=F32)


def places():
    x = lax.axis_index("seq")
    s = lax.axis_index("shard")
    return x, s // 8, (s // 2) % 4, s % 2


def at(x, z, y, c):
    return (x, (z * 4 + y) * 2 + c)


ERFC = (0.254829592, -0.284496736, 1.421413741, -1.453152027, 1.061405429)


def gelu_and_slope(h):
    t = 1.0 / (1.0 + (0.3275911 * 2.0**-0.5) * jnp.abs(h))
    e = jnp.exp(h * h * -0.5)
    poly = t * (ERFC[0] + t * (ERFC[1] + t * (ERFC[2] + t * (ERFC[3] + t * ERFC[4]))))
    tail_part = 0.5 * poly * e
    cdf = jnp.where(h >= 0, 1.0 - tail_part, tail_part)
    return h * cdf, cdf + h * e * 0.3989422804014327


def iota(shape, dim):
    return lax.broadcasted_iota(jnp.int32, shape, dim)


def front_kernel(
    rows_ref, grad_ref, pair_ref, pos_ref,
    mixed_o, act_o, actt_o, slope_o, unitt_o, cg_o, w_o, vec_o, table_o,
    rows_all, w, pos_all, grad, mixed, act, actt, slope, unitt, cg, cgs, vec, table,
    s1, r1, s2, r2, s3, r3, sx, rx, sf, rf, sp, rp, sc, rc, loc, wr,
):
    x, z, y, c = places()
    is0 = c == 0
    right, left, far = lax.rem(x + 1, 4), lax.rem(x + 3, 4), lax.rem(x + 2, 4)
    me = lax.axis_index("shard")
    mine, other = w.at[c], w.at[1 - c]

    def first(k):
        return at(x, jnp.where(is0, z, lax.rem(z + k, 4)), jnp.where(is0, lax.rem(y + k, 4), y), c)

    def second(k):
        return at(x, jnp.where(is0, lax.rem(z + k, 4), z), jnp.where(is0, y, lax.rem(y + k, 4)), c)

    def block(dz, dy):
        return lax.rem(z + dz, 4) * 4 + lax.rem(y + dy, 4)

    def held(a, b):
        da, db = (4 - a) % 4, (4 - b) % 4
        return jnp.where(is0, block(db, da), block(da, db))

    def rows_of(ref, b):
        return ref.at[pl.ds(pl.multiple_of(b * PAIR, 16), PAIR)]

    def quarter(who, q):
        return rows_all.at[pl.ds(pl.multiple_of(who * 512 + q * 128, 128), 128)]

    def remote(src, dst, ss, rs, dev):
        return pltpu.make_async_remote_copy(
            src_ref=src, dst_ref=dst, send_sem=ss, recv_sem=rs, device_id=dev, device_id_type=MESH
        )

    started = []

    def send(*args):
        cp = remote(*args)
        cp.start()
        started.append(cp)

    sibling = (x, me + 1 - 2 * c)

    def landed(dst, sem):
        remote(dst, dst, sem, sem, sibling).wait_recv()

    own_block = z * 4 + y
    own_pos = pos_all.at[pl.ds(pl.multiple_of(x * 8, 8), 8)]
    local_copies = []
    for n, (src, dst) in enumerate(
        (
            (pair_ref, rows_of(mine, own_block)),
            (rows_ref, rows_all.at[pl.ds(pl.multiple_of(x * 512, 512), 512)]),
            (pos_ref, own_pos),
            (grad_ref, grad),
        )
    ):
        cp = pltpu.make_async_copy(src, dst, loc.at[n])
        cp.start()
        local_copies.append(cp)
    barrier = pltpu.get_barrier_semaphore()
    peers = [first(k) for k in (1, 2, 3)] + [second(k) for k in (1, 2, 3)]
    peers += [sibling, (right, me), (left, me), (far, me)]
    for peer in peers:
        pl.semaphore_signal(barrier, inc=1, device_id=peer, device_id_type=MESH)
    pl.semaphore_wait(barrier, len(peers))

    order = (1, 3, 2)
    for k in order:
        send(pair_ref, rows_of(mine, own_block), s1.at[k - 1], r1.at[k - 1], first(k))
    own = [rows_ref.at[pl.ds(q * 128, 128)] for q in range(4)]
    for i in range(4):
        send(own[i], quarter(x, i), sx.at[0, i], rx.at[0, i], (right, me))
        send(own[3 - i], quarter(x, 3 - i), sx.at[1, 3 - i], rx.at[1, 3 - i], (left, me))
    for k in order:
        send(pair_ref, rows_of(mine, own_block), s2.at[0, k - 1], r2.at[0, k - 1], second(k))
    send(pair_ref, rows_of(mine, own_block), s3.at[0, 0], r3.at[0, 0], sibling)
    for k in order:
        send(pos_ref, own_pos, sp.at[k - 1], rp.at[k - 1], (lax.rem(x + k, 4), me))
    for cp in local_copies:
        cp.wait()

    for k in order:
        b = held(k, 0)
        landed(rows_of(mine, b), r1.at[k - 1])
        for j in order:
            send(rows_of(mine, b), rows_of(mine, b), s2.at[k, j - 1], r2.at[k, j - 1], second(j))
        send(rows_of(mine, b), rows_of(mine, b), s3.at[k, 0], r3.at[k, 0], sibling)

    for k in order:
        src = lax.rem(x + 4 - k, 4)
        landed(pos_all.at[pl.ds(pl.multiple_of(src * 8, 8), 8)], rp.at[k - 1])
    place = jnp.concatenate(
        [pos_all[8 * d + q : 8 * d + q + 1] for d in range(4) for q in range(4)], axis=1
    ).astype(F32)
    freqs = jnp.ones((8, 2048), F32)
    for n in range(1, 8):
        freqs = jnp.where(iota((8, 2048), 0) == n, 10000.0 ** (-2.0 * n / ROT), freqs)
    angles = place * freqs
    cos8, sin8 = jnp.cos(angles), jnp.sin(angles)
    start = jnp.broadcast_to(iota((1, 2048), 1).astype(F32) - place, (8, 2048))
    table[...] = jnp.concatenate(
        [cos8, cos8, jnp.ones((48, 2048), F32), sin8, sin8, start, jnp.zeros((40, 2048), F32)], axis=0
    ).T

    for i in range(2):
        landed(quarter(left, i), rx.at[0, i])
        send(quarter(left, i), quarter(left, i), sf.at[0, i], rf.at[0, i], (right, me))
        landed(quarter(right, 3 - i), rx.at[1, 3 - i])
        send(quarter(right, 3 - i), quarter(right, 3 - i), sf.at[1, i], rf.at[1, i], (left, me))
    for j in order:
        for k in (0,) + order:
            b = held(k, j)
            landed(rows_of(mine, b), r2.at[k, j - 1])
            send(rows_of(mine, b), rows_of(mine, b), s3.at[k, j], r3.at[k, j], sibling)
    for a in range(4):
        for b in range(4):
            da, db = (4 - a) % 4, (4 - b) % 4
            blk = jnp.where(is0, block(da, db), block(db, da))
            landed(rows_of(other, blk), r3.at[a, b])

    own_tok = pl.ds(pl.multiple_of(x * 512, 512), 512)
    for k in (2, 1, 3, 0):
        dev = lax.rem(x + k, 4)
        heads = w[0, pl.ds(pl.multiple_of(dev * 192, 64), 192), 0:768]

        @pl.loop(0, 2)
        def _(i):
            r = pl.ds(pl.multiple_of(i * 256, 256), 256)
            cgs[k, r] = dot_nt(grad[r], heads).astype(BF)

        if k:
            send(cgs.at[k], cg.at[own_tok], sc.at[k - 1], rc.at[k - 1], (dev, me))
        else:
            cg[own_tok] = cgs[0]

    packed = w[0, :, 1344:1536]
    pick = [dot((iota((32, 768), 1) == 24 * iota((32, 768), 0) + n).astype(BF), packed).astype(BF) for n in range(2)]

    def spread(src, width, base, group, shift):
        lane = iota((192, width), 1)
        one_hot = iota((192, width), 0) == lax.rem(lane, group) + base
        lane = iota((32, width), 1)
        keep = iota((32, width), 0) == lax.div(lane, group) + shift
        return jnp.sum(jnp.where(keep, dot(src, one_hot.astype(BF)), 0.0), axis=0, keepdims=True)

    g1, b1, g2, b2, out_b, down_b = (spread(pick[0], 768, 24 * n, 24, 0) for n in range(6))
    mix_b = spread(pick[1], 576, 0, 72, 8 * x)
    up_b = spread(pick[1], 768, 72 + 24 * x, 24, 0)
    vec[...] = jnp.concatenate([g1, b1, g2, b2, out_b + down_b, up_b, g1, g1], axis=0)

    writes = []

    def write(src, dst):
        cp = pltpu.make_async_copy(src, dst, wr.at[len(writes)])
        cp.start()
        writes.append(cp)

    write(w, w_o)
    write(vec, vec_o)
    write(table, table_o)

    def compute(who):
        @pl.loop(0, 2)
        def _(i):
            r = pl.ds(pl.multiple_of(who * 512 + i * 256, 256), 256)
            v = rows_all[r].astype(F32)
            v = v - jnp.mean(v, axis=-1, keepdims=True)
            unit = v * lax.rsqrt(jnp.mean(v * v, axis=-1, keepdims=True) + 1e-05)
            cols = pl.ds(pl.multiple_of(i * 256, 256), 256)
            unitt[who, :, cols] = unit.astype(BF).T
            one = (unit * vec[0:1] + vec[1:2]).astype(BF)
            mixed[r] = (dot(one, w[0, :, 768:1344]) + mix_b).astype(BF)
            two = (unit * vec[2:3] + vec[3:4]).astype(BF)
            hidden = dot(two, w[1, :, 0:768]) + vec[5:6]
            a, s = gelu_and_slope(hidden)
            a = a.astype(BF)
            act[r] = a
            actt[who, :, cols] = a.T
            slope[r] = s.astype(BF)

        t = pl.ds(pl.multiple_of(who * 512, 512), 512)
        write(mixed.at[t], mixed_o.at[t])
        write(act.at[t], act_o.at[t])
        write(slope.at[t], slope_o.at[t])
        write(actt.at[who], actt_o.at[who])
        write(unitt.at[who], unitt_o.at[who])

    compute(x)
    for i in range(2):
        landed(quarter(left, 2 + i), rx.at[0, 2 + i])
    compute(left)
    for i in range(2):
        landed(quarter(right, i), rx.at[1, i])
    compute(right)
    for i in range(2):
        landed(quarter(far, i), rf.at[0, i])
        landed(quarter(far, 3 - i), rf.at[1, i])
    compute(far)
    for k in (1, 3, 2):
        t = pl.ds(pl.multiple_of(lax.rem(x + 4 - k, 4) * 512, 512), 512)
        landed(cg.at[t], rc.at[k - 1])
    write(cg, cg_o)
    for cp in writes:
        cp.wait()
    for cp in started:
        cp.wait_send()


def front(rows, grad, pair, pos):
    hbm = pl.BlockSpec(memory_space=pl.ANY)
    dma = pltpu.SemaphoreType.DMA
    outs = [
        ((2048, 576), BF), ((2048, 768), BF), ((4, 768, 512), BF), ((2048, 768), BF), ((4, 768, 512), BF),
        ((2048, 192), BF), ((2, 768, WIDE), BF), ((8, 768), F32), ((2048, 128), F32),
    ]
    return pl.pallas_call(
        front_kernel,
        out_shape=tuple(jax.ShapeDtypeStruct(s, t) for s, t in outs),
        in_specs=[hbm] * 4,
        out_specs=[hbm] * 9,
        scratch_shapes=[
            pltpu.VMEM((2048, 768), BF),
            pltpu.VMEM((2, 768, WIDE), BF),
            pltpu.VMEM((32, 128), jnp.int32),
            pltpu.VMEM((512, 768), BF),
            pltpu.VMEM((2048, 576), BF),
            pltpu.VMEM((2048, 768), BF),
            pltpu.VMEM((4, 768, 512), BF),
            pltpu.VMEM((2048, 768), BF),
            pltpu.VMEM((4, 768, 512), BF),
            pltpu.VMEM((2048, 192), BF),
            pltpu.VMEM((4, 512, 192), BF),
            pltpu.VMEM((8, 768), F32),
            pltpu.VMEM((2048, 128), F32),
            dma((3,)), dma((3,)), dma((4, 3)), dma((4, 3)), dma((4, 4)), dma((4, 4)),
            dma((2, 4)), dma((2, 4)), dma((2, 2)), dma((2, 2)), dma((3,)), dma((3,)), dma((3,)), dma((3,)),
            dma((4,)), dma((24,)),
        ],
        compiler_params=pltpu.CompilerParams(
            collective_id=0, has_side_effects=True, vmem_limit_bytes=VMEM_LIMIT
        ),
        name="front_all",
    )(rows, grad, pair, pos)


BQ = 512
NB = 2048 // BQ


def attention_kernel(
    mixed_ref, table_ref, grad_ref, ctx_ref, ctxt_ref, out_ref,
    qs, ks, vs, qt, es, ss, dkt, dvt, dqs, os, gs,
):
    row, lane = iota((64, 64), 0), iota((64, 64), 1)
    turn = jnp.where((lane == row + 8) & (row < 8), 1.0, jnp.where((row == lane + 8) & (lane < 8), -1.0, 0.0))
    turn = turn.astype(BF)

    def angles(r):
        t = table_ref[r]
        return t[:, 0:64], jnp.where(iota((BQ, 64), 1) < ROT, t[:, 64:128], 0.0)

    @pl.loop(0, NB)
    def _(i):
        r = pl.ds(pl.multiple_of(i * BQ, BQ), BQ)
        cosine, sine = angles(r)
        lane = lax.broadcasted_iota(jnp.int32, (BQ, 128), 1)
        for h in range(3):
            q = mixed_ref[r, h * 192 : h * 192 + 64]
            k = mixed_ref[r, h * 192 + 64 : h * 192 + 128]
            v = mixed_ref[r, h * 192 + 128 : h * 192 + 192]
            q = q.astype(F32) * cosine + dot(q, turn) * sine
            k = k.astype(F32) * cosine + dot(k, turn) * sine
            q = q.astype(BF) * 0.125
            qs[h, r] = q
            qt[h, i] = q.astype(F32).T.astype(BF)
            ks[h, r] = k.astype(BF)
            wide = jnp.concatenate([v.astype(F32), jnp.zeros((BQ, 64), F32)], axis=1)
            vs[h, r] = jnp.where((lane == 64) | (lane == 65), 1.0, wide).astype(BF)
            gs[h, r] = grad_ref[r, h * 64 : h * 64 + 64]

    @pl.loop(0, 3)
    def _(h):
        dkt[h] = jnp.zeros((64, 2048), F32)
        dvt[h] = jnp.zeros((64, 2048), F32)
        for i in range(NB):
            r = pl.ds(i * BQ, BQ)
            q = qs[h, r]
            start = table_ref[r, 80:81].astype(jnp.int32)
            top = None
            for b in range(i + 1):
                col = pl.ds(b * BQ, BQ)
                s = dot_nt(q, ks[h, col])
                cols = lax.broadcasted_iota(jnp.int32, (BQ, BQ), 1)
                keep = cols >= start - b * BQ
                if b == i:
                    keep &= cols <= lax.broadcasted_iota(jnp.int32, (BQ, BQ), 0)
                s = jnp.where(keep, s, -1e30)
                ss[:, col] = s
                m = jnp.max(s, axis=-1, keepdims=True)
                top = m if top is None else jnp.maximum(top, m)
            acc = None
            for b in range(i + 1):
                col = pl.ds(b * BQ, BQ)
                e = jnp.exp(ss[:, col] - top).astype(BF)
                es[:, col] = e
                o = dot(e, vs[h, col])
                acc = o if acc is None else acc + o
            inverse = 1.0 / acc[:, 64:65]
            o = acc[:, :64] * inverse
            os[h, r] = o.astype(BF)
            g = gs[h, r].astype(F32) * inverse
            delta = -jnp.sum(g * o, axis=-1, keepdims=True)
            high = delta.astype(BF).astype(F32)
            lane = lax.broadcasted_iota(jnp.int32, (BQ, 128), 1)
            wide = jnp.concatenate([g, jnp.zeros((BQ, 64), F32)], axis=1)
            wide = jnp.where(lane == 64, high, jnp.where(lane == 65, delta - high, wide)).astype(BF)
            gt = g.T.astype(BF)
            dq = None
            for b in range(i + 1):
                col = pl.ds(b * BQ, BQ)
                dp = dot_nt(wide, vs[h, col])
                e = es[:, col]
                ds = (e.astype(F32) * dp).astype(BF)
                part = dot(ds, ks[h, col])
                dq = part if dq is None else dq + part
                dkt[h, :, col] += dot(qt[h, i], ds)
                dvt[h, :, col] += dot(gt, e)
            dqs[h, r] = dq * 0.125

    @pl.loop(0, NB)
    def _(i):
        r = pl.ds(pl.multiple_of(i * BQ, BQ), BQ)
        cosine, sine = angles(r)

        def back(g):
            return g * cosine + dot_nt((g * sine).astype(BF), turn)

        parts = []
        for h in range(3):
            parts.append(back(dqs[h, r]))
            parts.append(back(dkt[h, :, r].T))
            parts.append(dvt[h, :, r].T)
        out_ref[r] = jnp.concatenate(parts, axis=1).astype(BF)
        ctx = jnp.concatenate([os[h, r].astype(F32) for h in range(3)], axis=1)
        ctx_ref[r] = ctx.astype(BF)
        ctxt_ref[:, r] = ctx.T.astype(BF)


def attention(mixed, table, grads):
    vm = pl.BlockSpec(memory_space=pltpu.VMEM)
    return pl.pallas_call(
        attention_kernel,
        out_shape=(
            jax.ShapeDtypeStruct((2048, 192), BF),
            jax.ShapeDtypeStruct((192, 2048), BF),
            jax.ShapeDtypeStruct((2048, 576), BF),
        ),
        in_specs=[vm] * 3,
        out_specs=[vm] * 3,
        scratch_shapes=[
            pltpu.VMEM((3, 2048, 64), BF),
            pltpu.VMEM((3, 2048, 64), BF),
            pltpu.VMEM((3, 2048, 128), BF),
            pltpu.VMEM((3, NB, 64, BQ), BF),
            pltpu.VMEM((BQ, 2048), BF),
            pltpu.VMEM((BQ, 2048), F32),
            pltpu.VMEM((3, 64, 2048), F32),
            pltpu.VMEM((3, 64, 2048), F32),
            pltpu.VMEM((3, 2048, 64), F32),
            pltpu.VMEM((3, 2048, 64), BF),
            pltpu.VMEM((3, 2048, 64), BF),
        ],
        compiler_params=pltpu.CompilerParams(vmem_limit_bytes=VMEM_LIMIT),
        cost_estimate=pl.CostEstimate(
            flops=30_000_000_000, bytes_accessed=10_000_000, transcendentals=8_000_000
        ),
        name="attention_both",
    )(mixed, table, grads)


def tail_kernel(
    ctx_h, ctxt_h, mg_h, act_h, actt_h, dg_h, unitt_h, w_h, vec_ref, ga_h, gb_h, gc_h, gd_h, rows_ref,
    out_ref, back_ref, fin_ref,
    ctx, ctxt, mg, act, actt, hl, unitt, w, g, buf, passed, got, grads, first_in, second_in, part, third_in, col,
    ld, sa, ra, sb, rb, s0, r0, s1, r1, s2, r2, s3, r3, s4, r4,
):
    x, z, y, c = places()
    is0 = c == 0
    me = lax.axis_index("shard")
    right, left = lax.rem(x + 1, 4), lax.rem(x + 3, 4)
    sibling = (x, me + 1 - 2 * c)

    def tok(k):
        return pl.ds(pl.multiple_of(lax.rem(x + 4 - k, 4) * 512, 512), 512)

    loads = []

    def load(src, dst):
        cp = pltpu.make_async_copy(src, dst, ld.at[len(loads)])
        cp.start()
        loads.append(cp)
        return cp

    l_ctx = load(ctx_h, ctx)
    l_w = load(w_h, w)
    l_act = load(act_h, act)
    l_g = [load(s, g.at[tok(k)]) for k, s in enumerate((ga_h, gb_h, gc_h, gd_h))]
    l_dg = load(dg_h, hl)
    l_mg = load(mg_h, mg)
    l_unitt = load(unitt_h, unitt)
    l_actt = load(actt_h, actt)
    l_ctxt = load(ctxt_h, ctxt)

    def first(k):
        return at(x, jnp.where(is0, lax.rem(z + k, 4), z), jnp.where(is0, y, lax.rem(y + k, 4)), c)

    def second(k):
        return at(x, jnp.where(is0, z, lax.rem(z + k, 4)), jnp.where(is0, lax.rem(y + k, 4), y), c)

    here1 = jnp.where(is0, z, y)
    here2 = jnp.where(is0, y, z)

    def rows(a, b, flip):
        blk = jnp.where(is0 != flip, a * 4 + b, b * 4 + a)
        return pl.ds(pl.multiple_of(blk * PAIR, 16), PAIR)

    barrier = pltpu.get_barrier_semaphore()
    peers = [first(k) for k in (1, 2, 3)] + [second(k) for k in (1, 2, 3)] + [sibling]
    peers += [(lax.rem(x + k, 4), me) for k in (1, 2, 3)]
    for peer in peers:
        pl.semaphore_signal(barrier, inc=1, device_id=peer, device_id_type=MESH)
    pl.semaphore_wait(barrier, len(peers))
    started = []

    def remote(src, dst, ss, rs, dev):
        cp = pltpu.make_async_remote_copy(
            src_ref=src, dst_ref=dst, send_sem=ss, recv_sem=rs, device_id=dev, device_id_type=MESH
        )
        return cp

    def send(*args):
        cp = remote(*args)
        cp.start()
        started.append(cp)

    def landed(dst, sem):
        remote(dst, dst, sem, sem, sibling).wait_recv()

    half = [pl.ds(0, 256), pl.ds(256, 256)]
    dev_x = [(right, me), (left, me)]

    def far_send(n):
        for d in range(2):
            send(buf.at[n, 2, half[d]], passed.at[n, d], sa.at[n, d], ra.at[n, d], dev_x[d])

    def near_send(n, d, h):
        send(buf.at[n, 3 - 2 * d, half[h]], got.at[n, d, half[h]], sb.at[n, d, h], rb.at[n, d, h], dev_x[d])

    def pass_on(n):
        for d in range(2):
            landed(passed.at[n, d], ra.at[n, d])
            k = 3 - 2 * d
            buf[n, k, half[d]] = (buf[n, k, half[d]].astype(F32) + passed[n, d].astype(F32)).astype(BF)
            near_send(n, d, d)

    def total(n, h):
        for d in range(2):
            landed(got.at[n, d, half[h]], rb.at[n, d, h])
        return buf[n, 0, half[h]].astype(F32) + got[n, 0, half[h]].astype(F32) + got[n, 1, half[h]].astype(F32)

    out_rows = pl.ds(pl.multiple_of(x * 192, 64), 192)

    def outputs_of(k):
        base = lax.rem(x + 4 - k, 4) * 512

        @pl.loop(0, 2)
        def _(i):
            r = pl.ds(pl.multiple_of(base + i * 256, 256), 256)
            o = dot(ctx[r], w[0, out_rows, 0:768]) + dot(act[r], w[1, :, 768:])
            buf[0, k, pl.ds(pl.multiple_of(i * 256, 256), 256)] = o.astype(BF)

    def pulls_of(k):
        base = lax.rem(x + 4 - k, 4) * 512

        @pl.loop(0, 2)
        def _(i):
            r = pl.ds(pl.multiple_of(base + i * 256, 256), 256)
            ag = dot_nt(g[r], w[1, :, 768:])
            low = (ag * hl[r].astype(F32)).astype(BF)
            hl[r] = low
            s = dot_nt(low, w[1, :, 0:768]) * vec_ref[2:3] + dot_nt(mg[r], w[0, :, 768:1344]) * vec_ref[0:1]
            buf[1, k, pl.ds(pl.multiple_of(i * 256, 256), 256)] = s.astype(BF)

    l_ctx.wait()
    l_w.wait()
    l_act.wait()
    for k in (2, 3, 1, 0):
        outputs_of(k)
        if k == 2:
            far_send(0)
        elif k == 3:
            near_send(0, 0, 1)
        elif k == 1:
            near_send(0, 1, 0)
    for cp in l_g:
        cp.wait()
    l_dg.wait()
    l_mg.wait()
    for k in (2, 3, 1, 0):
        pulls_of(k)
        if k == 2:
            far_send(1)
            pass_on(0)
        elif k == 3:
            near_send(1, 0, 1)
        elif k == 1:
            near_send(1, 1, 0)
    l_unitt.wait()
    l_actt.wait()
    l_ctxt.wait()
    ones = jnp.ones((16, 2048), BF)
    sum_mix = dot(ones, mg[...])[0:8]
    sum_up = dot(ones, hl[...])[0:8]
    sum_g = dot(ones, g[...])[0:8]
    gains = jnp.concatenate([vec_ref[...], sum_up, sum_g], axis=0)
    col[...] = jnp.concatenate([gains, jnp.zeros((104, 768), F32)], axis=0).T

    grads[0, :, 0:768] = jnp.zeros((768, 768), BF)
    grads[0, out_rows, 0:768] = dot(ctxt[...], g[...]).astype(BF)

    @pl.loop(0, 3)
    def _(i):
        r = pl.ds(pl.multiple_of(i * 256, 256), 256)
        cols = col[r]

        def over_tokens(a, b):
            return sum(dot(a[n, r], b[n * 512 : n * 512 + 512]) for n in range(4))

        u1 = over_tokens(unitt, mg)
        wm = w[0, r, 768:1344].astype(F32)
        gain1 = jnp.sum(wm * u1, axis=-1, keepdims=True)
        shift1 = jnp.sum(wm * sum_mix[0:1], axis=-1, keepdims=True)
        dmix = u1 * cols[:, 0:1] + cols[:, 1:2] * sum_mix[0:1]
        u2 = over_tokens(unitt, hl)
        wu = w[1, r, 0:768].astype(F32)
        gain2 = jnp.sum(wu * u2, axis=-1, keepdims=True)
        shift2 = jnp.sum(wu * sum_up[0:1], axis=-1, keepdims=True)
        grads[1, r, 0:768] = (u2 * cols[:, 2:3] + cols[:, 3:4] * sum_up[0:1]).astype(BF)
        grads[1, r, 768:] = over_tokens(actt, g).astype(BF)
        lane = lax.broadcasted_iota(jnp.int32, (256, 192), 1)
        small = jnp.zeros((256, 192), F32)
        for n, v in enumerate((gain1, shift1, gain2, shift2, cols[:, 16:17], cols[:, 8:9])):
            small = jnp.where(lane == n, v, small)
        grads[0, r, 768:1536] = jnp.concatenate([dmix, small], axis=1).astype(BF)

    mixcol = jnp.concatenate([sum_mix, jnp.zeros((120, 576), F32)], axis=0).T
    col[pl.ds(0, 576)] = mixcol
    lane = lax.broadcasted_iota(jnp.int32, (192, 192), 1)
    more = jnp.zeros((192, 192), F32)
    for n in range(3):
        more = jnp.where(lane == 6 + n, col[pl.ds(n, 192, stride=3), 0:1], more)
    old = grads[0, out_rows, 768:1536].astype(F32)
    grads[0, out_rows, 768:1536] = (
        old + jnp.concatenate([jnp.zeros((192, 576), F32), more], axis=1)
    ).astype(BF)

    order = (1, 3, 2, 0)
    for k in order:
        for b in range(4):
            r = rows(lax.rem(here2 + k, 4), b, True)
            send(grads.at[1 - c, r], first_in.at[r], s0.at[k, b], r0.at[k, b], sibling)
    pass_on(1)
    for k in order:
        place = lax.rem(here1 + k, 4)
        for b in range(4):
            r = rows(place, b, False)
            landed(first_in.at[r], r0.at[k, b])
            grads[c, r] = (grads[c, r].astype(F32) + first_in[r].astype(F32)).astype(BF)
            if k:
                send(grads.at[c, r], second_in.at[k - 1, b], s1.at[k - 1, b], r1.at[k - 1, b], first(k))
    for h in range(2):
        o = total(0, h) + rows_ref[half[h]].astype(F32) + vec_ref[4:5]
        out_ref[half[h]] = o.astype(BF)
    for j in order:
        b = lax.rem(here2 + j, 4)
        r = rows(here1, b, False)
        acc = grads[c, r].astype(F32)
        for k in (1, 3, 2):
            landed(second_in.at[k - 1, b], r1.at[k - 1, b])
            acc = acc + second_in[k - 1, b].astype(F32)
        part[j] = acc.astype(BF)
        if j:
            send(part.at[j], third_in.at[j - 1], s2.at[j - 1], r2.at[j - 1], second(j))
    acc = part[0].astype(F32)
    for j in (1, 3, 2):
        landed(third_in.at[j - 1], r2.at[j - 1])
        acc = acc + third_in[j - 1].astype(F32)
    fin_ref[c, x] = acc.astype(BF)
    for k in (1, 3, 2):
        slot = fin_ref.at[c, x]
        send(slot, slot, s3.at[k - 1], r3.at[k - 1], (lax.rem(x + k, 4), me))
    slot = fin_ref.at[c, x]
    send(slot, slot, s4.at[0], r4.at[0], sibling)
    for h in range(2):
        s = total(1, h)
        v = rows_ref[half[h]].astype(F32)
        v = v - jnp.mean(v, axis=-1, keepdims=True)
        inverse = lax.rsqrt(jnp.mean(v * v, axis=-1, keepdims=True) + 1e-05)
        unit = v * inverse
        s = s - jnp.mean(s, axis=-1, keepdims=True) - unit * jnp.mean(s * unit, axis=-1, keepdims=True)
        own = pl.ds(pl.multiple_of(x * 512 + h * 256, 256), 256)
        back_ref[half[h]] = (g[own].astype(F32) + inverse * s).astype(BF)
    for k in (1, 3, 2):
        slot = fin_ref.at[c, lax.rem(x + 4 - k, 4)]
        landed(slot, r3.at[k - 1])
        send(slot, slot, s4.at[k], r4.at[k], sibling)
    for k in range(4):
        landed(fin_ref.at[1 - c, lax.rem(x + 4 - k, 4)], r4.at[k])
    for cp in started:
        cp.wait_send()


def tail(ctx, ctxt, mg, act, actt, dg, unitt, w, vec, g, rows):
    vm = pl.BlockSpec(memory_space=pltpu.VMEM)
    hbm = pl.BlockSpec(memory_space=pl.ANY)
    dma = pltpu.SemaphoreType.DMA
    return pl.pallas_call(
        tail_kernel,
        out_shape=(
            jax.ShapeDtypeStruct((512, 768), BF),
            jax.ShapeDtypeStruct((512, 768), BF),
            jax.ShapeDtypeStruct((2, 4, PAIR, WIDE), BF),
        ),
        in_specs=[hbm] * 8 + [vm] + [hbm] * 4 + [vm],
        out_specs=[vm, vm, vm],
        scratch_shapes=[
            pltpu.VMEM((2048, 192), BF),
            pltpu.VMEM((192, 2048), BF),
            pltpu.VMEM((2048, 576), BF),
            pltpu.VMEM((2048, 768), BF),
            pltpu.VMEM((4, 768, 512), BF),
            pltpu.VMEM((2048, 768), BF),
            pltpu.VMEM((4, 768, 512), BF),
            pltpu.VMEM((2, 768, WIDE), BF),
            pltpu.VMEM((2048, 768), BF),
            pltpu.VMEM((2, 4, 512, 768), BF),
            pltpu.VMEM((2, 2, 256, 768), BF),
            pltpu.VMEM((2, 2, 512, 768), BF),
            pltpu.VMEM((2, 768, WIDE), BF),
            pltpu.VMEM((768, WIDE), BF),
            pltpu.VMEM((3, 4, PAIR, WIDE), BF),
            pltpu.VMEM((4, PAIR, WIDE), BF),
            pltpu.VMEM((3, PAIR, WIDE), BF),
            pltpu.VMEM((768, 128), F32),
            dma((12,)),
            dma((2, 2)), dma((2, 2)), dma((2, 2, 2)), dma((2, 2, 2)),
            dma((4, 4)), dma((4, 4)), dma((3, 4)), dma((3, 4)), dma((3,)), dma((3,)),
            dma((3,)), dma((3,)), dma((4,)), dma((4,)),
        ],
        compiler_params=pltpu.CompilerParams(
            collective_id=1, has_side_effects=True, vmem_limit_bytes=60 * 1024 * 1024
        ),
        name="tail_all",
    )(ctx, ctxt, mg, act, actt, dg, unitt, w, vec, *g, rows)


def shift_x(v, k):
    return lax.ppermute(v, "seq", [(i, (i + k) % NX) for i in range(NX)])


def swap_core(v):
    return lax.ppermute(v, "shard", [(i, i ^ 1) for i in range(32)])


def local(
    inputs, positions, first_gain, first_shift, second_gain, second_shift, mix_weight, mix_bias,
    out_weight, out_bias, up_weight, up_bias, down_weight, down_bias, cotangent,
):
    x, _, _, c = places()
    is0 = c == 0
    none = functools.partial(jnp.zeros, dtype=BF)
    vectors = (first_gain, first_shift, second_gain, second_shift, out_bias, down_bias, none((48,)))
    flat = jnp.concatenate(vectors + (mix_bias, up_bias, none((24,))))
    packed = jnp.concatenate([flat.reshape(2, 192), none((22, 192))], axis=0)
    half_a = jnp.concatenate(
        [
            out_weight,
            lax.dynamic_slice_in_dim(mix_weight, x * 576, 576, 1),
            packed,
        ],
        axis=1,
    )
    up_part = lax.dynamic_index_in_dim(up_weight.reshape(24, 32, 4, 24), x, 2, keepdims=False)
    half_b = jnp.concatenate(
        [up_part.reshape(24, 768), lax.dynamic_slice_in_dim(down_weight, x * 24, 24, 0)], axis=1
    )
    kept = jnp.where(is0, half_a, half_b)
    came = swap_core(jnp.where(is0, half_b, half_a))
    pair = jnp.where(is0, jnp.concatenate([kept, came], 0), jnp.concatenate([came, kept], 0))
    pos_own = jnp.concatenate([positions.reshape(4, 128)] * 2, axis=0)
    grad = cotangent[0]
    mixed, act, actt, slope, unitt, context_grad, w, vec, table = front(inputs[0], grad, pair, pos_own)
    late, table = lax.optimization_barrier((grad, table))
    grads = [grad] + [shift_x(late, k) for k in (1, 2, 3)]
    context, context_t, mix_grad = attention(mixed, table, context_grad)
    outputs, input_grad, shares = tail(
        context, context_t, mix_grad, act, actt, slope, unitt, w, vec, grads, inputs[0]
    )
    shares = lax.dynamic_slice_in_dim(shares, c * 24, 24, 2).astype(F32)
    half_a, half_b = shares[0], shares[1]
    got_out = jnp.sum(half_a[:, :, :768], axis=0)
    got_mix = half_a[:, :, 768:1344].transpose(1, 0, 2).reshape(24, 2304)
    got_small = jnp.sum(half_a[:, :, 1344:1353], axis=0)
    got_bias = half_a[0, :, 1348]
    got_up = half_b[:, :, :768].reshape(4, 24, 32, 24).transpose(1, 2, 0, 3).reshape(24, 3072)
    got_down = half_b[:, :, 768:].reshape(96, 768)
    return (
        outputs[None],
        input_grad[None],
        got_small[:, 0],
        got_small[:, 1],
        got_small[:, 2],
        got_small[:, 3],
        got_mix,
        got_small[:, 6:9].reshape(72),
        got_out,
        got_bias,
        got_up,
        half_a[:, :, 1349].reshape(96),
        got_down,
        got_bias,
    )


def solution(mesh):
    vec, mat, tok = P("shard"), P("shard", None), P("shard", "seq", None)
    return jax.shard_map(
        local,
        mesh=mesh,
        in_specs=(tok, P("shard", "seq"), vec, vec, vec, vec, mat, vec, mat, vec, mat, vec, mat, vec, tok),
        out_specs=(tok, tok, vec, vec, vec, vec, mat, vec, mat, vec, mat, vec, mat, vec),
        check_vma=False,
    )
```

```python
import jax
import jax.numpy as jnp
from jax import lax
from jax.experimental import pallas as pl
from jax.experimental.pallas import tpu as pltpu
from jax.sharding import PartitionSpec as P

HD = 64
ROT = 16
NX = 4
BF = jnp.bfloat16
F32 = jnp.float32
MESH = pl.DeviceIdType.MESH
NT = (((1,), (1,)), ((), ()))
VMEM_LIMIT = 56 * 1024 * 1024
WIDE = 1536
PAIR = 48


def dot(a, b):
    return jnp.dot(a, b, preferred_element_type=F32)


def dot_nt(a, b):
    return lax.dot_general(a, b, NT, preferred_element_type=F32)


def dot_tn(a, b):
    return lax.dot_general(a, b, (((0,), (0,)), ((), ())), preferred_element_type=F32)


def places():
    x = lax.axis_index("seq")
    s = lax.axis_index("shard")
    return x, s // 8, (s // 2) % 4, s % 2


def at(x, z, y, c):
    return (x, (z * 4 + y) * 2 + c)


ERFC = (0.254829592, -0.284496736, 1.421413741, -1.453152027, 1.061405429)


def gelu_and_slope(h):
    t = 1.0 / (1.0 + (0.3275911 * 2.0**-0.5) * jnp.abs(h))
    e = jnp.exp(h * h * -0.5)
    poly = t * (ERFC[0] + t * (ERFC[1] + t * (ERFC[2] + t * (ERFC[3] + t * ERFC[4]))))
    tail_part = 0.5 * poly * e
    cdf = jnp.where(h >= 0, 1.0 - tail_part, tail_part)
    return h * cdf, cdf + h * e * 0.3989422804014327


def iota(shape, dim):
    return lax.broadcasted_iota(jnp.int32, shape, dim)


def front_kernel(
    rows_ref, grad_ref, pair_ref, pos_ref,
    mixed_o, act_o, actt_o, slope_o, unitt_o, cg_o, w_o, vec_o, table_o,
    rows_all, units, w, pos_all, grad, mixed, act, actt, slope, unitt, cg, cgs, vec, table,
    s1, r1, s2, r2, s3, r3, sx, rx, sf, rf, sp, rp, sc, rc, loc, wr,
):
    x, z, y, c = places()
    is0 = c == 0
    right, left, far = lax.rem(x + 1, 4), lax.rem(x + 3, 4), lax.rem(x + 2, 4)
    me = lax.axis_index("shard")
    mine, other = w.at[c], w.at[1 - c]

    def first(k):
        return at(x, jnp.where(is0, z, lax.rem(z + k, 4)), jnp.where(is0, lax.rem(y + k, 4), y), c)

    def second(k):
        return at(x, jnp.where(is0, lax.rem(z + k, 4), z), jnp.where(is0, y, lax.rem(y + k, 4)), c)

    def block(dz, dy):
        return lax.rem(z + dz, 4) * 4 + lax.rem(y + dy, 4)

    def held(a, b):
        da, db = (4 - a) % 4, (4 - b) % 4
        return jnp.where(is0, block(db, da), block(da, db))

    def rows_of(ref, b):
        return ref.at[pl.ds(pl.multiple_of(b * PAIR, 16), PAIR)]

    def quarter(who, q):
        return rows_all.at[pl.ds(pl.multiple_of(who * 512 + q * 128, 128), 128)]

    def remote(src, dst, ss, rs, dev):
        return pltpu.make_async_remote_copy(
            src_ref=src, dst_ref=dst, send_sem=ss, recv_sem=rs, device_id=dev, device_id_type=MESH
        )

    started = []

    def send(*args):
        cp = remote(*args)
        cp.start()
        started.append(cp)

    sibling = (x, me + 1 - 2 * c)

    def landed(dst, sem):
        remote(dst, dst, sem, sem, sibling).wait_recv()

    own_block = z * 4 + y
    own_pos = pos_all.at[pl.ds(pl.multiple_of(x * 8, 8), 8)]
    local_copies = []
    for n, (src, dst) in enumerate(
        (
            (pair_ref, rows_of(mine, own_block)),
            (rows_ref, rows_all.at[pl.ds(pl.multiple_of(x * 512, 512), 512)]),
            (pos_ref, own_pos),
            (grad_ref, grad),
        )
    ):
        cp = pltpu.make_async_copy(src, dst, loc.at[n])
        cp.start()
        local_copies.append(cp)
    barrier = pltpu.get_barrier_semaphore()
    peers = [first(k) for k in (1, 2, 3)] + [second(k) for k in (1, 2, 3)]
    peers += [sibling, (right, me), (left, me), (far, me)]
    for peer in peers:
        pl.semaphore_signal(barrier, inc=1, device_id=peer, device_id_type=MESH)
    pl.semaphore_wait(barrier, len(peers))

    order = (1, 3, 2)
    for k in order:
        send(pair_ref, rows_of(mine, own_block), s1.at[k - 1], r1.at[k - 1], first(k))
    own = [rows_ref.at[pl.ds(q * 128, 128)] for q in range(4)]
    for i in range(4):
        send(own[i], quarter(x, i), sx.at[0, i], rx.at[0, i], (right, me))
        send(own[3 - i], quarter(x, 3 - i), sx.at[1, 3 - i], rx.at[1, 3 - i], (left, me))
    for k in order:
        send(pair_ref, rows_of(mine, own_block), s2.at[0, k - 1], r2.at[0, k - 1], second(k))
    send(pair_ref, rows_of(mine, own_block), s3.at[0, 0], r3.at[0, 0], sibling)
    for k in order:
        send(pos_ref, own_pos, sp.at[k - 1], rp.at[k - 1], (lax.rem(x + k, 4), me))
    for cp in local_copies:
        cp.wait()

    writes = []

    def write(src, dst):
        cp = pltpu.make_async_copy(src, dst, wr.at[len(writes)])
        cp.start()
        writes.append(cp)

    def norm(who):
        @pl.loop(0, 2)
        def _(i):
            r = pl.ds(pl.multiple_of(who * 512 + i * 256, 256), 256)
            v = rows_all[r].astype(F32)
            v = v - jnp.mean(v, axis=-1, keepdims=True)
            unit = v * lax.rsqrt(jnp.mean(v * v, axis=-1, keepdims=True) + 1e-05)
            units[r] = unit
            unitt[who, :, pl.ds(pl.multiple_of(i * 256, 256), 256)] = unit.astype(BF).T

        write(unitt.at[who], unitt_o.at[who])

    for k in order:
        b = held(k, 0)
        landed(rows_of(mine, b), r1.at[k - 1])
        for j in order:
            send(rows_of(mine, b), rows_of(mine, b), s2.at[k, j - 1], r2.at[k, j - 1], second(j))
        send(rows_of(mine, b), rows_of(mine, b), s3.at[k, 0], r3.at[k, 0], sibling)

    norm(x)
    for k in order:
        src = lax.rem(x + 4 - k, 4)
        landed(pos_all.at[pl.ds(pl.multiple_of(src * 8, 8), 8)], rp.at[k - 1])
    place = jnp.concatenate(
        [pos_all[8 * d + q : 8 * d + q + 1] for d in range(4) for q in range(4)], axis=1
    ).astype(F32)
    freqs = jnp.ones((8, 2048), F32)
    for n in range(1, 8):
        freqs = jnp.where(iota((8, 2048), 0) == n, 10000.0 ** (-2.0 * n / ROT), freqs)
    angles = place * freqs
    cos8, sin8 = jnp.cos(angles), jnp.sin(angles)
    start = jnp.broadcast_to(iota((1, 2048), 1).astype(F32) - place, (8, 2048))
    table[...] = jnp.concatenate(
        [cos8, cos8, jnp.ones((48, 2048), F32), sin8, sin8, start, jnp.zeros((40, 2048), F32)], axis=0
    ).T

    for i in range(2):
        landed(quarter(left, i), rx.at[0, i])
        send(quarter(left, i), quarter(left, i), sf.at[0, i], rf.at[0, i], (right, me))
        landed(quarter(right, 3 - i), rx.at[1, 3 - i])
        send(quarter(right, 3 - i), quarter(right, 3 - i), sf.at[1, i], rf.at[1, i], (left, me))
    for j in order:
        for k in (0,) + order:
            b = held(k, j)
            landed(rows_of(mine, b), r2.at[k, j - 1])
            send(rows_of(mine, b), rows_of(mine, b), s3.at[k, j], r3.at[k, j], sibling)
    for i in range(2):
        landed(quarter(left, 2 + i), rx.at[0, 2 + i])
        landed(quarter(right, i), rx.at[1, i])
    norm(left)
    norm(right)
    for a in range(4):
        for b in range(4):
            da, db = (4 - a) % 4, (4 - b) % 4
            blk = jnp.where(is0, block(da, db), block(db, da))
            landed(rows_of(other, blk), r3.at[a, b])

    own_tok = pl.ds(pl.multiple_of(x * 512, 512), 512)
    for k in (2, 1, 3, 0):
        dev = lax.rem(x + k, 4)
        heads = w[0, pl.ds(pl.multiple_of(dev * 192, 64), 192), 0:768]

        @pl.loop(0, 2)
        def _(i):
            r = pl.ds(pl.multiple_of(i * 256, 256), 256)
            cgs[k, r] = dot_nt(grad[r], heads).astype(BF)

        if k:
            send(cgs.at[k], cg.at[own_tok], sc.at[k - 1], rc.at[k - 1], (dev, me))
        else:
            cg[own_tok] = cgs[0]

    packed = w[0, :, 1344:1536]
    pick = [dot((iota((32, 768), 1) == 24 * iota((32, 768), 0) + n).astype(BF), packed).astype(BF) for n in range(2)]

    def spread(src, width, base, group, shift):
        lane = iota((192, width), 1)
        one_hot = iota((192, width), 0) == lax.rem(lane, group) + base
        lane = iota((32, width), 1)
        keep = iota((32, width), 0) == lax.div(lane, group) + shift
        return jnp.sum(jnp.where(keep, dot(src, one_hot.astype(BF)), 0.0), axis=0, keepdims=True)

    g1, b1, g2, b2, out_b, down_b = (spread(pick[0], 768, 24 * n, 24, 0) for n in range(6))
    mix_b = spread(pick[1], 576, 0, 72, 8 * x)
    up_b = spread(pick[1], 768, 72 + 24 * x, 24, 0)
    vec[...] = jnp.concatenate([g1, b1, g2, b2, out_b + down_b, up_b, g1, g1], axis=0)

    write(w, w_o)
    write(vec, vec_o)
    write(table, table_o)

    def compute(who):
        @pl.loop(0, 2)
        def _(i):
            r = pl.ds(pl.multiple_of(who * 512 + i * 256, 256), 256)
            cols = pl.ds(pl.multiple_of(i * 256, 256), 256)
            unit = units[r]
            one = (unit * vec[0:1] + vec[1:2]).astype(BF)
            mixed[r] = (dot(one, w[0, :, 768:1344]) + mix_b).astype(BF)
            two = (unit * vec[2:3] + vec[3:4]).astype(BF)
            hidden = dot(two, w[1, :, 0:768]) + vec[5:6]
            a, s = gelu_and_slope(hidden)
            a = a.astype(BF)
            act[r] = a
            actt[who, :, cols] = a.T
            slope[r] = s.astype(BF)

        t = pl.ds(pl.multiple_of(who * 512, 512), 512)
        write(mixed.at[t], mixed_o.at[t])
        write(act.at[t], act_o.at[t])
        write(slope.at[t], slope_o.at[t])
        write(actt.at[who], actt_o.at[who])

    compute(x)
    compute(left)
    compute(right)
    for i in range(2):
        landed(quarter(far, i), rf.at[0, i])
        landed(quarter(far, 3 - i), rf.at[1, i])
    norm(far)
    compute(far)
    for k in (1, 3, 2):
        t = pl.ds(pl.multiple_of(lax.rem(x + 4 - k, 4) * 512, 512), 512)
        landed(cg.at[t], rc.at[k - 1])
    write(cg, cg_o)
    for cp in writes:
        cp.wait()
    for cp in started:
        cp.wait_send()


def front(rows, grad, pair, pos):
    hbm = pl.BlockSpec(memory_space=pl.ANY)
    dma = pltpu.SemaphoreType.DMA
    outs = [
        ((2048, 576), BF), ((2048, 768), BF), ((4, 768, 512), BF), ((2048, 768), BF), ((4, 768, 512), BF),
        ((2048, 192), BF), ((2, 768, WIDE), BF), ((8, 768), F32), ((2048, 128), F32),
    ]
    return pl.pallas_call(
        front_kernel,
        out_shape=tuple(jax.ShapeDtypeStruct(s, t) for s, t in outs),
        in_specs=[hbm] * 4,
        out_specs=[hbm] * 9,
        scratch_shapes=[
            pltpu.VMEM((2048, 768), BF),
            pltpu.VMEM((2048, 768), F32),
            pltpu.VMEM((2, 768, WIDE), BF),
            pltpu.VMEM((32, 128), jnp.int32),
            pltpu.VMEM((512, 768), BF),
            pltpu.VMEM((2048, 576), BF),
            pltpu.VMEM((2048, 768), BF),
            pltpu.VMEM((4, 768, 512), BF),
            pltpu.VMEM((2048, 768), BF),
            pltpu.VMEM((4, 768, 512), BF),
            pltpu.VMEM((2048, 192), BF),
            pltpu.VMEM((4, 512, 192), BF),
            pltpu.VMEM((8, 768), F32),
            pltpu.VMEM((2048, 128), F32),
            dma((3,)), dma((3,)), dma((4, 3)), dma((4, 3)), dma((4, 4)), dma((4, 4)),
            dma((2, 4)), dma((2, 4)), dma((2, 2)), dma((2, 2)), dma((3,)), dma((3,)), dma((3,)), dma((3,)),
            dma((4,)), dma((24,)),
        ],
        compiler_params=pltpu.CompilerParams(
            collective_id=0, has_side_effects=True, vmem_limit_bytes=VMEM_LIMIT
        ),
        name="front_all",
    )(rows, grad, pair, pos)


BQ = 256
NB = 2048 // BQ


def attention_kernel(
    mixed_ref, table_ref, grad_ref, ctx_ref, ctxt_ref, out_ref,
    qs, ks, vs, qt, ea, eb, sa, sb, dkt, dvt, dqs, os, gs,
):
    row, lane = iota((64, 64), 0), iota((64, 64), 1)
    turn = jnp.where((lane == row + 8) & (row < 8), 1.0, jnp.where((row == lane + 8) & (lane < 8), -1.0, 0.0))
    turn = turn.astype(BF)
    scores, expd = (sa, sb), (ea, eb)

    def angles(r):
        t = table_ref[r]
        return t[:, 0:64], jnp.where(iota((512, 64), 1) < ROT, t[:, 64:128], 0.0)

    def with_lanes(v, first, second):
        lane = iota((v.shape[0], 128), 1)
        wide = jnp.concatenate([v, jnp.zeros((v.shape[0], 64), F32)], axis=1)
        return jnp.where(lane == 64, first, jnp.where(lane == 65, second, wide)).astype(BF)

    @pl.loop(0, 4)
    def _(i):
        r = pl.ds(pl.multiple_of(i * 512, 512), 512)
        cosine, sine = angles(r)
        for h in range(3):
            q = mixed_ref[r, h * 192 : h * 192 + 64]
            k = mixed_ref[r, h * 192 + 64 : h * 192 + 128]
            v = mixed_ref[r, h * 192 + 128 : h * 192 + 192]
            q = q.astype(F32) * cosine + dot(q, turn) * sine
            k = k.astype(F32) * cosine + dot(k, turn) * sine
            q = q.astype(BF) * 0.125
            qs[h, r] = q
            qt[h, :, r] = q.astype(F32).T.astype(BF)
            ks[h, r] = k.astype(BF)
            vs[h, r] = with_lanes(v.astype(F32), 1.0, 1.0)
            gs[h, r] = grad_ref[r, h * 64 : h * 64 + 64]

    @pl.loop(0, 3)
    def _(h):
        dkt[h] = jnp.zeros((64, 2048), F32)
        dvt[h] = jnp.zeros((64, 2048), F32)
        top, wide, grad_t = {}, {}, {}

        def score(i):
            r, n = pl.ds(i * BQ, BQ), (i + 1) * BQ
            s = dot_nt(qs[h, r], ks[h, 0:n])
            start = table_ref[r, 80:81].astype(jnp.int32)
            middle = 512 <= i * BQ < 1536
            parts = []
            for a in range(0, n, BQ):
                part = s[:, a : a + BQ]
                cols = iota((BQ, BQ), 1)
                keep = None if middle and a >= 512 else cols >= start - a
                if a + BQ == n:
                    causal = cols <= iota((BQ, BQ), 0)
                    keep = causal if keep is None else keep & causal
                parts.append(part if keep is None else jnp.where(keep, part, -1e30))
            s = jnp.concatenate(parts, axis=1)
            scores[i % 2][:, 0:n] = s
            m = s[:, 0:128]
            for t in range(128, n, 128):
                m = jnp.maximum(m, s[:, t : t + 128])
            top[i] = jnp.max(m, axis=-1, keepdims=True)

        def probs(i):
            r, n = pl.ds(i * BQ, BQ), (i + 1) * BQ
            e = jnp.exp(scores[i % 2][:, 0:n] - top[i]).astype(BF)
            expd[i % 2][:, 0:n] = e
            acc = dot(e, vs[h, 0:n])
            inverse = 1.0 / acc[:, 64:65]
            o = acc[:, :64] * inverse
            os[h, r] = o.astype(BF)
            g = gs[h, r].astype(F32) * inverse
            delta = -jnp.sum(g * o, axis=-1, keepdims=True)
            high = delta.astype(BF).astype(F32)
            wide[i] = with_lanes(g, high, delta - high)
            grad_t[i] = g.T.astype(BF)

        def back(i):
            r, n = pl.ds(i * BQ, BQ), (i + 1) * BQ
            dp = dot_nt(wide[i], vs[h, 0:n])
            e = expd[i % 2][:, 0:n]
            ds = e * dp.astype(BF)
            dqs[h, r] = dot(ds, ks[h, 0:n]) * 0.125
            dkt[h, :, 0:n] += dot(qt[h, :, r], ds)
            dvt[h, :, 0:n] += dot(grad_t[i], e)

        for step in range(NB + 2):
            if step >= 2:
                back(step - 2)
            if 1 <= step <= NB:
                probs(step - 1)
            if step < NB:
                score(step)

    @pl.loop(0, 4)
    def _(i):
        r = pl.ds(pl.multiple_of(i * 512, 512), 512)
        cosine, sine = angles(r)

        def unturn(g):
            return g * cosine + dot_nt((g * sine).astype(BF), turn)

        parts = []
        for h in range(3):
            parts.append(unturn(dqs[h, r]))
            parts.append(unturn(dkt[h, :, r].T))
            parts.append(dvt[h, :, r].T)
        out_ref[r] = jnp.concatenate(parts, axis=1).astype(BF)
        ctx = jnp.concatenate([os[h, r].astype(F32) for h in range(3)], axis=1)
        ctx_ref[r] = ctx.astype(BF)
        ctxt_ref[:, r] = ctx.T.astype(BF)


def attention(mixed, table, grads):
    vm = pl.BlockSpec(memory_space=pltpu.VMEM)
    return pl.pallas_call(
        attention_kernel,
        out_shape=(
            jax.ShapeDtypeStruct((2048, 192), BF),
            jax.ShapeDtypeStruct((192, 2048), BF),
            jax.ShapeDtypeStruct((2048, 576), BF),
        ),
        in_specs=[vm] * 3,
        out_specs=[vm] * 3,
        scratch_shapes=[
            pltpu.VMEM((3, 2048, 64), BF),
            pltpu.VMEM((3, 2048, 64), BF),
            pltpu.VMEM((3, 2048, 128), BF),
            pltpu.VMEM((3, 64, 2048), BF),
            pltpu.VMEM((BQ, 2048), BF),
            pltpu.VMEM((BQ, 2048), BF),
            pltpu.VMEM((BQ, 2048), F32),
            pltpu.VMEM((BQ, 2048), F32),
            pltpu.VMEM((3, 64, 2048), F32),
            pltpu.VMEM((3, 64, 2048), F32),
            pltpu.VMEM((3, 2048, 64), F32),
            pltpu.VMEM((3, 2048, 64), BF),
            pltpu.VMEM((3, 2048, 64), BF),
        ],
        compiler_params=pltpu.CompilerParams(vmem_limit_bytes=VMEM_LIMIT),
        cost_estimate=pl.CostEstimate(
            flops=30_000_000_000, bytes_accessed=10_000_000, transcendentals=8_000_000
        ),
        name="attention_both",
    )(mixed, table, grads)


def tail_kernel(
    ctx_h, ctxt_h, mg_h, act_h, actt_h, dg_h, unitt_h, w_h, vec_ref, ga_h, gb_h, gc_h, gd_h, rows_ref,
    out_ref, back_ref, wout_ref, wmix_ref, wup_ref, wdown_ref, small_ref,
    ctx, ctxt, mg, act, actt, hl, unitt, w, g, buf, passed, got, grads, first_in, second_in, part, third_in, fin_ref, col,
    ld, sa, ra, sb, rb, s0, r0, s1, r1, s2, r2, s3, r3, s4, r4,
):
    x, z, y, c = places()
    is0 = c == 0
    me = lax.axis_index("shard")
    right, left = lax.rem(x + 1, 4), lax.rem(x + 3, 4)
    sibling = (x, me + 1 - 2 * c)

    def tok(k):
        return pl.ds(pl.multiple_of(lax.rem(x + 4 - k, 4) * 512, 512), 512)

    loads = []

    def load(src, dst):
        cp = pltpu.make_async_copy(src, dst, ld.at[len(loads)])
        cp.start()
        loads.append(cp)
        return cp

    l_ctx = load(ctx_h, ctx)
    l_w = load(w_h, w)
    l_act = load(act_h, act)
    l_g = [load(s, g.at[tok(k)]) for k, s in enumerate((ga_h, gb_h, gc_h, gd_h))]
    l_dg = load(dg_h, hl)
    l_mg = load(mg_h, mg)
    l_unitt = load(unitt_h, unitt)
    l_actt = load(actt_h, actt)
    l_ctxt = load(ctxt_h, ctxt)

    def first(k):
        return at(x, jnp.where(is0, lax.rem(z + k, 4), z), jnp.where(is0, y, lax.rem(y + k, 4)), c)

    def second(k):
        return at(x, jnp.where(is0, z, lax.rem(z + k, 4)), jnp.where(is0, lax.rem(y + k, 4), y), c)

    here1 = jnp.where(is0, z, y)
    here2 = jnp.where(is0, y, z)

    def rows(a, b, flip):
        blk = jnp.where(is0 != flip, a * 4 + b, b * 4 + a)
        return pl.ds(pl.multiple_of(blk * PAIR, 16), PAIR)

    barrier = pltpu.get_barrier_semaphore()
    peers = [first(k) for k in (1, 2, 3)] + [second(k) for k in (1, 2, 3)] + [sibling]
    peers += [(lax.rem(x + k, 4), me) for k in (1, 2, 3)]
    for peer in peers:
        pl.semaphore_signal(barrier, inc=1, device_id=peer, device_id_type=MESH)
    pl.semaphore_wait(barrier, len(peers))
    started = []

    def remote(src, dst, ss, rs, dev):
        cp = pltpu.make_async_remote_copy(
            src_ref=src, dst_ref=dst, send_sem=ss, recv_sem=rs, device_id=dev, device_id_type=MESH
        )
        return cp

    def send(*args):
        cp = remote(*args)
        cp.start()
        started.append(cp)

    def landed(dst, sem):
        remote(dst, dst, sem, sem, sibling).wait_recv()

    half = [pl.ds(0, 256), pl.ds(256, 256)]
    dev_x = [(right, me), (left, me)]

    def far_send(n):
        for d in range(2):
            send(buf.at[n, 2, half[d]], passed.at[n, d], sa.at[n, d], ra.at[n, d], dev_x[d])

    def near_send(n, d, h):
        send(buf.at[n, 3 - 2 * d, half[h]], got.at[n, d, half[h]], sb.at[n, d, h], rb.at[n, d, h], dev_x[d])

    def pass_on(n):
        for d in range(2):
            landed(passed.at[n, d], ra.at[n, d])
            k = 3 - 2 * d
            buf[n, k, half[d]] = (buf[n, k, half[d]].astype(F32) + passed[n, d].astype(F32)).astype(BF)
            near_send(n, d, d)

    def total(n, h):
        for d in range(2):
            landed(got.at[n, d, half[h]], rb.at[n, d, h])
        return buf[n, 0, half[h]].astype(F32) + got[n, 0, half[h]].astype(F32) + got[n, 1, half[h]].astype(F32)

    out_rows = pl.ds(pl.multiple_of(x * 192, 64), 192)

    def outputs_of(k):
        base = lax.rem(x + 4 - k, 4) * 512

        @pl.loop(0, 2)
        def _(i):
            r = pl.ds(pl.multiple_of(base + i * 256, 256), 256)
            o = dot(ctx[r], w[0, out_rows, 0:768]) + dot(act[r], w[1, :, 768:])
            buf[0, k, pl.ds(pl.multiple_of(i * 256, 256), 256)] = o.astype(BF)

    def pulls_of(k):
        base = lax.rem(x + 4 - k, 4) * 512

        @pl.loop(0, 2)
        def _(i):
            r = pl.ds(pl.multiple_of(base + i * 256, 256), 256)
            ag = dot_nt(g[r], w[1, :, 768:])
            low = (ag * hl[r].astype(F32)).astype(BF)
            hl[r] = low
            s = dot_nt(low, w[1, :, 0:768]) * vec_ref[2:3] + dot_nt(mg[r], w[0, :, 768:1344]) * vec_ref[0:1]
            buf[1, k, pl.ds(pl.multiple_of(i * 256, 256), 256)] = s.astype(BF)

    l_ctx.wait()
    l_w.wait()
    l_act.wait()
    for k in (2, 3, 1, 0):
        outputs_of(k)
        if k == 2:
            far_send(0)
        elif k == 3:
            near_send(0, 0, 1)
        elif k == 1:
            near_send(0, 1, 0)
    for cp in l_g:
        cp.wait()
    l_dg.wait()
    l_mg.wait()
    for k in (2, 3, 1, 0):
        pulls_of(k)
        if k == 2:
            far_send(1)
        elif k == 3:
            near_send(1, 0, 1)
        elif k == 1:
            near_send(1, 1, 0)
    pass_on(0)
    l_unitt.wait()
    l_actt.wait()
    l_ctxt.wait()
    ones = jnp.ones((16, 2048), BF)
    sum_mix = dot(ones, mg[...])[0:8]
    sum_up = dot(ones, hl[...])[0:8]
    sum_g = dot(ones, g[...])[0:8]
    gains = jnp.concatenate([vec_ref[...], sum_up, sum_g], axis=0)
    col[...] = jnp.concatenate([gains, jnp.zeros((104, 768), F32)], axis=0).T

    grads[0, :, 0:768] = jnp.zeros((768, 768), BF)
    grads[0, out_rows, 0:768] = dot(ctxt[...], g[...]).astype(BF)

    @pl.loop(0, 3)
    def _(i):
        r = pl.ds(pl.multiple_of(i * 256, 256), 256)
        cols = col[r]

        def over_tokens(a, b):
            return sum(dot(a[n, r], b[n * 512 : n * 512 + 512]) for n in range(4))

        u1 = over_tokens(unitt, mg)
        wm = w[0, r, 768:1344].astype(F32)
        gain1 = jnp.sum(wm * u1, axis=-1, keepdims=True)
        shift1 = jnp.sum(wm * sum_mix[0:1], axis=-1, keepdims=True)
        dmix = u1 * cols[:, 0:1] + cols[:, 1:2] * sum_mix[0:1]
        u2 = over_tokens(unitt, hl)
        wu = w[1, r, 0:768].astype(F32)
        gain2 = jnp.sum(wu * u2, axis=-1, keepdims=True)
        shift2 = jnp.sum(wu * sum_up[0:1], axis=-1, keepdims=True)
        grads[1, r, 0:768] = (u2 * cols[:, 2:3] + cols[:, 3:4] * sum_up[0:1]).astype(BF)
        grads[1, r, 768:] = over_tokens(actt, g).astype(BF)
        lane = lax.broadcasted_iota(jnp.int32, (256, 192), 1)
        small = jnp.zeros((256, 192), F32)
        for n, v in enumerate((gain1, shift1, gain2, shift2, cols[:, 16:17], cols[:, 8:9])):
            small = jnp.where(lane == n, v, small)
        grads[0, r, 768:1536] = jnp.concatenate([dmix, small], axis=1).astype(BF)

    mixcol = jnp.concatenate([sum_mix, jnp.zeros((120, 576), F32)], axis=0).T
    col[pl.ds(0, 576)] = mixcol
    lane = lax.broadcasted_iota(jnp.int32, (192, 192), 1)
    more = jnp.zeros((192, 192), F32)
    for n in range(3):
        more = jnp.where(lane == 6 + n, col[pl.ds(n, 192, stride=3), 0:1], more)
    old = grads[0, out_rows, 768:1536].astype(F32)
    grads[0, out_rows, 768:1536] = (
        old + jnp.concatenate([jnp.zeros((192, 576), F32), more], axis=1)
    ).astype(BF)

    order = (1, 3, 2, 0)
    for k in order:
        for b in range(4):
            r = rows(lax.rem(here2 + k, 4), b, True)
            send(grads.at[1 - c, r], first_in.at[r], s0.at[k, b], r0.at[k, b], sibling)
    for k in order:
        place = lax.rem(here1 + k, 4)
        for b in range(4):
            r = rows(place, b, False)
            landed(first_in.at[r], r0.at[k, b])
            grads[c, r] = (grads[c, r].astype(F32) + first_in[r].astype(F32)).astype(BF)
            if k:
                send(grads.at[c, r], second_in.at[k - 1, b], s1.at[k - 1, b], r1.at[k - 1, b], first(k))
    pass_on(1)
    lane = iota((1, WIDE), 1)
    group = lax.rem(lax.div(lane, 24), 4)
    source = lax.div(lane, 96) * 24 + lax.rem(lane, 24)
    for d in range(4):
        hot = iota((384, WIDE), 0) == jnp.where(group == d, source, -1)
        w[d // 2, (d % 2) * 384 : (d % 2) * 384 + 384] = hot.astype(F32).astype(BF)
    for j in order:
        b = lax.rem(here2 + j, 4)
        r = rows(here1, b, False)
        acc = grads[c, r].astype(F32)
        for k in (1, 3, 2):
            landed(second_in.at[k - 1, b], r1.at[k - 1, b])
            acc = acc + second_in[k - 1, b].astype(F32)
        part[j] = acc.astype(BF)
        if j:
            send(part.at[j], third_in.at[j - 1], s2.at[j - 1], r2.at[j - 1], second(j))
    for h in range(2):
        o = total(0, h) + rows_ref[half[h]].astype(F32) + vec_ref[4:5]
        out_ref[half[h]] = o.astype(BF)
    acc = part[0].astype(F32)
    for j in (1, 3, 2):
        landed(third_in.at[j - 1], r2.at[j - 1])
        acc = acc + third_in[j - 1].astype(F32)
    fin_ref[c, x] = acc.astype(BF)
    for k in (1, 3, 2):
        slot = fin_ref.at[c, x]
        send(slot, slot, s3.at[k - 1], r3.at[k - 1], (lax.rem(x + k, 4), me))
    slot = fin_ref.at[c, x]
    send(slot, slot, s4.at[0], r4.at[0], sibling)
    for h in range(2):
        s = total(1, h)
        v = rows_ref[half[h]].astype(F32)
        v = v - jnp.mean(v, axis=-1, keepdims=True)
        inverse = lax.rsqrt(jnp.mean(v * v, axis=-1, keepdims=True) + 1e-05)
        unit = v * inverse
        s = s - jnp.mean(s, axis=-1, keepdims=True) - unit * jnp.mean(s * unit, axis=-1, keepdims=True)
        own = pl.ds(pl.multiple_of(x * 512 + h * 256, 256), 256)
        back_ref[half[h]] = (g[own].astype(F32) + inverse * s).astype(BF)
    for k in (1, 3, 2):
        slot = fin_ref.at[c, lax.rem(x + 4 - k, 4)]
        landed(slot, r3.at[k - 1])
        send(slot, slot, s4.at[k], r4.at[k], sibling)
    for k in range(4):
        landed(fin_ref.at[1 - c, lax.rem(x + 4 - k, 4)], r4.at[k])

    def mine(role, d, a, b):
        v = fin_ref[role, d, :, a:b].astype(F32)
        return jnp.where(is0, v[0:24], v[24:48])

    wout_ref[...] = sum(mine(0, d, 0, 768) for d in range(4))
    tails = [mine(0, d, 768, WIDE) for d in range(4)]
    wmix_ref[...] = jnp.concatenate([t[:, 0:576] for t in tails], axis=1)
    lane = iota((24, 128), 1)
    small = sum(t[:, 576:704] for t in tails)
    for d in range(4):
        small = jnp.where(lane == 16 + d, tails[d][:, 581:582], small)
    small_ref[...] = jnp.where(lane == 4, tails[0][:, 576:704], small)
    ups = [mine(1, d, 0, 768).astype(BF) for d in range(4)]
    for n in range(2):
        wup_ref[:, n * WIDE : n * WIDE + WIDE] = sum(
            dot(ups[d][:, n * 384 : n * 384 + 384], w[d // 2, (d % 2) * 384 : (d % 2) * 384 + 384])
            for d in range(4)
        )
    for d in range(4):
        wdown_ref[d * 24 : d * 24 + 24] = mine(1, d, 768, WIDE)
    for cp in started:
        cp.wait_send()


def tail(ctx, ctxt, mg, act, actt, dg, unitt, w, vec, g, rows):
    vm = pl.BlockSpec(memory_space=pltpu.VMEM)
    hbm = pl.BlockSpec(memory_space=pl.ANY)
    dma = pltpu.SemaphoreType.DMA
    return pl.pallas_call(
        tail_kernel,
        out_shape=(
            jax.ShapeDtypeStruct((512, 768), BF),
            jax.ShapeDtypeStruct((512, 768), BF),
            jax.ShapeDtypeStruct((24, 768), F32),
            jax.ShapeDtypeStruct((24, 2304), F32),
            jax.ShapeDtypeStruct((24, 3072), F32),
            jax.ShapeDtypeStruct((96, 768), F32),
            jax.ShapeDtypeStruct((24, 128), F32),
        ),
        in_specs=[hbm] * 8 + [vm] + [hbm] * 4 + [vm],
        out_specs=[vm] * 7,
        scratch_shapes=[
            pltpu.VMEM((2048, 192), BF),
            pltpu.VMEM((192, 2048), BF),
            pltpu.VMEM((2048, 576), BF),
            pltpu.VMEM((2048, 768), BF),
            pltpu.VMEM((4, 768, 512), BF),
            pltpu.VMEM((2048, 768), BF),
            pltpu.VMEM((4, 768, 512), BF),
            pltpu.VMEM((2, 768, WIDE), BF),
            pltpu.VMEM((2048, 768), BF),
            pltpu.VMEM((2, 4, 512, 768), BF),
            pltpu.VMEM((2, 2, 256, 768), BF),
            pltpu.VMEM((2, 2, 512, 768), BF),
            pltpu.VMEM((2, 768, WIDE), BF),
            pltpu.VMEM((768, WIDE), BF),
            pltpu.VMEM((3, 4, PAIR, WIDE), BF),
            pltpu.VMEM((4, PAIR, WIDE), BF),
            pltpu.VMEM((3, PAIR, WIDE), BF),
            pltpu.VMEM((2, 4, PAIR, WIDE), BF),
            pltpu.VMEM((768, 128), F32),
            dma((12,)),
            dma((2, 2)), dma((2, 2)), dma((2, 2, 2)), dma((2, 2, 2)),
            dma((4, 4)), dma((4, 4)), dma((3, 4)), dma((3, 4)), dma((3,)), dma((3,)),
            dma((3,)), dma((3,)), dma((4,)), dma((4,)),
        ],
        compiler_params=pltpu.CompilerParams(
            collective_id=1, has_side_effects=True, vmem_limit_bytes=60 * 1024 * 1024
        ),
        name="tail_all",
    )(ctx, ctxt, mg, act, actt, dg, unitt, w, vec, *g, rows)


def shift_x(v, k):
    return lax.ppermute(v, "seq", [(i, (i + k) % NX) for i in range(NX)])


def swap_core(v):
    return lax.ppermute(v, "shard", [(i, i ^ 1) for i in range(32)])


def local(
    inputs, positions, first_gain, first_shift, second_gain, second_shift, mix_weight, mix_bias,
    out_weight, out_bias, up_weight, up_bias, down_weight, down_bias, cotangent,
):
    x, _, _, c = places()
    is0 = c == 0
    flat = jnp.zeros((384,), BF)
    for place, v in (
        (0, first_gain), (24, first_shift), (48, second_gain), (72, second_shift), (96, out_bias),
        (120, down_bias), (192, mix_bias), (264, up_bias),
    ):
        flat = flat + jnp.pad(v, (place, 384 - place - v.shape[0]))
    packed = jnp.pad(flat.reshape(2, 192), ((0, 22), (0, 0)))
    half_a = jnp.concatenate(
        [
            out_weight,
            lax.dynamic_slice_in_dim(mix_weight, x * 576, 576, 1),
            packed,
        ],
        axis=1,
    )
    up_part = lax.dynamic_index_in_dim(up_weight.reshape(24, 32, 4, 24), x, 2, keepdims=False)
    half_b = jnp.concatenate(
        [up_part.reshape(24, 768), lax.dynamic_slice_in_dim(down_weight, x * 24, 24, 0)], axis=1
    )
    kept = jnp.where(is0, half_a, half_b)
    came = swap_core(jnp.where(is0, half_b, half_a))
    pair = jnp.where(is0, jnp.concatenate([kept, came], 0), jnp.concatenate([came, kept], 0))
    pos_own = jnp.concatenate([positions.reshape(4, 128)] * 2, axis=0)
    grad = cotangent[0]
    mixed, act, actt, slope, unitt, context_grad, w, vec, table = front(inputs[0], grad, pair, pos_own)
    late, table = lax.optimization_barrier((grad, table))
    grads = [grad] + [shift_x(late, k) for k in (1, 2, 3)]
    context, context_t, mix_grad = attention(mixed, table, context_grad)
    outputs, input_grad, g_out, g_mix, g_up, g_down, small = tail(
        context, context_t, mix_grad, act, actt, slope, unitt, w, vec, grads, inputs[0]
    )
    return (
        outputs[None],
        input_grad[None],
        small[:, 0],
        small[:, 1],
        small[:, 2],
        small[:, 3],
        g_mix,
        small[:, 6:9].reshape(72),
        g_out,
        small[:, 4],
        g_up,
        small[:, 16:20].T.reshape(96),
        g_down,
        small[:, 4],
    )


def solution(mesh):
    vec, mat, tok = P("shard"), P("shard", None), P("shard", "seq", None)
    return jax.shard_map(
        local,
        mesh=mesh,
        in_specs=(tok, P("shard", "seq"), vec, vec, vec, vec, mat, vec, mat, vec, mat, vec, mat, vec, tok),
        out_specs=(tok, tok, vec, vec, vec, vec, mat, vec, mat, vec, mat, vec, mat, vec),
        check_vma=False,
    )
```

```python
import jax
import jax.numpy as jnp
from jax import lax
from jax.experimental import pallas as pl
from jax.experimental.pallas import tpu as pltpu
from jax.sharding import PartitionSpec as P

HD = 64
ROT = 16
NX = 4
BF = jnp.bfloat16
F32 = jnp.float32
MESH = pl.DeviceIdType.MESH
NT = (((1,), (1,)), ((), ()))
VMEM_LIMIT = 56 * 1024 * 1024
WIDE = 1536
PAIR = 48


def dot(a, b):
    return jnp.dot(a, b, preferred_element_type=F32)


def dot_nt(a, b):
    return lax.dot_general(a, b, NT, preferred_element_type=F32)


def dot_tn(a, b):
    return lax.dot_general(a, b, (((0,), (0,)), ((), ())), preferred_element_type=F32)


def places():
    x = lax.axis_index("seq")
    s = lax.axis_index("shard")
    return x, s // 8, (s // 2) % 4, s % 2


def at(x, z, y, c):
    return (x, (z * 4 + y) * 2 + c)


ERFC = (0.254829592, -0.284496736, 1.421413741, -1.453152027, 1.061405429)


def gelu_and_slope(h):
    t = 1.0 / (1.0 + (0.3275911 * 2.0**-0.5) * jnp.abs(h))
    e = jnp.exp(h * h * -0.5)
    poly = t * (ERFC[0] + t * (ERFC[1] + t * (ERFC[2] + t * (ERFC[3] + t * ERFC[4]))))
    tail_part = 0.5 * poly * e
    cdf = jnp.where(h >= 0, 1.0 - tail_part, tail_part)
    return h * cdf, cdf + h * e * 0.3989422804014327


def iota(shape, dim):
    return lax.broadcasted_iota(jnp.int32, shape, dim)


def front_kernel(
    rows_ref, grad_ref, pos_ref, packed_ref, mix_ref, out_ref, up_ref, down_ref,
    mixed_o, act_o, actt_o, slope_o, unitt_o, cg_o, w_o, vec_o, table_o,
    rows_all, units, w, pos_all, grad, mixed, act, actt, slope, unitt, cg, cgs, vec, table, give, came, pair_ref,
    s1, r1, s2, r2, s3, r3, sx, rx, sf, rf, sp, rp, sc, rc, sg, rg, loc, wr,
):
    x, z, y, c = places()
    is0 = c == 0
    right, left, far = lax.rem(x + 1, 4), lax.rem(x + 3, 4), lax.rem(x + 2, 4)
    me = lax.axis_index("shard")
    mine, other = w.at[c], w.at[1 - c]

    def first(k):
        return at(x, jnp.where(is0, z, lax.rem(z + k, 4)), jnp.where(is0, lax.rem(y + k, 4), y), c)

    def second(k):
        return at(x, jnp.where(is0, lax.rem(z + k, 4), z), jnp.where(is0, y, lax.rem(y + k, 4)), c)

    def block(dz, dy):
        return lax.rem(z + dz, 4) * 4 + lax.rem(y + dy, 4)

    def held(a, b):
        da, db = (4 - a) % 4, (4 - b) % 4
        return jnp.where(is0, block(db, da), block(da, db))

    def rows_of(ref, b):
        return ref.at[pl.ds(pl.multiple_of(b * PAIR, 16), PAIR)]

    def quarter(who, q):
        return rows_all.at[pl.ds(pl.multiple_of(who * 512 + q * 128, 128), 128)]

    def remote(src, dst, ss, rs, dev):
        return pltpu.make_async_remote_copy(
            src_ref=src, dst_ref=dst, send_sem=ss, recv_sem=rs, device_id=dev, device_id_type=MESH
        )

    started = []

    def send(*args):
        cp = remote(*args)
        cp.start()
        started.append(cp)

    sibling = (x, me + 1 - 2 * c)

    def landed(dst, sem):
        remote(dst, dst, sem, sem, sibling).wait_recv()

    own_block = z * 4 + y
    own_pos = pos_all.at[x]
    local_copies = []
    for n, (src, dst) in enumerate(
        (
            (rows_ref, rows_all.at[pl.ds(pl.multiple_of(x * 512, 512), 512)]),
            (pos_ref, own_pos),
            (grad_ref, grad),
        )
    ):
        cp = pltpu.make_async_copy(src, dst, loc.at[n])
        cp.start()
        local_copies.append(cp)
    barrier = pltpu.get_barrier_semaphore()
    peers = [first(k) for k in (1, 2, 3)] + [second(k) for k in (1, 2, 3)]
    peers += [sibling, (right, me), (left, me), (far, me)]
    for peer in peers:
        pl.semaphore_signal(barrier, inc=1, device_id=peer, device_id_type=MESH)
    pl.semaphore_wait(barrier, len(peers))

    order = (1, 3, 2)
    own = [rows_ref.at[pl.ds(q * 128, 128)] for q in range(4)]
    for i in range(4):
        send(own[i], quarter(x, i), sx.at[0, i], rx.at[0, i], (right, me))
        send(own[3 - i], quarter(x, 3 - i), sx.at[1, 3 - i], rx.at[1, 3 - i], (left, me))
    for k in order:
        send(pos_ref, own_pos, sp.at[k - 1], rp.at[k - 1], (lax.rem(x + k, 4), me))

    def pick_x(parts):
        v = parts[0]
        for d in range(1, 4):
            v = jnp.where(x == d, parts[d], v)
        return v

    mix_part = pick_x([mix_ref[:, d * 576 : d * 576 + 576].astype(F32) for d in range(4)])
    half_a = jnp.concatenate([out_ref[...].astype(F32), mix_part, packed_ref[...].astype(F32)], axis=1)
    lane = iota((1, 384), 1)
    hot = iota((WIDE, 384), 0) == lax.div(lane, 24) * 96 + lax.rem(lane, 24) + 24 * x
    hot = hot.astype(F32).astype(BF)
    down_own = down_ref[...].astype(F32)
    half_b = jnp.concatenate(
        [dot(up_ref[:, 0:WIDE], hot), dot(up_ref[:, WIDE:], hot), pick_x([down_own[d * 24 : d * 24 + 24] for d in range(4)])],
        axis=1,
    )
    give[...] = jnp.concatenate([jnp.where(is0, half_b, half_a), jnp.zeros((8, WIDE), F32)], axis=0).astype(BF)
    send(give, came, sg.at[0], rg.at[0], sibling)
    for cp in local_copies:
        cp.wait()
    writes = []

    def write(src, dst):
        cp = pltpu.make_async_copy(src, dst, wr.at[len(writes)])
        cp.start()
        writes.append(cp)

    def norm(who):
        @pl.loop(0, 2)
        def _(i):
            r = pl.ds(pl.multiple_of(who * 512 + i * 256, 256), 256)
            v = rows_all[r].astype(F32)
            v = v - jnp.mean(v, axis=-1, keepdims=True)
            unit = v * lax.rsqrt(jnp.mean(v * v, axis=-1, keepdims=True) + 1e-05)
            units[r] = unit
            unitt[who, :, pl.ds(pl.multiple_of(i * 256, 256), 256)] = unit.astype(BF).T

        write(unitt.at[who], unitt_o.at[who])

    norm(x)
    landed(came, rg.at[0])
    theirs = came[...].astype(F32)[0:24]
    kept = jnp.where(is0, half_a, half_b)
    pair = jnp.concatenate([jnp.where(is0, kept, theirs), jnp.where(is0, theirs, kept)], axis=0).astype(BF)
    pair_ref[...] = pair
    w[c, pl.ds(pl.multiple_of(own_block * PAIR, 16), PAIR)] = pair
    for k in order:
        send(pair_ref, rows_of(mine, own_block), s1.at[k - 1], r1.at[k - 1], first(k))
    for k in order:
        send(pair_ref, rows_of(mine, own_block), s2.at[0, k - 1], r2.at[0, k - 1], second(k))
    send(pair_ref, rows_of(mine, own_block), s3.at[0, 0], r3.at[0, 0], sibling)

    for k in order:
        b = held(k, 0)
        landed(rows_of(mine, b), r1.at[k - 1])
        for j in order:
            send(rows_of(mine, b), rows_of(mine, b), s2.at[k, j - 1], r2.at[k, j - 1], second(j))
        send(rows_of(mine, b), rows_of(mine, b), s3.at[k, 0], r3.at[k, 0], sibling)

    for k in order:
        landed(pos_all.at[lax.rem(x + 4 - k, 4)], rp.at[k - 1])
    place = jnp.concatenate([pos_all[d] for d in range(4)], axis=1).astype(F32)
    freqs = jnp.ones((8, 2048), F32)
    for n in range(1, 8):
        freqs = jnp.where(iota((8, 2048), 0) == n, 10000.0 ** (-2.0 * n / ROT), freqs)
    angles = place * freqs
    cos8, sin8 = jnp.cos(angles), jnp.sin(angles)
    start = jnp.broadcast_to(iota((1, 2048), 1).astype(F32) - place, (8, 2048))
    table[...] = jnp.concatenate(
        [cos8, cos8, jnp.ones((48, 2048), F32), sin8, sin8, start, jnp.zeros((40, 2048), F32)], axis=0
    ).T

    for i in range(2):
        landed(quarter(left, i), rx.at[0, i])
        send(quarter(left, i), quarter(left, i), sf.at[0, i], rf.at[0, i], (right, me))
        landed(quarter(right, 3 - i), rx.at[1, 3 - i])
        send(quarter(right, 3 - i), quarter(right, 3 - i), sf.at[1, i], rf.at[1, i], (left, me))
    for j in order:
        for k in (0,) + order:
            b = held(k, j)
            landed(rows_of(mine, b), r2.at[k, j - 1])
            send(rows_of(mine, b), rows_of(mine, b), s3.at[k, j], r3.at[k, j], sibling)
    for i in range(2):
        landed(quarter(left, 2 + i), rx.at[0, 2 + i])
        landed(quarter(right, i), rx.at[1, i])
    norm(left)
    norm(right)
    for a in range(4):
        for b in range(4):
            da, db = (4 - a) % 4, (4 - b) % 4
            blk = jnp.where(is0, block(da, db), block(db, da))
            landed(rows_of(other, blk), r3.at[a, b])

    own_tok = pl.ds(pl.multiple_of(x * 512, 512), 512)
    for k in (2, 1, 3, 0):
        dev = lax.rem(x + k, 4)
        heads = w[0, pl.ds(pl.multiple_of(dev * 192, 64), 192), 0:768]

        @pl.loop(0, 2)
        def _(i):
            r = pl.ds(pl.multiple_of(i * 256, 256), 256)
            cgs[k, r] = dot_nt(grad[r], heads).astype(BF)

        if k:
            send(cgs.at[k], cg.at[own_tok], sc.at[k - 1], rc.at[k - 1], (dev, me))
        else:
            cg[own_tok] = cgs[0]

    packed = w[0, :, 1344:1536]
    pick = [dot((iota((32, 768), 1) == 24 * iota((32, 768), 0) + n).astype(BF), packed).astype(BF) for n in range(2)]

    def spread(src, width, base, group, shift):
        lane = iota((192, width), 1)
        one_hot = iota((192, width), 0) == lax.rem(lane, group) + base
        lane = iota((32, width), 1)
        keep = iota((32, width), 0) == lax.div(lane, group) + shift
        return jnp.sum(jnp.where(keep, dot(src, one_hot.astype(BF)), 0.0), axis=0, keepdims=True)

    g1, b1, g2, b2, out_b, down_b = (spread(pick[0], 768, 24 * n, 24, 0) for n in range(6))
    mix_b = spread(pick[1], 576, 0, 72, 8 * x)
    up_b = spread(pick[1], 768, 72 + 24 * x, 24, 0)
    vec[...] = jnp.concatenate([g1, b1, g2, b2, out_b + down_b, up_b, g1, g1], axis=0)

    write(w, w_o)
    write(vec, vec_o)
    write(table, table_o)

    def compute(who):
        @pl.loop(0, 2)
        def _(i):
            r = pl.ds(pl.multiple_of(who * 512 + i * 256, 256), 256)
            cols = pl.ds(pl.multiple_of(i * 256, 256), 256)
            unit = units[r]
            one = (unit * vec[0:1] + vec[1:2]).astype(BF)
            mixed[r] = (dot(one, w[0, :, 768:1344]) + mix_b).astype(BF)
            two = (unit * vec[2:3] + vec[3:4]).astype(BF)
            hidden = dot(two, w[1, :, 0:768]) + vec[5:6]
            a, s = gelu_and_slope(hidden)
            a = a.astype(BF)
            act[r] = a
            actt[who, :, cols] = a.T
            slope[r] = s.astype(BF)

        t = pl.ds(pl.multiple_of(who * 512, 512), 512)
        write(mixed.at[t], mixed_o.at[t])
        write(act.at[t], act_o.at[t])
        write(slope.at[t], slope_o.at[t])
        write(actt.at[who], actt_o.at[who])

    compute(x)
    compute(left)
    compute(right)
    for i in range(2):
        landed(quarter(far, i), rf.at[0, i])
        landed(quarter(far, 3 - i), rf.at[1, i])
    norm(far)
    compute(far)
    for k in (1, 3, 2):
        t = pl.ds(pl.multiple_of(lax.rem(x + 4 - k, 4) * 512, 512), 512)
        landed(cg.at[t], rc.at[k - 1])
    write(cg, cg_o)
    for cp in writes:
        cp.wait()
    for cp in started:
        cp.wait_send()


def front(rows, grad, pos, packed, mix, out, up, down):
    hbm = pl.BlockSpec(memory_space=pl.ANY)
    vm = pl.BlockSpec(memory_space=pltpu.VMEM)
    dma = pltpu.SemaphoreType.DMA
    outs = [
        ((2048, 576), BF), ((2048, 768), BF), ((4, 768, 512), BF), ((2048, 768), BF), ((4, 768, 512), BF),
        ((2048, 192), BF), ((2, 768, WIDE), BF), ((8, 768), F32), ((2048, 128), F32),
    ]
    return pl.pallas_call(
        front_kernel,
        out_shape=tuple(jax.ShapeDtypeStruct(s, t) for s, t in outs),
        in_specs=[hbm] * 2 + [vm] * 6,
        out_specs=[hbm] * 9,
        scratch_shapes=[
            pltpu.VMEM((2048, 768), BF),
            pltpu.VMEM((2048, 768), F32),
            pltpu.VMEM((2, 768, WIDE), BF),
            pltpu.VMEM((4, 1, 512), jnp.int32),
            pltpu.VMEM((512, 768), BF),
            pltpu.VMEM((2048, 576), BF),
            pltpu.VMEM((2048, 768), BF),
            pltpu.VMEM((4, 768, 512), BF),
            pltpu.VMEM((2048, 768), BF),
            pltpu.VMEM((4, 768, 512), BF),
            pltpu.VMEM((2048, 192), BF),
            pltpu.VMEM((4, 512, 192), BF),
            pltpu.VMEM((8, 768), F32),
            pltpu.VMEM((2048, 128), F32),
            pltpu.VMEM((32, WIDE), BF),
            pltpu.VMEM((32, WIDE), BF),
            pltpu.VMEM((PAIR, WIDE), BF),
            dma((3,)), dma((3,)), dma((4, 3)), dma((4, 3)), dma((4, 4)), dma((4, 4)),
            dma((2, 4)), dma((2, 4)), dma((2, 2)), dma((2, 2)), dma((3,)), dma((3,)), dma((3,)), dma((3,)),
            dma((1,)), dma((1,)), dma((3,)), dma((24,)),
        ],
        compiler_params=pltpu.CompilerParams(
            collective_id=0, has_side_effects=True, vmem_limit_bytes=VMEM_LIMIT
        ),
        name="front_all",
    )(rows, grad, pos, packed, mix, out, up, down)


BQ = 256
NB = 2048 // BQ


def attention_kernel(
    mixed_ref, table_ref, grad_ref, ctx_ref, ctxt_ref, out_ref,
    qs, ks, vs, qt, ea, eb, sa, sb, dkt, dvt, dqs, os, gs,
):
    row, lane = iota((64, 64), 0), iota((64, 64), 1)
    turn = jnp.where((lane == row + 8) & (row < 8), 1.0, jnp.where((row == lane + 8) & (lane < 8), -1.0, 0.0))
    turn = turn.astype(BF)
    scores, expd = (sa, sb), (ea, eb)

    def angles(r):
        t = table_ref[r]
        return t[:, 0:64], jnp.where(iota((512, 64), 1) < ROT, t[:, 64:128], 0.0)

    def with_lanes(v, first, second):
        lane = iota((v.shape[0], 128), 1)
        wide = jnp.concatenate([v, jnp.zeros((v.shape[0], 64), F32)], axis=1)
        return jnp.where(lane == 64, first, jnp.where(lane == 65, second, wide)).astype(BF)

    @pl.loop(0, 4)
    def _(i):
        r = pl.ds(pl.multiple_of(i * 512, 512), 512)
        cosine, sine = angles(r)
        for h in range(3):
            q = mixed_ref[r, h * 192 : h * 192 + 64]
            k = mixed_ref[r, h * 192 + 64 : h * 192 + 128]
            v = mixed_ref[r, h * 192 + 128 : h * 192 + 192]
            q = q.astype(F32) * cosine + dot(q, turn) * sine
            k = k.astype(F32) * cosine + dot(k, turn) * sine
            q = q.astype(BF) * 0.125
            qs[h, r] = q
            qt[h, :, r] = q.astype(F32).T.astype(BF)
            ks[h, r] = k.astype(BF)
            vs[h, r] = with_lanes(v.astype(F32), 1.0, 1.0)
            gs[h, r] = grad_ref[r, h * 64 : h * 64 + 64]

    @pl.loop(0, 3)
    def _(h):
        dkt[h] = jnp.zeros((64, 2048), F32)
        dvt[h] = jnp.zeros((64, 2048), F32)
        top, wide, grad_t = {}, {}, {}

        def score(i):
            r, n = pl.ds(i * BQ, BQ), (i + 1) * BQ
            s = dot_nt(qs[h, r], ks[h, 0:n])
            start = table_ref[r, 80:81].astype(jnp.int32)
            middle = 512 <= i * BQ < 1536
            parts = []
            for a in range(0, n, BQ):
                part = s[:, a : a + BQ]
                cols = iota((BQ, BQ), 1)
                keep = None if middle and a >= 512 else cols >= start - a
                if a + BQ == n:
                    causal = cols <= iota((BQ, BQ), 0)
                    keep = causal if keep is None else keep & causal
                parts.append(part if keep is None else jnp.where(keep, part, -1e30))
            s = jnp.concatenate(parts, axis=1)
            scores[i % 2][:, 0:n] = s
            m = s[:, 0:128]
            for t in range(128, n, 128):
                m = jnp.maximum(m, s[:, t : t + 128])
            top[i] = jnp.max(m, axis=-1, keepdims=True)

        def probs(i):
            r, n = pl.ds(i * BQ, BQ), (i + 1) * BQ
            e = jnp.exp(scores[i % 2][:, 0:n] - top[i]).astype(BF)
            expd[i % 2][:, 0:n] = e
            acc = dot(e, vs[h, 0:n])
            inverse = 1.0 / acc[:, 64:65]
            o = acc[:, :64] * inverse
            os[h, r] = o.astype(BF)
            g = gs[h, r].astype(F32) * inverse
            delta = -jnp.sum(g * o, axis=-1, keepdims=True)
            high = delta.astype(BF).astype(F32)
            wide[i] = with_lanes(g, high, delta - high)
            grad_t[i] = g.T.astype(BF)

        def back(i):
            r, n = pl.ds(i * BQ, BQ), (i + 1) * BQ
            dp = dot_nt(wide[i], vs[h, 0:n])
            e = expd[i % 2][:, 0:n]
            ds = e * dp.astype(BF)
            dqs[h, r] = dot(ds, ks[h, 0:n]) * 0.125
            dkt[h, :, 0:n] += dot(qt[h, :, r], ds)
            dvt[h, :, 0:n] += dot(grad_t[i], e)

        for step in range(NB + 2):
            if step >= 2:
                back(step - 2)
            if 1 <= step <= NB:
                probs(step - 1)
            if step < NB:
                score(step)

    @pl.loop(0, 4)
    def _(i):
        r = pl.ds(pl.multiple_of(i * 512, 512), 512)
        cosine, sine = angles(r)

        def unturn(g):
            return g * cosine + dot_nt((g * sine).astype(BF), turn)

        parts = []
        for h in range(3):
            parts.append(unturn(dqs[h, r]))
            parts.append(unturn(dkt[h, :, r].T))
            parts.append(dvt[h, :, r].T)
        out_ref[r] = jnp.concatenate(parts, axis=1).astype(BF)
        ctx = jnp.concatenate([os[h, r].astype(F32) for h in range(3)], axis=1)
        ctx_ref[r] = ctx.astype(BF)
        ctxt_ref[:, r] = ctx.T.astype(BF)


def attention(mixed, table, grads):
    vm = pl.BlockSpec(memory_space=pltpu.VMEM)
    return pl.pallas_call(
        attention_kernel,
        out_shape=(
            jax.ShapeDtypeStruct((2048, 192), BF),
            jax.ShapeDtypeStruct((192, 2048), BF),
            jax.ShapeDtypeStruct((2048, 576), BF),
        ),
        in_specs=[vm] * 3,
        out_specs=[vm] * 3,
        scratch_shapes=[
            pltpu.VMEM((3, 2048, 64), BF),
            pltpu.VMEM((3, 2048, 64), BF),
            pltpu.VMEM((3, 2048, 128), BF),
            pltpu.VMEM((3, 64, 2048), BF),
            pltpu.VMEM((BQ, 2048), BF),
            pltpu.VMEM((BQ, 2048), BF),
            pltpu.VMEM((BQ, 2048), F32),
            pltpu.VMEM((BQ, 2048), F32),
            pltpu.VMEM((3, 64, 2048), F32),
            pltpu.VMEM((3, 64, 2048), F32),
            pltpu.VMEM((3, 2048, 64), F32),
            pltpu.VMEM((3, 2048, 64), BF),
            pltpu.VMEM((3, 2048, 64), BF),
        ],
        compiler_params=pltpu.CompilerParams(vmem_limit_bytes=VMEM_LIMIT),
        cost_estimate=pl.CostEstimate(
            flops=30_000_000_000, bytes_accessed=10_000_000, transcendentals=8_000_000
        ),
        name="attention_both",
    )(mixed, table, grads)


def tail_kernel(
    ctx_h, ctxt_h, mg_h, act_h, actt_h, dg_h, unitt_h, w_h, vec_ref, ga_h, gb_h, gc_h, gd_h, rows_ref,
    out_ref, back_ref, wout_ref, wmix_ref, wup_ref, wdown_ref, small_ref,
    ctx, ctxt, mg, act, actt, hl, unitt, w, g, buf, passed, got, grads, first_in, second_in, part, third_in, fin_ref, col, mixcol,
    ld, sa, ra, sb, rb, s0, r0, s1, r1, s2, r2, s3, r3, s4, r4,
):
    x, z, y, c = places()
    is0 = c == 0
    me = lax.axis_index("shard")
    right, left = lax.rem(x + 1, 4), lax.rem(x + 3, 4)
    sibling = (x, me + 1 - 2 * c)

    def tok(k):
        return pl.ds(pl.multiple_of(lax.rem(x + 4 - k, 4) * 512, 512), 512)

    loads = []

    def load(src, dst):
        cp = pltpu.make_async_copy(src, dst, ld.at[len(loads)])
        cp.start()
        loads.append(cp)
        return cp

    l_ctx = load(ctx_h, ctx)
    l_w = load(w_h, w)
    l_act = load(act_h, act)
    l_g = [load(s, g.at[tok(k)]) for k, s in enumerate((ga_h, gb_h, gc_h, gd_h))]
    l_dg = load(dg_h, hl)
    l_mg = load(mg_h, mg)
    l_unitt = load(unitt_h, unitt)
    l_actt = load(actt_h, actt)
    l_ctxt = load(ctxt_h, ctxt)

    def first(k):
        return at(x, jnp.where(is0, lax.rem(z + k, 4), z), jnp.where(is0, y, lax.rem(y + k, 4)), c)

    def second(k):
        return at(x, jnp.where(is0, z, lax.rem(z + k, 4)), jnp.where(is0, lax.rem(y + k, 4), y), c)

    here1 = jnp.where(is0, z, y)
    here2 = jnp.where(is0, y, z)

    def rows(a, b, flip):
        blk = jnp.where(is0 != flip, a * 4 + b, b * 4 + a)
        return pl.ds(pl.multiple_of(blk * PAIR, 16), PAIR)

    barrier = pltpu.get_barrier_semaphore()
    peers = [first(k) for k in (1, 2, 3)] + [second(k) for k in (1, 2, 3)] + [sibling]
    peers += [(lax.rem(x + k, 4), me) for k in (1, 2, 3)]
    for peer in peers:
        pl.semaphore_signal(barrier, inc=1, device_id=peer, device_id_type=MESH)
    pl.semaphore_wait(barrier, len(peers))
    started = []

    def remote(src, dst, ss, rs, dev):
        cp = pltpu.make_async_remote_copy(
            src_ref=src, dst_ref=dst, send_sem=ss, recv_sem=rs, device_id=dev, device_id_type=MESH
        )
        return cp

    def send(*args):
        cp = remote(*args)
        cp.start()
        started.append(cp)

    def landed(dst, sem):
        remote(dst, dst, sem, sem, sibling).wait_recv()

    half = [pl.ds(0, 256), pl.ds(256, 256)]
    dev_x = [(right, me), (left, me)]

    def far_send(n):
        for d in range(2):
            send(buf.at[n, 2, half[d]], passed.at[n, d], sa.at[n, d], ra.at[n, d], dev_x[d])

    def near_send(n, d, h):
        send(buf.at[n, 3 - 2 * d, half[h]], got.at[n, d, half[h]], sb.at[n, d, h], rb.at[n, d, h], dev_x[d])

    def pass_on(n):
        for d in range(2):
            landed(passed.at[n, d], ra.at[n, d])
            k = 3 - 2 * d
            buf[n, k, half[d]] = (buf[n, k, half[d]].astype(F32) + passed[n, d].astype(F32)).astype(BF)
            near_send(n, d, d)

    def total(n, h):
        for d in range(2):
            landed(got.at[n, d, half[h]], rb.at[n, d, h])
        return buf[n, 0, half[h]].astype(F32) + got[n, 0, half[h]].astype(F32) + got[n, 1, half[h]].astype(F32)

    out_rows = pl.ds(pl.multiple_of(x * 192, 64), 192)

    def outputs_of(k):
        base = lax.rem(x + 4 - k, 4) * 512

        @pl.loop(0, 2)
        def _(i):
            r = pl.ds(pl.multiple_of(base + i * 256, 256), 256)
            o = dot(ctx[r], w[0, out_rows, 0:768]) + dot(act[r], w[1, :, 768:])
            buf[0, k, pl.ds(pl.multiple_of(i * 256, 256), 256)] = o.astype(BF)

    def pulls_of(k):
        base = lax.rem(x + 4 - k, 4) * 512

        @pl.loop(0, 2)
        def _(i):
            r = pl.ds(pl.multiple_of(base + i * 256, 256), 256)
            ag = dot_nt(g[r], w[1, :, 768:])
            low = (ag * hl[r].astype(F32)).astype(BF)
            hl[r] = low
            s = dot_nt(low, w[1, :, 0:768]) * vec_ref[2:3] + dot_nt(mg[r], w[0, :, 768:1344]) * vec_ref[0:1]
            buf[1, k, pl.ds(pl.multiple_of(i * 256, 256), 256)] = s.astype(BF)

    l_ctx.wait()
    l_w.wait()
    l_act.wait()
    for k in (2, 3, 1, 0):
        outputs_of(k)
        if k == 2:
            far_send(0)
        elif k == 3:
            near_send(0, 0, 1)
        elif k == 1:
            near_send(0, 1, 0)
    for cp in l_g:
        cp.wait()
    l_dg.wait()
    l_mg.wait()
    for k in (2, 3, 1, 0):
        pulls_of(k)
        if k == 2:
            far_send(1)
        elif k == 3:
            near_send(1, 0, 1)
        elif k == 1:
            near_send(1, 1, 0)
    pass_on(0)
    l_unitt.wait()
    l_actt.wait()
    l_ctxt.wait()
    ones = jnp.ones((16, 2048), BF)
    sum_mix = dot(ones, mg[...])[0:8]
    sum_up = dot(ones, hl[...])[0:8]
    sum_g = dot(ones, g[...])[0:8]
    gains = jnp.concatenate([vec_ref[...], sum_up, sum_g], axis=0)
    col[...] = jnp.concatenate([gains, jnp.zeros((104, 768), F32)], axis=0).T

    grads[0, :, 0:768] = jnp.zeros((768, 768), BF)
    grads[0, out_rows, 0:768] = dot(ctxt[...], g[...]).astype(BF)
    mixcol[...] = jnp.concatenate([sum_mix, jnp.zeros((120, 576), F32)], axis=0).T
    lane = iota((192, 192), 1)
    bias = jnp.zeros((192, 192), F32)
    for n in range(3):
        bias = jnp.where(lane == 6 + n, mixcol[pl.ds(n, 192, stride=3), 0:1], bias)

    def gradients_of(zone):
        r = pl.ds(pl.multiple_of(zone * 192, 64), 192)
        cols = col[r]

        def over_tokens(a, b):
            return sum(dot(a[n, r], b[n * 512 : n * 512 + 512]) for n in range(4))

        u1 = over_tokens(unitt, mg)
        wm = w[0, r, 768:1344].astype(F32)
        gain1 = jnp.sum(wm * u1, axis=-1, keepdims=True)
        shift1 = jnp.sum(wm * sum_mix[0:1], axis=-1, keepdims=True)
        dmix = u1 * cols[:, 0:1] + cols[:, 1:2] * sum_mix[0:1]
        u2 = over_tokens(unitt, hl)
        wu = w[1, r, 0:768].astype(F32)
        gain2 = jnp.sum(wu * u2, axis=-1, keepdims=True)
        shift2 = jnp.sum(wu * sum_up[0:1], axis=-1, keepdims=True)
        grads[1, r, 0:768] = (u2 * cols[:, 2:3] + cols[:, 3:4] * sum_up[0:1]).astype(BF)
        grads[1, r, 768:] = over_tokens(actt, g).astype(BF)
        small = jnp.where(zone == x, bias, 0.0)
        for n, v in enumerate((gain1, shift1, gain2, shift2, cols[:, 16:17], cols[:, 8:9])):
            small = jnp.where(lane == n, v, small)
        grads[0, r, 768:1536] = jnp.concatenate([dmix, small], axis=1).astype(BF)

    def block_rows(zone, b):
        return pl.ds(pl.multiple_of((zone * 4 + b) * PAIR, 16), PAIR)

    def add_sibling(zone):
        for b in range(4):
            r = block_rows(zone, b)
            landed(first_in.at[r], r0.at[zone, b])
            grads[c, r] = (grads[c, r].astype(F32) + first_in[r].astype(F32)).astype(BF)
            one, two = jnp.where(is0, zone, b), jnp.where(is0, b, zone)
            k = lax.rem(one + 4 - here1, 4)

            @pl.when(k != 0)
            def _():
                remote(
                    grads.at[c, r], second_in.at[k - 1, two], s1.at[k - 1, two], r1.at[k - 1, two], first(k)
                ).start()

    order = (1, 3, 2, 0)
    zones = [lax.rem(z + k, 4) for k in order]
    for n, zone in enumerate(zones):
        gradients_of(zone)
        for b in range(4):
            r = block_rows(zone, b)
            send(grads.at[1 - c, r], first_in.at[r], s0.at[zone, b], r0.at[zone, b], sibling)
        if n:
            add_sibling(zones[n - 1])
    add_sibling(zones[3])
    pass_on(1)
    lane = iota((1, WIDE), 1)
    group = lax.rem(lax.div(lane, 24), 4)
    source = lax.div(lane, 96) * 24 + lax.rem(lane, 24)
    for d in range(4):
        hot = iota((384, WIDE), 0) == jnp.where(group == d, source, -1)
        w[d // 2, (d % 2) * 384 : (d % 2) * 384 + 384] = hot.astype(F32).astype(BF)
    for j in order:
        b = lax.rem(here2 + j, 4)
        r = rows(here1, b, False)
        acc = grads[c, r].astype(F32)
        for k in (1, 3, 2):
            landed(second_in.at[k - 1, b], r1.at[k - 1, b])
            acc = acc + second_in[k - 1, b].astype(F32)
        part[j] = acc.astype(BF)
        if j:
            send(part.at[j], third_in.at[j - 1], s2.at[j - 1], r2.at[j - 1], second(j))
    for h in range(2):
        o = total(0, h) + rows_ref[half[h]].astype(F32) + vec_ref[4:5]
        out_ref[half[h]] = o.astype(BF)
    acc = part[0].astype(F32)
    for j in (1, 3, 2):
        landed(third_in.at[j - 1], r2.at[j - 1])
        acc = acc + third_in[j - 1].astype(F32)
    fin_ref[c, x] = acc.astype(BF)
    for k in (1, 3, 2):
        slot = fin_ref.at[c, x]
        send(slot, slot, s3.at[k - 1], r3.at[k - 1], (lax.rem(x + k, 4), me))
    slot = fin_ref.at[c, x]
    send(slot, slot, s4.at[0], r4.at[0], sibling)
    for h in range(2):
        s = total(1, h)
        v = rows_ref[half[h]].astype(F32)
        v = v - jnp.mean(v, axis=-1, keepdims=True)
        inverse = lax.rsqrt(jnp.mean(v * v, axis=-1, keepdims=True) + 1e-05)
        unit = v * inverse
        s = s - jnp.mean(s, axis=-1, keepdims=True) - unit * jnp.mean(s * unit, axis=-1, keepdims=True)
        own = pl.ds(pl.multiple_of(x * 512 + h * 256, 256), 256)
        back_ref[half[h]] = (g[own].astype(F32) + inverse * s).astype(BF)
    for k in (1, 3, 2):
        slot = fin_ref.at[c, lax.rem(x + 4 - k, 4)]
        landed(slot, r3.at[k - 1])
        send(slot, slot, s4.at[k], r4.at[k], sibling)
    for k in range(4):
        landed(fin_ref.at[1 - c, lax.rem(x + 4 - k, 4)], r4.at[k])

    def mine(role, d, a, b):
        v = fin_ref[role, d, :, a:b].astype(F32)
        return jnp.where(is0, v[0:24], v[24:48])

    wout_ref[...] = sum(mine(0, d, 0, 768) for d in range(4))
    tails = [mine(0, d, 768, WIDE) for d in range(4)]
    wmix_ref[...] = jnp.concatenate([t[:, 0:576] for t in tails], axis=1)
    lane = iota((24, 128), 1)
    small = sum(t[:, 576:704] for t in tails)
    for d in range(4):
        small = jnp.where(lane == 16 + d, tails[d][:, 581:582], small)
    small_ref[...] = jnp.where(lane == 4, tails[0][:, 576:704], small)
    ups = [mine(1, d, 0, 768).astype(BF) for d in range(4)]
    for n in range(2):
        wup_ref[:, n * WIDE : n * WIDE + WIDE] = sum(
            dot(ups[d][:, n * 384 : n * 384 + 384], w[d // 2, (d % 2) * 384 : (d % 2) * 384 + 384])
            for d in range(4)
        )
    for d in range(4):
        wdown_ref[d * 24 : d * 24 + 24] = mine(1, d, 768, WIDE)
    for cp in started:
        cp.wait_send()
    for k in range(3):
        for b in range(4):
            remote(second_in.at[k, b], second_in.at[k, b], s1.at[k, b], r1.at[k, b], sibling).wait_send()


def tail(ctx, ctxt, mg, act, actt, dg, unitt, w, vec, g, rows):
    vm = pl.BlockSpec(memory_space=pltpu.VMEM)
    hbm = pl.BlockSpec(memory_space=pl.ANY)
    dma = pltpu.SemaphoreType.DMA
    return pl.pallas_call(
        tail_kernel,
        out_shape=(
            jax.ShapeDtypeStruct((512, 768), BF),
            jax.ShapeDtypeStruct((512, 768), BF),
            jax.ShapeDtypeStruct((24, 768), F32),
            jax.ShapeDtypeStruct((24, 2304), F32),
            jax.ShapeDtypeStruct((24, 3072), F32),
            jax.ShapeDtypeStruct((96, 768), F32),
            jax.ShapeDtypeStruct((24, 128), F32),
        ),
        in_specs=[hbm] * 8 + [vm] + [hbm] * 4 + [vm],
        out_specs=[vm] * 7,
        scratch_shapes=[
            pltpu.VMEM((2048, 192), BF),
            pltpu.VMEM((192, 2048), BF),
            pltpu.VMEM((2048, 576), BF),
            pltpu.VMEM((2048, 768), BF),
            pltpu.VMEM((4, 768, 512), BF),
            pltpu.VMEM((2048, 768), BF),
            pltpu.VMEM((4, 768, 512), BF),
            pltpu.VMEM((2, 768, WIDE), BF),
            pltpu.VMEM((2048, 768), BF),
            pltpu.VMEM((2, 4, 512, 768), BF),
            pltpu.VMEM((2, 2, 256, 768), BF),
            pltpu.VMEM((2, 2, 512, 768), BF),
            pltpu.VMEM((2, 768, WIDE), BF),
            pltpu.VMEM((768, WIDE), BF),
            pltpu.VMEM((3, 4, PAIR, WIDE), BF),
            pltpu.VMEM((4, PAIR, WIDE), BF),
            pltpu.VMEM((3, PAIR, WIDE), BF),
            pltpu.VMEM((2, 4, PAIR, WIDE), BF),
            pltpu.VMEM((768, 128), F32),
            pltpu.VMEM((576, 128), F32),
            dma((12,)),
            dma((2, 2)), dma((2, 2)), dma((2, 2, 2)), dma((2, 2, 2)),
            dma((4, 4)), dma((4, 4)), dma((3, 4)), dma((3, 4)), dma((3,)), dma((3,)),
            dma((3,)), dma((3,)), dma((4,)), dma((4,)),
        ],
        compiler_params=pltpu.CompilerParams(
            collective_id=1, has_side_effects=True, vmem_limit_bytes=60 * 1024 * 1024
        ),
        name="tail_all",
    )(ctx, ctxt, mg, act, actt, dg, unitt, w, vec, *g, rows)


def shift_x(v, k):
    return lax.ppermute(v, "seq", [(i, (i + k) % NX) for i in range(NX)])


def local(
    inputs, positions, first_gain, first_shift, second_gain, second_shift, mix_weight, mix_bias,
    out_weight, out_bias, up_weight, up_bias, down_weight, down_bias, cotangent,
):
    flat = jnp.zeros((384,), BF)
    for place, v in (
        (0, first_gain), (24, first_shift), (48, second_gain), (72, second_shift), (96, out_bias),
        (120, down_bias), (192, mix_bias), (264, up_bias),
    ):
        flat = flat + jnp.pad(v, (place, 384 - place - v.shape[0]))
    packed = jnp.pad(flat.reshape(2, 192), ((0, 22), (0, 0)))
    grad = cotangent[0]
    mixed, act, actt, slope, unitt, context_grad, w, vec, table = front(
        inputs[0], grad, positions, packed, mix_weight, out_weight, up_weight, down_weight
    )
    late, table = lax.optimization_barrier((grad, table))
    grads = [grad] + [shift_x(late, k) for k in (1, 2, 3)]
    context, context_t, mix_grad = attention(mixed, table, context_grad)
    outputs, input_grad, g_out, g_mix, g_up, g_down, small = tail(
        context, context_t, mix_grad, act, actt, slope, unitt, w, vec, grads, inputs[0]
    )
    return (
        outputs[None],
        input_grad[None],
        small[:, 0],
        small[:, 1],
        small[:, 2],
        small[:, 3],
        g_mix,
        small[:, 6:9].reshape(72),
        g_out,
        small[:, 4],
        g_up,
        small[:, 16:20].T.reshape(96),
        g_down,
        small[:, 4],
    )


def solution(mesh):
    vec, mat, tok = P("shard"), P("shard", None), P("shard", "seq", None)
    return jax.shard_map(
        local,
        mesh=mesh,
        in_specs=(tok, P("shard", "seq"), vec, vec, vec, vec, mat, vec, mat, vec, mat, vec, mat, vec, tok),
        out_specs=(tok, tok, vec, vec, vec, vec, mat, vec, mat, vec, mat, vec, mat, vec),
        check_vma=False,
    )
```

```python
import jax
import jax.numpy as jnp
from jax import lax
from jax.experimental import pallas as pl
from jax.experimental.pallas import tpu as pltpu
from jax.sharding import PartitionSpec as P

HD = 64
ROT = 16
NX = 4
BF = jnp.bfloat16
F32 = jnp.float32
MESH = pl.DeviceIdType.MESH
NT = (((1,), (1,)), ((), ()))
VMEM_LIMIT = 56 * 1024 * 1024
WIDE = 1536
PAIR = 48


def dot(a, b):
    return jnp.dot(a, b, preferred_element_type=F32)


def dot_nt(a, b):
    return lax.dot_general(a, b, NT, preferred_element_type=F32)


def dot_tn(a, b):
    return lax.dot_general(a, b, (((0,), (0,)), ((), ())), preferred_element_type=F32)


def places():
    x = lax.axis_index("seq")
    s = lax.axis_index("shard")
    return x, s // 8, (s // 2) % 4, s % 2


def at(x, z, y, c):
    return (x, (z * 4 + y) * 2 + c)


ERFC = (0.254829592, -0.284496736, 1.421413741, -1.453152027, 1.061405429)


def gelu_and_slope(h):
    t = 1.0 / (1.0 + (0.3275911 * 2.0**-0.5) * jnp.abs(h))
    e = jnp.exp(h * h * -0.5)
    poly = t * (ERFC[0] + t * (ERFC[1] + t * (ERFC[2] + t * (ERFC[3] + t * ERFC[4]))))
    tail_part = 0.5 * poly * e
    cdf = jnp.where(h >= 0, 1.0 - tail_part, tail_part)
    return h * cdf, cdf + h * e * 0.3989422804014327


def iota(shape, dim):
    return lax.broadcasted_iota(jnp.int32, shape, dim)


def front_kernel(
    rows_ref, grad_ref, pos_ref, packed_ref, mix_ref, out_ref, up_ref, down_ref,
    mixed_o, act_o, actt_o, slope_o, unitt_o, cg_o, w_o, vec_o, table_o,
    rows_all, units, w, pos_all, grad, mixed, act, actt, slope, unitt, cg, cgs, vec, table, give, came, pair_ref,
    s1, r1, s2, r2, s3, r3, sx, rx, sf, rf, sp, rp, sc, rc, sg, rg, loc, wr,
):
    x, z, y, c = places()
    is0 = c == 0
    right, left, far = lax.rem(x + 1, 4), lax.rem(x + 3, 4), lax.rem(x + 2, 4)
    me = lax.axis_index("shard")
    mine, other = w.at[c], w.at[1 - c]

    def first(k):
        return at(x, jnp.where(is0, z, lax.rem(z + k, 4)), jnp.where(is0, lax.rem(y + k, 4), y), c)

    def second(k):
        return at(x, jnp.where(is0, lax.rem(z + k, 4), z), jnp.where(is0, y, lax.rem(y + k, 4)), c)

    def block(dz, dy):
        return lax.rem(z + dz, 4) * 4 + lax.rem(y + dy, 4)

    def held(a, b):
        da, db = (4 - a) % 4, (4 - b) % 4
        return jnp.where(is0, block(db, da), block(da, db))

    def rows_of(ref, b):
        return ref.at[pl.ds(pl.multiple_of(b * PAIR, 16), PAIR)]

    def quarter(who, q):
        return rows_all.at[pl.ds(pl.multiple_of(who * 512 + q * 128, 128), 128)]

    def remote(src, dst, ss, rs, dev):
        return pltpu.make_async_remote_copy(
            src_ref=src, dst_ref=dst, send_sem=ss, recv_sem=rs, device_id=dev, device_id_type=MESH
        )

    started = []

    def send(*args):
        cp = remote(*args)
        cp.start()
        started.append(cp)

    sibling = (x, me + 1 - 2 * c)

    def landed(dst, sem):
        remote(dst, dst, sem, sem, sibling).wait_recv()

    own_block = z * 4 + y
    own_pos = pos_all.at[x]
    local_copies = []
    for n, (src, dst) in enumerate(
        (
            (rows_ref, rows_all.at[pl.ds(pl.multiple_of(x * 512, 512), 512)]),
            (pos_ref, own_pos),
            (grad_ref, grad),
        )
    ):
        cp = pltpu.make_async_copy(src, dst, loc.at[n])
        cp.start()
        local_copies.append(cp)
    barrier = pltpu.get_barrier_semaphore()
    peers = [first(k) for k in (1, 2, 3)] + [second(k) for k in (1, 2, 3)]
    peers += [sibling, (right, me), (left, me), (far, me)]
    for peer in peers:
        pl.semaphore_signal(barrier, inc=1, device_id=peer, device_id_type=MESH)
    pl.semaphore_wait(barrier, len(peers))

    order = (1, 3, 2)
    own = [rows_ref.at[pl.ds(q * 128, 128)] for q in range(4)]
    for i in range(4):
        send(own[i], quarter(x, i), sx.at[0, i], rx.at[0, i], (right, me))
        send(own[3 - i], quarter(x, 3 - i), sx.at[1, 3 - i], rx.at[1, 3 - i], (left, me))
    for k in order:
        send(pos_ref, own_pos, sp.at[k - 1], rp.at[k - 1], (lax.rem(x + k, 4), me))

    def pick_x(parts):
        v = parts[0]
        for d in range(1, 4):
            v = jnp.where(x == d, parts[d], v)
        return v

    mix_part = pick_x([mix_ref[:, d * 576 : d * 576 + 576].astype(F32) for d in range(4)])
    half_a = jnp.concatenate([out_ref[...].astype(F32), mix_part, packed_ref[...].astype(F32)], axis=1)
    lane = iota((1, 384), 1)
    hot = iota((WIDE, 384), 0) == lax.div(lane, 24) * 96 + lax.rem(lane, 24) + 24 * x
    hot = hot.astype(F32).astype(BF)
    down_own = down_ref[...].astype(F32)
    half_b = jnp.concatenate(
        [dot(up_ref[:, 0:WIDE], hot), dot(up_ref[:, WIDE:], hot), pick_x([down_own[d * 24 : d * 24 + 24] for d in range(4)])],
        axis=1,
    )
    give[...] = jnp.concatenate([jnp.where(is0, half_b, half_a), jnp.zeros((8, WIDE), F32)], axis=0).astype(BF)
    send(give, came, sg.at[0], rg.at[0], sibling)
    for cp in local_copies:
        cp.wait()
    writes = []

    def write(src, dst):
        cp = pltpu.make_async_copy(src, dst, wr.at[len(writes)])
        cp.start()
        writes.append(cp)

    def norm(who):
        @pl.loop(0, 2)
        def _(i):
            r = pl.ds(pl.multiple_of(who * 512 + i * 256, 256), 256)
            v = rows_all[r].astype(F32)
            v = v - jnp.mean(v, axis=-1, keepdims=True)
            unit = v * lax.rsqrt(jnp.mean(v * v, axis=-1, keepdims=True) + 1e-05)
            units[r] = unit
            unitt[who, :, pl.ds(pl.multiple_of(i * 256, 256), 256)] = unit.astype(BF).T

        write(unitt.at[who], unitt_o.at[who])

    norm(x)
    landed(came, rg.at[0])
    theirs = came[...].astype(F32)[0:24]
    kept = jnp.where(is0, half_a, half_b)
    pair = jnp.concatenate([jnp.where(is0, kept, theirs), jnp.where(is0, theirs, kept)], axis=0).astype(BF)
    pair_ref[...] = pair
    w[c, pl.ds(pl.multiple_of(own_block * PAIR, 16), PAIR)] = pair
    for k in order:
        send(pair_ref, rows_of(mine, own_block), s1.at[k - 1], r1.at[k - 1], first(k))
    for k in (1, 3):
        send(pair_ref, rows_of(mine, own_block), s2.at[0, k - 1], r2.at[0, k - 1], second(k))
    send(pair_ref, rows_of(mine, own_block), s3.at[0, 0], r3.at[0, 0], sibling)

    for k in order:
        b = held(k, 0)
        landed(rows_of(mine, b), r1.at[k - 1])
        for j in (1, 3):
            send(rows_of(mine, b), rows_of(mine, b), s2.at[k, j - 1], r2.at[k, j - 1], second(j))
        send(rows_of(mine, b), rows_of(mine, b), s3.at[k, 0], r3.at[k, 0], sibling)

    for k in order:
        landed(pos_all.at[lax.rem(x + 4 - k, 4)], rp.at[k - 1])
    place = jnp.concatenate([pos_all[d] for d in range(4)], axis=1).astype(F32)
    freqs = jnp.ones((8, 2048), F32)
    for n in range(1, 8):
        freqs = jnp.where(iota((8, 2048), 0) == n, 10000.0 ** (-2.0 * n / ROT), freqs)
    angles = place * freqs
    cos8, sin8 = jnp.cos(angles), jnp.sin(angles)
    start = jnp.broadcast_to(iota((1, 2048), 1).astype(F32) - place, (8, 2048))
    table[...] = jnp.concatenate(
        [cos8, cos8, jnp.ones((48, 2048), F32), sin8, sin8, start, jnp.zeros((40, 2048), F32)], axis=0
    ).T

    for i in range(2):
        landed(quarter(left, i), rx.at[0, i])
        send(quarter(left, i), quarter(left, i), sf.at[0, i], rf.at[0, i], (right, me))
        landed(quarter(right, 3 - i), rx.at[1, 3 - i])
        send(quarter(right, 3 - i), quarter(right, 3 - i), sf.at[1, i], rf.at[1, i], (left, me))
    for j in order:
        for k in (0,) + order:
            b = held(k, j)
            landed(rows_of(mine, b), r2.at[k, j - 1])
            if (j == 1 and k < 2) or (j == 3 and k >= 2):
                send(rows_of(mine, b), rows_of(mine, b), s2.at[k, 1], r2.at[k, 1], second(j))
            send(rows_of(mine, b), rows_of(mine, b), s3.at[k, j], r3.at[k, j], sibling)
    for i in range(2):
        landed(quarter(left, 2 + i), rx.at[0, 2 + i])
        landed(quarter(right, i), rx.at[1, i])
    norm(left)
    norm(right)
    for a in range(4):
        for b in range(4):
            da, db = (4 - a) % 4, (4 - b) % 4
            blk = jnp.where(is0, block(da, db), block(db, da))
            landed(rows_of(other, blk), r3.at[a, b])

    own_tok = pl.ds(pl.multiple_of(x * 512, 512), 512)
    for k in (2, 1, 3, 0):
        dev = lax.rem(x + k, 4)
        heads = w[0, pl.ds(pl.multiple_of(dev * 192, 64), 192), 0:768]

        @pl.loop(0, 2)
        def _(i):
            r = pl.ds(pl.multiple_of(i * 256, 256), 256)
            cgs[k, r] = dot_nt(grad[r], heads).astype(BF)

        if k:
            send(cgs.at[k], cg.at[own_tok], sc.at[k - 1], rc.at[k - 1], (dev, me))
        else:
            cg[own_tok] = cgs[0]

    packed = w[0, :, 1344:1536]
    pick = [dot((iota((32, 768), 1) == 24 * iota((32, 768), 0) + n).astype(BF), packed).astype(BF) for n in range(2)]

    def spread(src, width, base, group, shift):
        lane = iota((192, width), 1)
        one_hot = iota((192, width), 0) == lax.rem(lane, group) + base
        lane = iota((32, width), 1)
        keep = iota((32, width), 0) == lax.div(lane, group) + shift
        return jnp.sum(jnp.where(keep, dot(src, one_hot.astype(BF)), 0.0), axis=0, keepdims=True)

    g1, b1, g2, b2, out_b, down_b = (spread(pick[0], 768, 24 * n, 24, 0) for n in range(6))
    mix_b = spread(pick[1], 576, 0, 72, 8 * x)
    up_b = spread(pick[1], 768, 72 + 24 * x, 24, 0)
    vec[...] = jnp.concatenate([g1, b1, g2, b2, out_b + down_b, up_b, g1, g1], axis=0)

    write(w, w_o)
    write(vec, vec_o)
    write(table, table_o)

    def compute(who):
        @pl.loop(0, 2)
        def _(i):
            r = pl.ds(pl.multiple_of(who * 512 + i * 256, 256), 256)
            cols = pl.ds(pl.multiple_of(i * 256, 256), 256)
            unit = units[r]
            one = (unit * vec[0:1] + vec[1:2]).astype(BF)
            mixed[r] = (dot(one, w[0, :, 768:1344]) + mix_b).astype(BF)
            two = (unit * vec[2:3] + vec[3:4]).astype(BF)
            hidden = dot(two, w[1, :, 0:768]) + vec[5:6]
            a, s = gelu_and_slope(hidden)
            a = a.astype(BF)
            act[r] = a
            actt[who, :, cols] = a.T
            slope[r] = s.astype(BF)

        t = pl.ds(pl.multiple_of(who * 512, 512), 512)
        write(mixed.at[t], mixed_o.at[t])
        write(act.at[t], act_o.at[t])
        write(slope.at[t], slope_o.at[t])
        write(actt.at[who], actt_o.at[who])

    compute(x)
    compute(left)
    compute(right)
    for i in range(2):
        landed(quarter(far, i), rf.at[0, i])
        landed(quarter(far, 3 - i), rf.at[1, i])
    norm(far)
    compute(far)
    for k in (1, 3, 2):
        t = pl.ds(pl.multiple_of(lax.rem(x + 4 - k, 4) * 512, 512), 512)
        landed(cg.at[t], rc.at[k - 1])
    write(cg, cg_o)
    for cp in writes:
        cp.wait()
    for cp in started:
        cp.wait_send()


def front(rows, grad, pos, packed, mix, out, up, down):
    hbm = pl.BlockSpec(memory_space=pl.ANY)
    vm = pl.BlockSpec(memory_space=pltpu.VMEM)
    dma = pltpu.SemaphoreType.DMA
    outs = [
        ((2048, 576), BF), ((2048, 768), BF), ((4, 768, 512), BF), ((2048, 768), BF), ((4, 768, 512), BF),
        ((2048, 192), BF), ((2, 768, WIDE), BF), ((8, 768), F32), ((2048, 128), F32),
    ]
    return pl.pallas_call(
        front_kernel,
        out_shape=tuple(jax.ShapeDtypeStruct(s, t) for s, t in outs),
        in_specs=[hbm] * 2 + [vm] * 6,
        out_specs=[hbm] * 9,
        scratch_shapes=[
            pltpu.VMEM((2048, 768), BF),
            pltpu.VMEM((2048, 768), F32),
            pltpu.VMEM((2, 768, WIDE), BF),
            pltpu.VMEM((4, 1, 512), jnp.int32),
            pltpu.VMEM((512, 768), BF),
            pltpu.VMEM((2048, 576), BF),
            pltpu.VMEM((2048, 768), BF),
            pltpu.VMEM((4, 768, 512), BF),
            pltpu.VMEM((2048, 768), BF),
            pltpu.VMEM((4, 768, 512), BF),
            pltpu.VMEM((2048, 192), BF),
            pltpu.VMEM((4, 512, 192), BF),
            pltpu.VMEM((8, 768), F32),
            pltpu.VMEM((2048, 128), F32),
            pltpu.VMEM((32, WIDE), BF),
            pltpu.VMEM((32, WIDE), BF),
            pltpu.VMEM((PAIR, WIDE), BF),
            dma((3,)), dma((3,)), dma((4, 3)), dma((4, 3)), dma((4, 4)), dma((4, 4)),
            dma((2, 4)), dma((2, 4)), dma((2, 2)), dma((2, 2)), dma((3,)), dma((3,)), dma((3,)), dma((3,)),
            dma((1,)), dma((1,)), dma((3,)), dma((24,)),
        ],
        compiler_params=pltpu.CompilerParams(
            collective_id=0, has_side_effects=True, vmem_limit_bytes=VMEM_LIMIT
        ),
        name="front_all",
    )(rows, grad, pos, packed, mix, out, up, down)


BQ = 256
NB = 2048 // BQ


def attention_kernel(
    mixed_ref, table_ref, grad_ref, ctx_ref, ctxt_ref, out_ref,
    qs, ks, vs, qt, ea, eb, sa, sb, dkt, dvt, dqs, os, gs,
):
    row, lane = iota((64, 64), 0), iota((64, 64), 1)
    turn = jnp.where((lane == row + 8) & (row < 8), 1.0, jnp.where((row == lane + 8) & (lane < 8), -1.0, 0.0))
    turn = turn.astype(BF)
    scores, expd = (sa, sb), (ea, eb)

    def angles(r):
        t = table_ref[r]
        return t[:, 0:64], jnp.where(iota((512, 64), 1) < ROT, t[:, 64:128], 0.0)

    def with_lanes(v, first, second):
        lane = iota((v.shape[0], 128), 1)
        wide = jnp.concatenate([v, jnp.zeros((v.shape[0], 64), F32)], axis=1)
        return jnp.where(lane == 64, first, jnp.where(lane == 65, second, wide)).astype(BF)

    @pl.loop(0, 4)
    def _(i):
        r = pl.ds(pl.multiple_of(i * 512, 512), 512)
        cosine, sine = angles(r)
        for h in range(3):
            q = mixed_ref[r, h * 192 : h * 192 + 64]
            k = mixed_ref[r, h * 192 + 64 : h * 192 + 128]
            v = mixed_ref[r, h * 192 + 128 : h * 192 + 192]
            q = q.astype(F32) * cosine + dot(q, turn) * sine
            k = k.astype(F32) * cosine + dot(k, turn) * sine
            q = q.astype(BF) * 0.125
            qs[h, r] = q
            qt[h, :, r] = q.astype(F32).T.astype(BF)
            ks[h, r] = k.astype(BF)
            vs[h, r] = with_lanes(v.astype(F32), 1.0, 1.0)
            gs[h, r] = grad_ref[r, h * 64 : h * 64 + 64]

    @pl.loop(0, 3)
    def _(h):
        dkt[h] = jnp.zeros((64, 2048), F32)
        dvt[h] = jnp.zeros((64, 2048), F32)
        top, wide, grad_t = {}, {}, {}

        def score(i):
            r, n = pl.ds(i * BQ, BQ), (i + 1) * BQ
            s = dot_nt(qs[h, r], ks[h, 0:n])
            start = table_ref[r, 80:81].astype(jnp.int32)
            middle = 512 <= i * BQ < 1536
            parts = []
            for a in range(0, n, BQ):
                part = s[:, a : a + BQ]
                cols = iota((BQ, BQ), 1)
                keep = None if middle and a >= 512 else cols >= start - a
                if a + BQ == n:
                    causal = cols <= iota((BQ, BQ), 0)
                    keep = causal if keep is None else keep & causal
                parts.append(part if keep is None else jnp.where(keep, part, -1e30))
            s = jnp.concatenate(parts, axis=1)
            scores[i % 2][:, 0:n] = s
            m = s[:, 0:128]
            for t in range(128, n, 128):
                m = jnp.maximum(m, s[:, t : t + 128])
            top[i] = jnp.max(m, axis=-1, keepdims=True)

        def probs(i):
            r, n = pl.ds(i * BQ, BQ), (i + 1) * BQ
            e = jnp.exp(scores[i % 2][:, 0:n] - top[i]).astype(BF)
            expd[i % 2][:, 0:n] = e
            acc = dot(e, vs[h, 0:n])
            inverse = 1.0 / acc[:, 64:65]
            o = acc[:, :64] * inverse
            os[h, r] = o.astype(BF)
            g = gs[h, r].astype(F32) * inverse
            delta = -jnp.sum(g * o, axis=-1, keepdims=True)
            high = delta.astype(BF).astype(F32)
            wide[i] = with_lanes(g, high, delta - high)
            grad_t[i] = g.T.astype(BF)

        def back(i):
            r, n = pl.ds(i * BQ, BQ), (i + 1) * BQ
            dp = dot_nt(wide[i], vs[h, 0:n])
            e = expd[i % 2][:, 0:n]
            ds = e * dp.astype(BF)
            dqs[h, r] = dot(ds, ks[h, 0:n]) * 0.125
            dkt[h, :, 0:n] += dot(qt[h, :, r], ds)
            dvt[h, :, 0:n] += dot(grad_t[i], e)

        for step in range(NB + 2):
            if step >= 2:
                back(step - 2)
            if 1 <= step <= NB:
                probs(step - 1)
            if step < NB:
                score(step)

    @pl.loop(0, 4)
    def _(i):
        r = pl.ds(pl.multiple_of(i * 512, 512), 512)
        cosine, sine = angles(r)

        def unturn(g):
            return g * cosine + dot_nt((g * sine).astype(BF), turn)

        parts = []
        for h in range(3):
            parts.append(unturn(dqs[h, r]))
            parts.append(unturn(dkt[h, :, r].T))
            parts.append(dvt[h, :, r].T)
        out_ref[r] = jnp.concatenate(parts, axis=1).astype(BF)
        ctx = jnp.concatenate([os[h, r].astype(F32) for h in range(3)], axis=1)
        ctx_ref[r] = ctx.astype(BF)
        ctxt_ref[:, r] = ctx.T.astype(BF)


def attention(mixed, table, grads):
    vm = pl.BlockSpec(memory_space=pltpu.VMEM)
    return pl.pallas_call(
        attention_kernel,
        out_shape=(
            jax.ShapeDtypeStruct((2048, 192), BF),
            jax.ShapeDtypeStruct((192, 2048), BF),
            jax.ShapeDtypeStruct((2048, 576), BF),
        ),
        in_specs=[vm] * 3,
        out_specs=[vm] * 3,
        scratch_shapes=[
            pltpu.VMEM((3, 2048, 64), BF),
            pltpu.VMEM((3, 2048, 64), BF),
            pltpu.VMEM((3, 2048, 128), BF),
            pltpu.VMEM((3, 64, 2048), BF),
            pltpu.VMEM((BQ, 2048), BF),
            pltpu.VMEM((BQ, 2048), BF),
            pltpu.VMEM((BQ, 2048), F32),
            pltpu.VMEM((BQ, 2048), F32),
            pltpu.VMEM((3, 64, 2048), F32),
            pltpu.VMEM((3, 64, 2048), F32),
            pltpu.VMEM((3, 2048, 64), F32),
            pltpu.VMEM((3, 2048, 64), BF),
            pltpu.VMEM((3, 2048, 64), BF),
        ],
        compiler_params=pltpu.CompilerParams(vmem_limit_bytes=VMEM_LIMIT),
        cost_estimate=pl.CostEstimate(
            flops=30_000_000_000, bytes_accessed=10_000_000, transcendentals=8_000_000
        ),
        name="attention_both",
    )(mixed, table, grads)


def tail_kernel(
    ctx_h, ctxt_h, mg_h, act_h, actt_h, dg_h, unitt_h, w_h, vec_ref, ga_h, gb_h, gc_h, gd_h, rows_ref,
    out_ref, back_ref, wout_ref, wmix_ref, wup_ref, wdown_ref, small_ref,
    ctx, ctxt, mg, act, actt, hl, unitt, w, g, buf, passed, got, grads, first_in, second_in, relay, part, third_in, fin_ref, col, mixcol,
    ld, sa, ra, sb, rb, s0, r0, s1, r1, s2, r2, s3, r3, s4, r4, s5, r5,
):
    x, z, y, c = places()
    is0 = c == 0
    me = lax.axis_index("shard")
    right, left = lax.rem(x + 1, 4), lax.rem(x + 3, 4)
    sibling = (x, me + 1 - 2 * c)

    def tok(k):
        return pl.ds(pl.multiple_of(lax.rem(x + 4 - k, 4) * 512, 512), 512)

    loads = []

    def load(src, dst):
        cp = pltpu.make_async_copy(src, dst, ld.at[len(loads)])
        cp.start()
        loads.append(cp)
        return cp

    l_ctx = load(ctx_h, ctx)
    l_w = load(w_h, w)
    l_act = load(act_h, act)
    l_g = [load(s, g.at[tok(k)]) for k, s in enumerate((ga_h, gb_h, gc_h, gd_h))]
    l_dg = load(dg_h, hl)
    l_mg = load(mg_h, mg)
    l_unitt = load(unitt_h, unitt)
    l_actt = load(actt_h, actt)
    l_ctxt = load(ctxt_h, ctxt)

    def first(k):
        return at(x, jnp.where(is0, lax.rem(z + k, 4), z), jnp.where(is0, y, lax.rem(y + k, 4)), c)

    def second(k):
        return at(x, jnp.where(is0, z, lax.rem(z + k, 4)), jnp.where(is0, lax.rem(y + k, 4), y), c)

    here1 = jnp.where(is0, z, y)
    here2 = jnp.where(is0, y, z)

    def rows(a, b, flip):
        blk = jnp.where(is0 != flip, a * 4 + b, b * 4 + a)
        return pl.ds(pl.multiple_of(blk * PAIR, 16), PAIR)

    barrier = pltpu.get_barrier_semaphore()
    peers = [first(k) for k in (1, 2, 3)] + [second(k) for k in (1, 2, 3)] + [sibling]
    peers += [(lax.rem(x + k, 4), me) for k in (1, 2, 3)]
    for peer in peers:
        pl.semaphore_signal(barrier, inc=1, device_id=peer, device_id_type=MESH)
    pl.semaphore_wait(barrier, len(peers))
    started = []

    def remote(src, dst, ss, rs, dev):
        cp = pltpu.make_async_remote_copy(
            src_ref=src, dst_ref=dst, send_sem=ss, recv_sem=rs, device_id=dev, device_id_type=MESH
        )
        return cp

    def send(*args):
        cp = remote(*args)
        cp.start()
        started.append(cp)

    def landed(dst, sem):
        remote(dst, dst, sem, sem, sibling).wait_recv()

    half = [pl.ds(0, 256), pl.ds(256, 256)]
    dev_x = [(right, me), (left, me)]

    def far_send(n):
        for d in range(2):
            send(buf.at[n, 2, half[d]], passed.at[n, d], sa.at[n, d], ra.at[n, d], dev_x[d])

    def near_send(n, d, h):
        send(buf.at[n, 3 - 2 * d, half[h]], got.at[n, d, half[h]], sb.at[n, d, h], rb.at[n, d, h], dev_x[d])

    def pass_on(n):
        for d in range(2):
            landed(passed.at[n, d], ra.at[n, d])
            k = 3 - 2 * d
            buf[n, k, half[d]] = (buf[n, k, half[d]].astype(F32) + passed[n, d].astype(F32)).astype(BF)
            near_send(n, d, d)

    def total(n, h):
        for d in range(2):
            landed(got.at[n, d, half[h]], rb.at[n, d, h])
        return buf[n, 0, half[h]].astype(F32) + got[n, 0, half[h]].astype(F32) + got[n, 1, half[h]].astype(F32)

    out_rows = pl.ds(pl.multiple_of(x * 192, 64), 192)

    def outputs_of(k):
        base = lax.rem(x + 4 - k, 4) * 512

        @pl.loop(0, 2)
        def _(i):
            r = pl.ds(pl.multiple_of(base + i * 256, 256), 256)
            o = dot(ctx[r], w[0, out_rows, 0:768]) + dot(act[r], w[1, :, 768:])
            buf[0, k, pl.ds(pl.multiple_of(i * 256, 256), 256)] = o.astype(BF)

    def pulls_of(k):
        base = lax.rem(x + 4 - k, 4) * 512

        @pl.loop(0, 2)
        def _(i):
            r = pl.ds(pl.multiple_of(base + i * 256, 256), 256)
            ag = dot_nt(g[r], w[1, :, 768:])
            low = (ag * hl[r].astype(F32)).astype(BF)
            hl[r] = low
            s = dot_nt(low, w[1, :, 0:768]) * vec_ref[2:3] + dot_nt(mg[r], w[0, :, 768:1344]) * vec_ref[0:1]
            buf[1, k, pl.ds(pl.multiple_of(i * 256, 256), 256)] = s.astype(BF)

    l_ctx.wait()
    l_w.wait()
    l_act.wait()
    for k in (2, 3, 1, 0):
        outputs_of(k)
        if k == 2:
            far_send(0)
        elif k == 3:
            near_send(0, 0, 1)
        elif k == 1:
            near_send(0, 1, 0)
    for cp in l_g:
        cp.wait()
    l_dg.wait()
    l_mg.wait()
    for k in (2, 3, 1, 0):
        pulls_of(k)
        if k == 2:
            far_send(1)
        elif k == 3:
            near_send(1, 0, 1)
        elif k == 1:
            near_send(1, 1, 0)
    pass_on(0)
    l_unitt.wait()
    l_actt.wait()
    l_ctxt.wait()
    ones = jnp.ones((16, 2048), BF)
    sum_mix = dot(ones, mg[...])[0:8]
    sum_up = dot(ones, hl[...])[0:8]
    sum_g = dot(ones, g[...])[0:8]
    gains = jnp.concatenate([vec_ref[...], sum_up, sum_g], axis=0)
    col[...] = jnp.concatenate([gains, jnp.zeros((104, 768), F32)], axis=0).T

    grads[0, :, 0:768] = jnp.zeros((768, 768), BF)
    grads[0, out_rows, 0:768] = dot(ctxt[...], g[...]).astype(BF)
    mixcol[...] = jnp.concatenate([sum_mix, jnp.zeros((120, 576), F32)], axis=0).T
    lane = iota((192, 192), 1)
    bias = jnp.zeros((192, 192), F32)
    for n in range(3):
        bias = jnp.where(lane == 6 + n, mixcol[pl.ds(n, 192, stride=3), 0:1], bias)

    def gradients_of(zone):
        r = pl.ds(pl.multiple_of(zone * 192, 64), 192)
        cols = col[r]

        def over_tokens(a, b):
            return sum(dot(a[n, r], b[n * 512 : n * 512 + 512]) for n in range(4))

        u1 = over_tokens(unitt, mg)
        wm = w[0, r, 768:1344].astype(F32)
        gain1 = jnp.sum(wm * u1, axis=-1, keepdims=True)
        shift1 = jnp.sum(wm * sum_mix[0:1], axis=-1, keepdims=True)
        dmix = u1 * cols[:, 0:1] + cols[:, 1:2] * sum_mix[0:1]
        u2 = over_tokens(unitt, hl)
        wu = w[1, r, 0:768].astype(F32)
        gain2 = jnp.sum(wu * u2, axis=-1, keepdims=True)
        shift2 = jnp.sum(wu * sum_up[0:1], axis=-1, keepdims=True)
        grads[1, r, 0:768] = (u2 * cols[:, 2:3] + cols[:, 3:4] * sum_up[0:1]).astype(BF)
        grads[1, r, 768:] = over_tokens(actt, g).astype(BF)
        small = jnp.where(zone == x, bias, 0.0)
        for n, v in enumerate((gain1, shift1, gain2, shift2, cols[:, 16:17], cols[:, 8:9])):
            small = jnp.where(lane == n, v, small)
        grads[0, r, 768:1536] = jnp.concatenate([dmix, small], axis=1).astype(BF)

    def block_rows(zone, b):
        return pl.ds(pl.multiple_of((zone * 4 + b) * PAIR, 16), PAIR)

    def add_sibling(zone):
        for b in range(4):
            r = block_rows(zone, b)
            landed(first_in.at[r], r0.at[zone, b])
            grads[c, r] = (grads[c, r].astype(F32) + first_in[r].astype(F32)).astype(BF)
            one, two = jnp.where(is0, zone, b), jnp.where(is0, b, zone)
            k, q = lax.rem(one + 4 - here1, 4), lax.rem(two, 2)
            block = grads.at[c, r]
            for d in range(2):
                here_first = two < 2 if d == 0 else two >= 2

                @pl.when((k == 1 + 2 * d) & jnp.logical_not(here_first))
                def _():
                    remote(block, second_in.at[d, two], s1.at[d, two], r1.at[d, two], first(1 + 2 * d)).start()

                @pl.when((k == 2) & here_first)
                def _():
                    remote(block, relay.at[d, q], s5.at[d, q], r5.at[d, q], first(1 + 2 * d)).start()

    order = (2, 1, 3, 0)
    zones = [lax.rem(z + k, 4) for k in order]
    for n, zone in enumerate(zones):
        gradients_of(zone)
        for b in range(4):
            r = block_rows(zone, b)
            send(grads.at[1 - c, r], first_in.at[r], s0.at[zone, b], r0.at[zone, b], sibling)
        if n:
            add_sibling(zones[n - 1])
    add_sibling(zones[3])
    for d in range(2):
        for q in range(2):
            two = q + 2 * d
            r = rows(lax.rem(here1 + 1 + 2 * d, 4), two, False)
            landed(relay.at[d, q], r5.at[d, q])
            grads[c, r] = (grads[c, r].astype(F32) + relay[d, q].astype(F32)).astype(BF)
            send(grads.at[c, r], second_in.at[d, two], s1.at[d, two], r1.at[d, two], first(1 + 2 * d))
    pass_on(1)
    lane = iota((1, WIDE), 1)
    group = lax.rem(lax.div(lane, 24), 4)
    source = lax.div(lane, 96) * 24 + lax.rem(lane, 24)
    for d in range(4):
        hot = iota((384, WIDE), 0) == jnp.where(group == d, source, -1)
        w[d // 2, (d % 2) * 384 : (d % 2) * 384 + 384] = hot.astype(F32).astype(BF)
    for j in order:
        b = lax.rem(here2 + j, 4)
        r = rows(here1, b, False)
        acc = grads[c, r].astype(F32)
        for d in range(2):
            landed(second_in.at[d, b], r1.at[d, b])
            acc = acc + second_in[d, b].astype(F32)
        part[j] = acc.astype(BF)
        if j:
            send(part.at[j], third_in.at[j - 1], s2.at[j - 1], r2.at[j - 1], second(j))
    for h in range(2):
        o = total(0, h) + rows_ref[half[h]].astype(F32) + vec_ref[4:5]
        out_ref[half[h]] = o
    acc = part[0].astype(F32)
    for j in (1, 3, 2):
        landed(third_in.at[j - 1], r2.at[j - 1])
        acc = acc + third_in[j - 1].astype(F32)
    fin_ref[c, x] = acc.astype(BF)
    for k in (1, 3, 2):
        slot = fin_ref.at[c, x]
        send(slot, slot, s3.at[k - 1], r3.at[k - 1], (lax.rem(x + k, 4), me))
    slot = fin_ref.at[c, x]
    send(slot, slot, s4.at[0], r4.at[0], sibling)
    for h in range(2):
        s = total(1, h)
        v = rows_ref[half[h]].astype(F32)
        v = v - jnp.mean(v, axis=-1, keepdims=True)
        inverse = lax.rsqrt(jnp.mean(v * v, axis=-1, keepdims=True) + 1e-05)
        unit = v * inverse
        s = s - jnp.mean(s, axis=-1, keepdims=True) - unit * jnp.mean(s * unit, axis=-1, keepdims=True)
        own = pl.ds(pl.multiple_of(x * 512 + h * 256, 256), 256)
        back_ref[half[h]] = g[own].astype(F32) + inverse * s
    for k in (1, 3, 2):
        slot = fin_ref.at[c, lax.rem(x + 4 - k, 4)]
        landed(slot, r3.at[k - 1])
        send(slot, slot, s4.at[k], r4.at[k], sibling)
    for k in range(4):
        landed(fin_ref.at[1 - c, lax.rem(x + 4 - k, 4)], r4.at[k])

    def mine(role, d, a, b):
        v = fin_ref[role, d, :, a:b].astype(F32)
        return jnp.where(is0, v[0:24], v[24:48])

    wout_ref[...] = sum(mine(0, d, 0, 768) for d in range(4))
    tails = [mine(0, d, 768, WIDE) for d in range(4)]
    wmix_ref[...] = jnp.concatenate([t[:, 0:576] for t in tails], axis=1)
    lane = iota((24, 128), 1)
    small = sum(t[:, 576:704] for t in tails)
    for d in range(4):
        small = jnp.where(lane == 16 + d, tails[d][:, 581:582], small)
    small_ref[...] = jnp.where(lane == 4, tails[0][:, 576:704], small)
    ups = [mine(1, d, 0, 768).astype(BF) for d in range(4)]
    for n in range(2):
        wup_ref[:, n * WIDE : n * WIDE + WIDE] = sum(
            dot(ups[d][:, n * 384 : n * 384 + 384], w[d // 2, (d % 2) * 384 : (d % 2) * 384 + 384])
            for d in range(4)
        )
    for d in range(4):
        wdown_ref[d * 24 : d * 24 + 24] = mine(1, d, 768, WIDE)
    for cp in started:
        cp.wait_send()
    for d in range(2):
        for q in range(2):
            two = 2 - 2 * d + q
            remote(second_in.at[d, two], second_in.at[d, two], s1.at[d, two], r1.at[d, two], sibling).wait_send()
            remote(relay.at[d, q], relay.at[d, q], s5.at[d, q], r5.at[d, q], sibling).wait_send()


def tail(ctx, ctxt, mg, act, actt, dg, unitt, w, vec, g, rows):
    vm = pl.BlockSpec(memory_space=pltpu.VMEM)
    hbm = pl.BlockSpec(memory_space=pl.ANY)
    dma = pltpu.SemaphoreType.DMA
    return pl.pallas_call(
        tail_kernel,
        out_shape=(
            jax.ShapeDtypeStruct((512, 768), F32),
            jax.ShapeDtypeStruct((512, 768), F32),
            jax.ShapeDtypeStruct((24, 768), F32),
            jax.ShapeDtypeStruct((24, 2304), F32),
            jax.ShapeDtypeStruct((24, 3072), F32),
            jax.ShapeDtypeStruct((96, 768), F32),
            jax.ShapeDtypeStruct((24, 128), F32),
        ),
        in_specs=[hbm] * 8 + [vm] + [hbm] * 4 + [vm],
        out_specs=[vm] * 7,
        scratch_shapes=[
            pltpu.VMEM((2048, 192), BF),
            pltpu.VMEM((192, 2048), BF),
            pltpu.VMEM((2048, 576), BF),
            pltpu.VMEM((2048, 768), BF),
            pltpu.VMEM((4, 768, 512), BF),
            pltpu.VMEM((2048, 768), BF),
            pltpu.VMEM((4, 768, 512), BF),
            pltpu.VMEM((2, 768, WIDE), BF),
            pltpu.VMEM((2048, 768), BF),
            pltpu.VMEM((2, 4, 512, 768), BF),
            pltpu.VMEM((2, 2, 256, 768), BF),
            pltpu.VMEM((2, 2, 512, 768), BF),
            pltpu.VMEM((2, 768, WIDE), BF),
            pltpu.VMEM((768, WIDE), BF),
            pltpu.VMEM((2, 4, PAIR, WIDE), BF),
            pltpu.VMEM((2, 2, PAIR, WIDE), BF),
            pltpu.VMEM((4, PAIR, WIDE), BF),
            pltpu.VMEM((3, PAIR, WIDE), BF),
            pltpu.VMEM((2, 4, PAIR, WIDE), BF),
            pltpu.VMEM((768, 128), F32),
            pltpu.VMEM((576, 128), F32),
            dma((12,)),
            dma((2, 2)), dma((2, 2)), dma((2, 2, 2)), dma((2, 2, 2)),
            dma((4, 4)), dma((4, 4)), dma((2, 4)), dma((2, 4)), dma((3,)), dma((3,)),
            dma((3,)), dma((3,)), dma((4,)), dma((4,)), dma((2, 2)), dma((2, 2)),
        ],
        compiler_params=pltpu.CompilerParams(
            collective_id=1, has_side_effects=True, vmem_limit_bytes=60 * 1024 * 1024
        ),
        name="tail_all",
    )(ctx, ctxt, mg, act, actt, dg, unitt, w, vec, *g, rows)


def shift_x(v, k):
    return lax.ppermute(v, "seq", [(i, (i + k) % NX) for i in range(NX)])


def local(
    inputs, positions, first_gain, first_shift, second_gain, second_shift, mix_weight, mix_bias,
    out_weight, out_bias, up_weight, up_bias, down_weight, down_bias, cotangent,
):
    flat = jnp.zeros((384,), BF)
    for place, v in (
        (0, first_gain), (24, first_shift), (48, second_gain), (72, second_shift), (96, out_bias),
        (120, down_bias), (192, mix_bias), (264, up_bias),
    ):
        flat = flat + jnp.pad(v, (place, 384 - place - v.shape[0]))
    packed = jnp.pad(flat.reshape(2, 192), ((0, 22), (0, 0)))
    grad = cotangent[0]
    mixed, act, actt, slope, unitt, context_grad, w, vec, table = front(
        inputs[0], grad, positions, packed, mix_weight, out_weight, up_weight, down_weight
    )
    late, table = lax.optimization_barrier((grad, table))
    grads = [grad] + [shift_x(late, k) for k in (1, 2, 3)]
    context, context_t, mix_grad = attention(mixed, table, context_grad)
    outputs, input_grad, g_out, g_mix, g_up, g_down, small = tail(
        context, context_t, mix_grad, act, actt, slope, unitt, w, vec, grads, inputs[0]
    )
    return (
        outputs.astype(BF)[None],
        input_grad.astype(BF)[None],
        small[:, 0],
        small[:, 1],
        small[:, 2],
        small[:, 3],
        g_mix,
        small[:, 6:9].reshape(72),
        g_out,
        small[:, 4],
        g_up,
        small[:, 16:20].T.reshape(96),
        g_down,
        small[:, 4],
    )


def solution(mesh):
    vec, mat, tok = P("shard"), P("shard", None), P("shard", "seq", None)
    return jax.shard_map(
        local,
        mesh=mesh,
        in_specs=(tok, P("shard", "seq"), vec, vec, vec, vec, mat, vec, mat, vec, mat, vec, mat, vec, tok),
        out_specs=(tok, tok, vec, vec, vec, vec, mat, vec, mat, vec, mat, vec, mat, vec),
        check_vma=False,
    )
```

```python
import jax
import jax.numpy as jnp
from jax import lax
from jax.experimental import pallas as pl
from jax.experimental.pallas import tpu as pltpu
from jax.sharding import PartitionSpec as P

HD = 64
ROT = 16
NX = 4
BF = jnp.bfloat16
F32 = jnp.float32
MESH = pl.DeviceIdType.MESH
NT = (((1,), (1,)), ((), ()))
VMEM_LIMIT = 56 * 1024 * 1024
WIDE = 1536
PAIR = 48


def dot(a, b):
    return jnp.dot(a, b, preferred_element_type=F32)


def dot_nt(a, b):
    return lax.dot_general(a, b, NT, preferred_element_type=F32)


def dot_tn(a, b):
    return lax.dot_general(a, b, (((0,), (0,)), ((), ())), preferred_element_type=F32)


def places():
    x = lax.axis_index("seq")
    s = lax.axis_index("shard")
    return x, s // 8, (s // 2) % 4, s % 2


def at(x, z, y, c):
    return (x, (z * 4 + y) * 2 + c)


ERFC = (0.254829592, -0.284496736, 1.421413741, -1.453152027, 1.061405429)


def gelu_and_slope(h):
    t = 1.0 / (1.0 + (0.3275911 * 2.0**-0.5) * jnp.abs(h))
    e = jnp.exp(h * h * -0.5)
    poly = t * (ERFC[0] + t * (ERFC[1] + t * (ERFC[2] + t * (ERFC[3] + t * ERFC[4]))))
    tail_part = 0.5 * poly * e
    cdf = jnp.where(h >= 0, 1.0 - tail_part, tail_part)
    return h * cdf, cdf + h * e * 0.3989422804014327


def iota(shape, dim):
    return lax.broadcasted_iota(jnp.int32, shape, dim)


def front_kernel(
    rows_ref, grad_ref, pos_ref, packed_ref, mix_ref, out_ref, up_ref, down_ref,
    mixed_o, act_o, actt_o, slope_o, unitt_o, cg_o, w_o, vec_o, table_o,
    rows_all, units, w, pos_all, grad, mixed, act, actt, slope, unitt, cg, cgs, vec, table, give, came, pair_ref,
    s1, r1, s2, r2, s3, r3, sx, rx, sf, rf, sp, rp, sc, rc, sg, rg, loc, wr,
):
    x, z, y, c = places()
    is0 = c == 0
    right, left, far = lax.rem(x + 1, 4), lax.rem(x + 3, 4), lax.rem(x + 2, 4)
    me = lax.axis_index("shard")
    mine, other = w.at[c], w.at[1 - c]

    def first(k):
        return at(x, jnp.where(is0, z, lax.rem(z + k, 4)), jnp.where(is0, lax.rem(y + k, 4), y), c)

    def second(k):
        return at(x, jnp.where(is0, lax.rem(z + k, 4), z), jnp.where(is0, y, lax.rem(y + k, 4)), c)

    def block(dz, dy):
        return lax.rem(z + dz, 4) * 4 + lax.rem(y + dy, 4)

    def held(a, b):
        da, db = (4 - a) % 4, (4 - b) % 4
        return jnp.where(is0, block(db, da), block(da, db))

    def rows_of(ref, b):
        return ref.at[pl.ds(pl.multiple_of(b * PAIR, 16), PAIR)]

    def quarter(who, q):
        return rows_all.at[pl.ds(pl.multiple_of(who * 512 + q * 128, 128), 128)]

    def remote(src, dst, ss, rs, dev):
        return pltpu.make_async_remote_copy(
            src_ref=src, dst_ref=dst, send_sem=ss, recv_sem=rs, device_id=dev, device_id_type=MESH
        )

    started = []

    def send(*args):
        cp = remote(*args)
        cp.start()
        started.append(cp)

    sibling = (x, me + 1 - 2 * c)

    def landed(dst, sem):
        remote(dst, dst, sem, sem, sibling).wait_recv()

    own_block = z * 4 + y
    own_pos = pos_all.at[x]
    local_copies = []
    for n, (src, dst) in enumerate(
        (
            (rows_ref, rows_all.at[pl.ds(pl.multiple_of(x * 512, 512), 512)]),
            (pos_ref, own_pos),
            (grad_ref, grad),
        )
    ):
        cp = pltpu.make_async_copy(src, dst, loc.at[n])
        cp.start()
        local_copies.append(cp)
    barrier = pltpu.get_barrier_semaphore()
    peers = [first(k) for k in (1, 2, 3)] + [second(k) for k in (1, 2, 3)]
    peers += [sibling, (right, me), (left, me), (far, me)]
    for peer in peers:
        pl.semaphore_signal(barrier, inc=1, device_id=peer, device_id_type=MESH)
    pl.semaphore_wait(barrier, len(peers))

    order = (1, 3, 2)
    own = [rows_ref.at[pl.ds(q * 128, 128)] for q in range(4)]
    for i in range(4):
        send(own[i], quarter(x, i), sx.at[0, i], rx.at[0, i], (right, me))
        send(own[3 - i], quarter(x, 3 - i), sx.at[1, 3 - i], rx.at[1, 3 - i], (left, me))
    for k in order:
        send(pos_ref, own_pos, sp.at[k - 1], rp.at[k - 1], (lax.rem(x + k, 4), me))

    def pick_x(parts):
        v = parts[0]
        for d in range(1, 4):
            v = jnp.where(x == d, parts[d], v)
        return v

    mix_part = pick_x([mix_ref[:, d * 576 : d * 576 + 576].astype(F32) for d in range(4)])
    half_a = jnp.concatenate([out_ref[...].astype(F32), mix_part, packed_ref[...].astype(F32)], axis=1)
    lane = iota((1, 384), 1)
    hot = iota((WIDE, 384), 0) == lax.div(lane, 24) * 96 + lax.rem(lane, 24) + 24 * x
    hot = hot.astype(F32).astype(BF)
    down_own = down_ref[...].astype(F32)
    half_b = jnp.concatenate(
        [dot(up_ref[:, 0:WIDE], hot), dot(up_ref[:, WIDE:], hot), pick_x([down_own[d * 24 : d * 24 + 24] for d in range(4)])],
        axis=1,
    )
    give[...] = jnp.concatenate([jnp.where(is0, half_b, half_a), jnp.zeros((8, WIDE), F32)], axis=0).astype(BF)
    send(give, came, sg.at[0], rg.at[0], sibling)
    for cp in local_copies:
        cp.wait()
    writes = []

    def write(src, dst):
        cp = pltpu.make_async_copy(src, dst, wr.at[len(writes)])
        cp.start()
        writes.append(cp)

    def norm(who):
        @pl.loop(0, 2)
        def _(i):
            r = pl.ds(pl.multiple_of(who * 512 + i * 256, 256), 256)
            v = rows_all[r].astype(F32)
            v = v - jnp.mean(v, axis=-1, keepdims=True)
            unit = v * lax.rsqrt(jnp.mean(v * v, axis=-1, keepdims=True) + 1e-05)
            units[r] = unit
            unitt[who, :, pl.ds(pl.multiple_of(i * 256, 256), 256)] = unit.astype(BF).T

        write(unitt.at[who], unitt_o.at[who])

    norm(x)
    landed(came, rg.at[0])
    theirs = came[...].astype(F32)[0:24]
    kept = jnp.where(is0, half_a, half_b)
    pair = jnp.concatenate([jnp.where(is0, kept, theirs), jnp.where(is0, theirs, kept)], axis=0).astype(BF)
    pair_ref[...] = pair
    w[c, pl.ds(pl.multiple_of(own_block * PAIR, 16), PAIR)] = pair
    for k in order:
        send(pair_ref, rows_of(mine, own_block), s1.at[k - 1], r1.at[k - 1], first(k))
    for k in order:
        send(pair_ref, rows_of(mine, own_block), s2.at[0, k - 1], r2.at[0, k - 1], second(k))
    send(pair_ref, rows_of(mine, own_block), s3.at[0, 0], r3.at[0, 0], sibling)

    for k in order:
        b = held(k, 0)
        landed(rows_of(mine, b), r1.at[k - 1])
        for j in order:
            send(rows_of(mine, b), rows_of(mine, b), s2.at[k, j - 1], r2.at[k, j - 1], second(j))
        send(rows_of(mine, b), rows_of(mine, b), s3.at[k, 0], r3.at[k, 0], sibling)

    for k in order:
        landed(pos_all.at[lax.rem(x + 4 - k, 4)], rp.at[k - 1])
    place = jnp.concatenate([pos_all[d] for d in range(4)], axis=1).astype(F32)
    freqs = jnp.ones((8, 2048), F32)
    for n in range(1, 8):
        freqs = jnp.where(iota((8, 2048), 0) == n, 10000.0 ** (-2.0 * n / ROT), freqs)
    angles = place * freqs
    cos8, sin8 = jnp.cos(angles), jnp.sin(angles)
    start = jnp.broadcast_to(iota((1, 2048), 1).astype(F32) - place, (8, 2048))
    table[...] = jnp.concatenate(
        [cos8, cos8, jnp.ones((48, 2048), F32), sin8, sin8, start, jnp.zeros((40, 2048), F32)], axis=0
    ).T

    for i in range(2):
        landed(quarter(left, i), rx.at[0, i])
        send(quarter(left, i), quarter(left, i), sf.at[0, i], rf.at[0, i], (right, me))
        landed(quarter(right, 3 - i), rx.at[1, 3 - i])
        send(quarter(right, 3 - i), quarter(right, 3 - i), sf.at[1, i], rf.at[1, i], (left, me))
    for j in order:
        for k in (0,) + order:
            b = held(k, j)
            landed(rows_of(mine, b), r2.at[k, j - 1])
            send(rows_of(mine, b), rows_of(mine, b), s3.at[k, j], r3.at[k, j], sibling)
    for i in range(2):
        landed(quarter(left, 2 + i), rx.at[0, 2 + i])
        landed(quarter(right, i), rx.at[1, i])
    norm(left)
    norm(right)
    for a in range(4):
        for b in range(4):
            da, db = (4 - a) % 4, (4 - b) % 4
            blk = jnp.where(is0, block(da, db), block(db, da))
            landed(rows_of(other, blk), r3.at[a, b])

    own_tok = pl.ds(pl.multiple_of(x * 512, 512), 512)
    for k in (2, 1, 3, 0):
        dev = lax.rem(x + k, 4)
        heads = w[0, pl.ds(pl.multiple_of(dev * 192, 64), 192), 0:768]

        @pl.loop(0, 2)
        def _(i):
            r = pl.ds(pl.multiple_of(i * 256, 256), 256)
            cgs[k, r] = dot_nt(grad[r], heads).astype(BF)

        if k:
            send(cgs.at[k], cg.at[own_tok], sc.at[k - 1], rc.at[k - 1], (dev, me))
        else:
            cg[own_tok] = cgs[0]

    packed = w[0, :, 1344:1536]
    pick = [dot((iota((32, 768), 1) == 24 * iota((32, 768), 0) + n).astype(BF), packed).astype(BF) for n in range(2)]

    def spread(src, width, base, group, shift):
        lane = iota((192, width), 1)
        one_hot = iota((192, width), 0) == lax.rem(lane, group) + base
        lane = iota((32, width), 1)
        keep = iota((32, width), 0) == lax.div(lane, group) + shift
        return jnp.sum(jnp.where(keep, dot(src, one_hot.astype(BF)), 0.0), axis=0, keepdims=True)

    g1, b1, g2, b2, out_b, down_b = (spread(pick[0], 768, 24 * n, 24, 0) for n in range(6))
    mix_b = spread(pick[1], 576, 0, 72, 8 * x)
    up_b = spread(pick[1], 768, 72 + 24 * x, 24, 0)
    vec[...] = jnp.concatenate([g1, b1, g2, b2, out_b + down_b, up_b, g1, g1], axis=0)

    write(w, w_o)
    write(vec, vec_o)
    write(table, table_o)

    def compute(who):
        @pl.loop(0, 2)
        def _(i):
            r = pl.ds(pl.multiple_of(who * 512 + i * 256, 256), 256)
            cols = pl.ds(pl.multiple_of(i * 256, 256), 256)
            unit = units[r]
            one = (unit * vec[0:1] + vec[1:2]).astype(BF)
            mixed[r] = (dot(one, w[0, :, 768:1344]) + mix_b).astype(BF)
            two = (unit * vec[2:3] + vec[3:4]).astype(BF)
            hidden = dot(two, w[1, :, 0:768]) + vec[5:6]
            a, s = gelu_and_slope(hidden)
            a = a.astype(BF)
            act[r] = a
            actt[who, :, cols] = a.T
            slope[r] = s.astype(BF)

        t = pl.ds(pl.multiple_of(who * 512, 512), 512)
        write(mixed.at[t], mixed_o.at[t])
        write(act.at[t], act_o.at[t])
        write(slope.at[t], slope_o.at[t])
        write(actt.at[who], actt_o.at[who])

    compute(x)
    compute(left)
    compute(right)
    for i in range(2):
        landed(quarter(far, i), rf.at[0, i])
        landed(quarter(far, 3 - i), rf.at[1, i])
    norm(far)
    compute(far)
    for k in (1, 3, 2):
        t = pl.ds(pl.multiple_of(lax.rem(x + 4 - k, 4) * 512, 512), 512)
        landed(cg.at[t], rc.at[k - 1])
    write(cg, cg_o)
    for cp in writes:
        cp.wait()
    for cp in started:
        cp.wait_send()


def front(rows, grad, pos, packed, mix, out, up, down):
    hbm = pl.BlockSpec(memory_space=pl.ANY)
    vm = pl.BlockSpec(memory_space=pltpu.VMEM)
    dma = pltpu.SemaphoreType.DMA
    outs = [
        ((2048, 576), BF), ((2048, 768), BF), ((4, 768, 512), BF), ((2048, 768), BF), ((4, 768, 512), BF),
        ((2048, 192), BF), ((2, 768, WIDE), BF), ((8, 768), F32), ((2048, 128), F32),
    ]
    return pl.pallas_call(
        front_kernel,
        out_shape=tuple(jax.ShapeDtypeStruct(s, t) for s, t in outs),
        in_specs=[hbm] * 2 + [vm] * 6,
        out_specs=[hbm] * 9,
        scratch_shapes=[
            pltpu.VMEM((2048, 768), BF),
            pltpu.VMEM((2048, 768), F32),
            pltpu.VMEM((2, 768, WIDE), BF),
            pltpu.VMEM((4, 1, 512), jnp.int32),
            pltpu.VMEM((512, 768), BF),
            pltpu.VMEM((2048, 576), BF),
            pltpu.VMEM((2048, 768), BF),
            pltpu.VMEM((4, 768, 512), BF),
            pltpu.VMEM((2048, 768), BF),
            pltpu.VMEM((4, 768, 512), BF),
            pltpu.VMEM((2048, 192), BF),
            pltpu.VMEM((4, 512, 192), BF),
            pltpu.VMEM((8, 768), F32),
            pltpu.VMEM((2048, 128), F32),
            pltpu.VMEM((32, WIDE), BF),
            pltpu.VMEM((32, WIDE), BF),
            pltpu.VMEM((PAIR, WIDE), BF),
            dma((3,)), dma((3,)), dma((4, 3)), dma((4, 3)), dma((4, 4)), dma((4, 4)),
            dma((2, 4)), dma((2, 4)), dma((2, 2)), dma((2, 2)), dma((3,)), dma((3,)), dma((3,)), dma((3,)),
            dma((1,)), dma((1,)), dma((3,)), dma((24,)),
        ],
        compiler_params=pltpu.CompilerParams(
            collective_id=0, has_side_effects=True, vmem_limit_bytes=VMEM_LIMIT
        ),
        name="front_all",
    )(rows, grad, pos, packed, mix, out, up, down)


BQ = 256
NB = 2048 // BQ


def attention_kernel(
    mixed_ref, table_ref, grad_ref, ctx_ref, ctxt_ref, out_ref,
    qs, ks, vs, qt, ea, eb, sa, sb, dkt, dvt, dqs, os, gs,
):
    row, lane = iota((64, 64), 0), iota((64, 64), 1)
    turn = jnp.where((lane == row + 8) & (row < 8), 1.0, jnp.where((row == lane + 8) & (lane < 8), -1.0, 0.0))
    turn = turn.astype(BF)
    scores, expd = (sa, sb), (ea, eb)

    def angles(r):
        t = table_ref[r]
        return t[:, 0:64], jnp.where(iota((512, 64), 1) < ROT, t[:, 64:128], 0.0)

    def with_lanes(v, first, second):
        lane = iota((v.shape[0], 128), 1)
        wide = jnp.concatenate([v, jnp.zeros((v.shape[0], 64), F32)], axis=1)
        return jnp.where(lane == 64, first, jnp.where(lane == 65, second, wide)).astype(BF)

    @pl.loop(0, 4)
    def _(i):
        r = pl.ds(pl.multiple_of(i * 512, 512), 512)
        cosine, sine = angles(r)
        for h in range(3):
            q = mixed_ref[r, h * 192 : h * 192 + 64]
            k = mixed_ref[r, h * 192 + 64 : h * 192 + 128]
            v = mixed_ref[r, h * 192 + 128 : h * 192 + 192]
            q = q.astype(F32) * cosine + dot(q, turn) * sine
            k = k.astype(F32) * cosine + dot(k, turn) * sine
            q = q.astype(BF) * 0.125
            qs[h, r] = q
            qt[h, :, r] = q.astype(F32).T.astype(BF)
            ks[h, r] = k.astype(BF)
            vs[h, r] = with_lanes(v.astype(F32), 1.0, 1.0)
            gs[h, r] = grad_ref[r, h * 64 : h * 64 + 64]

    @pl.loop(0, 3)
    def _(h):
        dkt[h] = jnp.zeros((64, 2048), F32)
        dvt[h] = jnp.zeros((64, 2048), F32)
        top, wide, grad_t = {}, {}, {}

        def score(i):
            r, n = pl.ds(i * BQ, BQ), (i + 1) * BQ
            s = dot_nt(qs[h, r], ks[h, 0:n])
            start = table_ref[r, 80:81].astype(jnp.int32)
            middle = 512 <= i * BQ < 1536
            parts = []
            for a in range(0, n, BQ):
                part = s[:, a : a + BQ]
                cols = iota((BQ, BQ), 1)
                keep = None if middle and a >= 512 else cols >= start - a
                if a + BQ == n:
                    causal = cols <= iota((BQ, BQ), 0)
                    keep = causal if keep is None else keep & causal
                parts.append(part if keep is None else jnp.where(keep, part, -1e30))
            s = jnp.concatenate(parts, axis=1)
            scores[i % 2][:, 0:n] = s
            m = s[:, 0:128]
            for t in range(128, n, 128):
                m = jnp.maximum(m, s[:, t : t + 128])
            top[i] = jnp.max(m, axis=-1, keepdims=True)

        def probs(i):
            r, n = pl.ds(i * BQ, BQ), (i + 1) * BQ
            e = jnp.exp(scores[i % 2][:, 0:n] - top[i]).astype(BF)
            expd[i % 2][:, 0:n] = e
            acc = dot(e, vs[h, 0:n])
            inverse = 1.0 / acc[:, 64:65]
            o = acc[:, :64] * inverse
            os[h, r] = o.astype(BF)
            g = gs[h, r].astype(F32) * inverse
            delta = -jnp.sum(g * o, axis=-1, keepdims=True)
            high = delta.astype(BF).astype(F32)
            wide[i] = with_lanes(g, high, delta - high)
            grad_t[i] = g.T.astype(BF)

        def back(i):
            r, n = pl.ds(i * BQ, BQ), (i + 1) * BQ
            dp = dot_nt(wide[i], vs[h, 0:n])
            e = expd[i % 2][:, 0:n]
            ds = e * dp.astype(BF)
            dqs[h, r] = dot(ds, ks[h, 0:n]) * 0.125
            dkt[h, :, 0:n] += dot(qt[h, :, r], ds)
            dvt[h, :, 0:n] += dot(grad_t[i], e)

        for step in range(NB + 2):
            if 1 <= step <= NB:
                probs(step - 1)
            if step < NB:
                score(step)
            if step >= 2:
                back(step - 2)

    @pl.loop(0, 4)
    def _(i):
        r = pl.ds(pl.multiple_of(i * 512, 512), 512)
        cosine, sine = angles(r)

        def unturn(g):
            return g * cosine + dot_nt((g * sine).astype(BF), turn)

        parts = []
        for h in range(3):
            parts.append(unturn(dqs[h, r]))
            parts.append(unturn(dkt[h, :, r].T))
            parts.append(dvt[h, :, r].T)
        out_ref[r] = jnp.concatenate(parts, axis=1).astype(BF)
        ctx = jnp.concatenate([os[h, r].astype(F32) for h in range(3)], axis=1)
        ctx_ref[r] = ctx.astype(BF)
        ctxt_ref[:, r] = ctx.T.astype(BF)


def attention(mixed, table, grads):
    vm = pl.BlockSpec(memory_space=pltpu.VMEM)
    return pl.pallas_call(
        attention_kernel,
        out_shape=(
            jax.ShapeDtypeStruct((2048, 192), BF),
            jax.ShapeDtypeStruct((192, 2048), BF),
            jax.ShapeDtypeStruct((2048, 576), BF),
        ),
        in_specs=[vm] * 3,
        out_specs=[vm] * 3,
        scratch_shapes=[
            pltpu.VMEM((3, 2048, 64), BF),
            pltpu.VMEM((3, 2048, 64), BF),
            pltpu.VMEM((3, 2048, 128), BF),
            pltpu.VMEM((3, 64, 2048), BF),
            pltpu.VMEM((BQ, 2048), BF),
            pltpu.VMEM((BQ, 2048), BF),
            pltpu.VMEM((BQ, 2048), F32),
            pltpu.VMEM((BQ, 2048), F32),
            pltpu.VMEM((3, 64, 2048), F32),
            pltpu.VMEM((3, 64, 2048), F32),
            pltpu.VMEM((3, 2048, 64), F32),
            pltpu.VMEM((3, 2048, 64), BF),
            pltpu.VMEM((3, 2048, 64), BF),
        ],
        compiler_params=pltpu.CompilerParams(vmem_limit_bytes=VMEM_LIMIT),
        cost_estimate=pl.CostEstimate(
            flops=30_000_000_000, bytes_accessed=10_000_000, transcendentals=8_000_000
        ),
        name="attention_both",
    )(mixed, table, grads)


def tail_kernel(
    ctx_h, ctxt_h, mg_h, act_h, actt_h, dg_h, unitt_h, w_h, vec_ref, ga_h, gb_h, gc_h, gd_h, rows_ref,
    out_ref, back_ref, wout_ref, wmix_ref, wup_ref, wdown_ref, small_ref,
    ctx, ctxt, mg, act, actt, hl, unitt, w, g, buf, passed, got, grads, first_in, second_in, part, third_in, fin_ref, col, mixcol,
    ld, sa, ra, sb, rb, s0, r0, s1, r1, s2, r2, s3, r3, s4, r4,
):
    x, z, y, c = places()
    is0 = c == 0
    me = lax.axis_index("shard")
    right, left = lax.rem(x + 1, 4), lax.rem(x + 3, 4)
    sibling = (x, me + 1 - 2 * c)

    def tok(k):
        return pl.ds(pl.multiple_of(lax.rem(x + 4 - k, 4) * 512, 512), 512)

    loads = []

    def load(src, dst):
        cp = pltpu.make_async_copy(src, dst, ld.at[len(loads)])
        cp.start()
        loads.append(cp)
        return cp

    l_ctx = load(ctx_h, ctx)
    l_w = load(w_h, w)
    l_act = load(act_h, act)
    l_g = [load(s, g.at[tok(k)]) for k, s in enumerate((ga_h, gb_h, gc_h, gd_h))]
    l_dg = load(dg_h, hl)
    l_mg = load(mg_h, mg)
    l_unitt = load(unitt_h, unitt)
    l_actt = load(actt_h, actt)
    l_ctxt = load(ctxt_h, ctxt)

    def first(k):
        return at(x, jnp.where(is0, lax.rem(z + k, 4), z), jnp.where(is0, y, lax.rem(y + k, 4)), c)

    def second(k):
        return at(x, jnp.where(is0, z, lax.rem(z + k, 4)), jnp.where(is0, lax.rem(y + k, 4), y), c)

    here1 = jnp.where(is0, z, y)
    here2 = jnp.where(is0, y, z)

    def rows(a, b, flip):
        blk = jnp.where(is0 != flip, a * 4 + b, b * 4 + a)
        return pl.ds(pl.multiple_of(blk * PAIR, 16), PAIR)

    barrier = pltpu.get_barrier_semaphore()
    peers = [first(k) for k in (1, 2, 3)] + [second(k) for k in (1, 2, 3)] + [sibling]
    peers += [(lax.rem(x + k, 4), me) for k in (1, 2, 3)]
    for peer in peers:
        pl.semaphore_signal(barrier, inc=1, device_id=peer, device_id_type=MESH)
    pl.semaphore_wait(barrier, len(peers))
    started = []

    def remote(src, dst, ss, rs, dev):
        cp = pltpu.make_async_remote_copy(
            src_ref=src, dst_ref=dst, send_sem=ss, recv_sem=rs, device_id=dev, device_id_type=MESH
        )
        return cp

    def send(*args):
        cp = remote(*args)
        cp.start()
        started.append(cp)

    def landed(dst, sem):
        remote(dst, dst, sem, sem, sibling).wait_recv()

    half = [pl.ds(0, 256), pl.ds(256, 256)]
    dev_x = [(right, me), (left, me)]

    def far_send(n):
        for d in range(2):
            send(buf.at[n, 2, half[d]], passed.at[n, d], sa.at[n, d], ra.at[n, d], dev_x[d])

    def near_send(n, d, h):
        send(buf.at[n, 3 - 2 * d, half[h]], got.at[n, d, half[h]], sb.at[n, d, h], rb.at[n, d, h], dev_x[d])

    def pass_on(n):
        for d in range(2):
            landed(passed.at[n, d], ra.at[n, d])
            k = 3 - 2 * d
            buf[n, k, half[d]] = (buf[n, k, half[d]].astype(F32) + passed[n, d].astype(F32)).astype(BF)
            near_send(n, d, d)

    def total(n, h):
        for d in range(2):
            landed(got.at[n, d, half[h]], rb.at[n, d, h])
        return buf[n, 0, half[h]].astype(F32) + got[n, 0, half[h]].astype(F32) + got[n, 1, half[h]].astype(F32)

    out_rows = pl.ds(pl.multiple_of(x * 192, 64), 192)

    def outputs_of(k):
        base = lax.rem(x + 4 - k, 4) * 512

        @pl.loop(0, 2)
        def _(i):
            r = pl.ds(pl.multiple_of(base + i * 256, 256), 256)
            o = dot(ctx[r], w[0, out_rows, 0:768]) + dot(act[r], w[1, :, 768:])
            buf[0, k, pl.ds(pl.multiple_of(i * 256, 256), 256)] = o.astype(BF)

    def pulls_of(k):
        base = lax.rem(x + 4 - k, 4) * 512

        @pl.loop(0, 2)
        def _(i):
            r = pl.ds(pl.multiple_of(base + i * 256, 256), 256)
            ag = dot_nt(g[r], w[1, :, 768:])
            low = (ag * hl[r].astype(F32)).astype(BF)
            hl[r] = low
            s = dot_nt(low, w[1, :, 0:768]) * vec_ref[2:3] + dot_nt(mg[r], w[0, :, 768:1344]) * vec_ref[0:1]
            buf[1, k, pl.ds(pl.multiple_of(i * 256, 256), 256)] = s.astype(BF)

    l_ctx.wait()
    l_w.wait()
    l_act.wait()
    for k in (2, 3, 1, 0):
        outputs_of(k)
        if k == 2:
            far_send(0)
        elif k == 3:
            near_send(0, 0, 1)
        elif k == 1:
            near_send(0, 1, 0)
    for cp in l_g:
        cp.wait()
    l_dg.wait()
    l_mg.wait()
    for k in (2, 3, 1, 0):
        pulls_of(k)
        if k == 2:
            far_send(1)
        elif k == 3:
            near_send(1, 0, 1)
        elif k == 1:
            near_send(1, 1, 0)
    pass_on(0)
    l_unitt.wait()
    l_actt.wait()
    l_ctxt.wait()
    ones = jnp.ones((16, 2048), BF)
    sum_mix = dot(ones, mg[...])[0:8]
    sum_up = dot(ones, hl[...])[0:8]
    sum_g = dot(ones, g[...])[0:8]
    gains = jnp.concatenate([vec_ref[...], sum_up, sum_g], axis=0)
    col[...] = jnp.concatenate([gains, jnp.zeros((104, 768), F32)], axis=0).T

    grads[0, :, 0:768] = jnp.zeros((768, 768), BF)
    grads[0, out_rows, 0:768] = dot(ctxt[...], g[...]).astype(BF)
    mixcol[...] = jnp.concatenate([sum_mix, jnp.zeros((120, 576), F32)], axis=0).T
    lane = iota((192, 192), 1)
    bias = jnp.zeros((192, 192), F32)
    for n in range(3):
        bias = jnp.where(lane == 6 + n, mixcol[pl.ds(n, 192, stride=3), 0:1], bias)

    def gradients_of(zone):
        r = pl.ds(pl.multiple_of(zone * 192, 64), 192)
        cols = col[r]

        def over_tokens(a, b):
            return sum(dot(a[n, r], b[n * 512 : n * 512 + 512]) for n in range(4))

        u1 = over_tokens(unitt, mg)
        wm = w[0, r, 768:1344].astype(F32)
        gain1 = jnp.sum(wm * u1, axis=-1, keepdims=True)
        shift1 = jnp.sum(wm * sum_mix[0:1], axis=-1, keepdims=True)
        dmix = u1 * cols[:, 0:1] + cols[:, 1:2] * sum_mix[0:1]
        u2 = over_tokens(unitt, hl)
        wu = w[1, r, 0:768].astype(F32)
        gain2 = jnp.sum(wu * u2, axis=-1, keepdims=True)
        shift2 = jnp.sum(wu * sum_up[0:1], axis=-1, keepdims=True)
        grads[1, r, 0:768] = (u2 * cols[:, 2:3] + cols[:, 3:4] * sum_up[0:1]).astype(BF)
        grads[1, r, 768:] = over_tokens(actt, g).astype(BF)
        small = jnp.where(zone == x, bias, 0.0)
        for n, v in enumerate((gain1, shift1, gain2, shift2, cols[:, 16:17], cols[:, 8:9])):
            small = jnp.where(lane == n, v, small)
        grads[0, r, 768:1536] = jnp.concatenate([dmix, small], axis=1).astype(BF)

    def block_rows(zone, b):
        return pl.ds(pl.multiple_of((zone * 4 + b) * PAIR, 16), PAIR)

    def add_sibling(zone):
        for b in range(4):
            r = block_rows(zone, b)
            landed(first_in.at[r], r0.at[zone, b])
            grads[c, r] = (grads[c, r].astype(F32) + first_in[r].astype(F32)).astype(BF)
            one, two = jnp.where(is0, zone, b), jnp.where(is0, b, zone)
            k = lax.rem(one + 4 - here1, 4)

            @pl.when(k != 0)
            def _():
                remote(
                    grads.at[c, r], second_in.at[k - 1, two], s1.at[k - 1, two], r1.at[k - 1, two], first(k)
                ).start()

    order = (1, 3, 2, 0)
    zones = [lax.rem(z + k, 4) for k in order]
    for n, zone in enumerate(zones):
        gradients_of(zone)
        for b in range(4):
            r = block_rows(zone, b)
            send(grads.at[1 - c, r], first_in.at[r], s0.at[zone, b], r0.at[zone, b], sibling)
        if n:
            add_sibling(zones[n - 1])
    add_sibling(zones[3])
    pass_on(1)
    lane = iota((1, WIDE), 1)
    group = lax.rem(lax.div(lane, 24), 4)
    source = lax.div(lane, 96) * 24 + lax.rem(lane, 24)
    for d in range(4):
        hot = iota((384, WIDE), 0) == jnp.where(group == d, source, -1)
        w[d // 2, (d % 2) * 384 : (d % 2) * 384 + 384] = hot.astype(F32).astype(BF)
    for j in order:
        b = lax.rem(here2 + j, 4)
        r = rows(here1, b, False)
        acc = grads[c, r].astype(F32)
        for k in (1, 3, 2):
            landed(second_in.at[k - 1, b], r1.at[k - 1, b])
            acc = acc + second_in[k - 1, b].astype(F32)
        part[j] = acc.astype(BF)
        if j:
            send(part.at[j], third_in.at[j - 1], s2.at[j - 1], r2.at[j - 1], second(j))
    for h in range(2):
        o = total(0, h) + rows_ref[half[h]].astype(F32) + vec_ref[4:5]
        out_ref[half[h]] = o
    acc = part[0].astype(F32)
    for j in (1, 3, 2):
        landed(third_in.at[j - 1], r2.at[j - 1])
        acc = acc + third_in[j - 1].astype(F32)
    fin_ref[c, x] = acc.astype(BF)
    for k in (1, 3, 2):
        slot = fin_ref.at[c, x]
        send(slot, slot, s3.at[k - 1], r3.at[k - 1], (lax.rem(x + k, 4), me))
    slot = fin_ref.at[c, x]
    send(slot, slot, s4.at[0], r4.at[0], sibling)
    for h in range(2):
        s = total(1, h)
        v = rows_ref[half[h]].astype(F32)
        v = v - jnp.mean(v, axis=-1, keepdims=True)
        inverse = lax.rsqrt(jnp.mean(v * v, axis=-1, keepdims=True) + 1e-05)
        unit = v * inverse
        s = s - jnp.mean(s, axis=-1, keepdims=True) - unit * jnp.mean(s * unit, axis=-1, keepdims=True)
        own = pl.ds(pl.multiple_of(x * 512 + h * 256, 256), 256)
        back_ref[half[h]] = g[own].astype(F32) + inverse * s
    for k in (1, 3, 2):
        slot = fin_ref.at[c, lax.rem(x + 4 - k, 4)]
        landed(slot, r3.at[k - 1])
        send(slot, slot, s4.at[k], r4.at[k], sibling)
    for k in range(4):
        landed(fin_ref.at[1 - c, lax.rem(x + 4 - k, 4)], r4.at[k])

    def mine(role, d, a, b):
        v = fin_ref[role, d, :, a:b].astype(F32)
        return jnp.where(is0, v[0:24], v[24:48])

    wout_ref[...] = sum(mine(0, d, 0, 768) for d in range(4))
    tails = [mine(0, d, 768, WIDE) for d in range(4)]
    wmix_ref[...] = jnp.concatenate([t[:, 0:576] for t in tails], axis=1)
    lane = iota((24, 128), 1)
    small = sum(t[:, 576:704] for t in tails)
    for d in range(4):
        small = jnp.where(lane == 16 + d, tails[d][:, 581:582], small)
    small = jnp.where(lane == 4, tails[0][:, 576:704], small)
    small_ref[...] = jnp.concatenate([small, jnp.zeros((104, 128), F32)], axis=0).T[0:24]
    ups = [mine(1, d, 0, 768).astype(BF) for d in range(4)]
    for n in range(2):
        wup_ref[:, n * WIDE : n * WIDE + WIDE] = sum(
            dot(ups[d][:, n * 384 : n * 384 + 384], w[d // 2, (d % 2) * 384 : (d % 2) * 384 + 384])
            for d in range(4)
        )
    for d in range(4):
        wdown_ref[d * 24 : d * 24 + 24] = mine(1, d, 768, WIDE)
    for cp in started:
        cp.wait_send()
    for k in range(3):
        for b in range(4):
            remote(second_in.at[k, b], second_in.at[k, b], s1.at[k, b], r1.at[k, b], sibling).wait_send()


def tail(ctx, ctxt, mg, act, actt, dg, unitt, w, vec, g, rows):
    vm = pl.BlockSpec(memory_space=pltpu.VMEM)
    hbm = pl.BlockSpec(memory_space=pl.ANY)
    dma = pltpu.SemaphoreType.DMA
    return pl.pallas_call(
        tail_kernel,
        out_shape=(
            jax.ShapeDtypeStruct((512, 768), F32),
            jax.ShapeDtypeStruct((512, 768), F32),
            jax.ShapeDtypeStruct((24, 768), F32),
            jax.ShapeDtypeStruct((24, 2304), F32),
            jax.ShapeDtypeStruct((24, 3072), F32),
            jax.ShapeDtypeStruct((96, 768), F32),
            jax.ShapeDtypeStruct((24, 128), F32),
        ),
        in_specs=[hbm] * 8 + [vm] + [hbm] * 4 + [vm],
        out_specs=[vm] * 7,
        scratch_shapes=[
            pltpu.VMEM((2048, 192), BF),
            pltpu.VMEM((192, 2048), BF),
            pltpu.VMEM((2048, 576), BF),
            pltpu.VMEM((2048, 768), BF),
            pltpu.VMEM((4, 768, 512), BF),
            pltpu.VMEM((2048, 768), BF),
            pltpu.VMEM((4, 768, 512), BF),
            pltpu.VMEM((2, 768, WIDE), BF),
            pltpu.VMEM((2048, 768), BF),
            pltpu.VMEM((2, 4, 512, 768), BF),
            pltpu.VMEM((2, 2, 256, 768), BF),
            pltpu.VMEM((2, 2, 512, 768), BF),
            pltpu.VMEM((2, 768, WIDE), BF),
            pltpu.VMEM((768, WIDE), BF),
            pltpu.VMEM((3, 4, PAIR, WIDE), BF),
            pltpu.VMEM((4, PAIR, WIDE), BF),
            pltpu.VMEM((3, PAIR, WIDE), BF),
            pltpu.VMEM((2, 4, PAIR, WIDE), BF),
            pltpu.VMEM((768, 128), F32),
            pltpu.VMEM((576, 128), F32),
            dma((12,)),
            dma((2, 2)), dma((2, 2)), dma((2, 2, 2)), dma((2, 2, 2)),
            dma((4, 4)), dma((4, 4)), dma((3, 4)), dma((3, 4)), dma((3,)), dma((3,)),
            dma((3,)), dma((3,)), dma((4,)), dma((4,)),
        ],
        compiler_params=pltpu.CompilerParams(
            collective_id=1, has_side_effects=True, vmem_limit_bytes=60 * 1024 * 1024
        ),
        name="tail_all",
    )(ctx, ctxt, mg, act, actt, dg, unitt, w, vec, *g, rows)


def shift_x(v, k):
    return lax.ppermute(v, "seq", [(i, (i + k) % NX) for i in range(NX)])


def local(
    inputs, positions, first_gain, first_shift, second_gain, second_shift, mix_weight, mix_bias,
    out_weight, out_bias, up_weight, up_bias, down_weight, down_bias, cotangent,
):
    flat = jnp.zeros((384,), BF)
    for place, v in (
        (0, first_gain), (24, first_shift), (48, second_gain), (72, second_shift), (96, out_bias),
        (120, down_bias), (192, mix_bias), (264, up_bias),
    ):
        flat = flat + jnp.pad(v, (place, 384 - place - v.shape[0]))
    packed = jnp.pad(flat.reshape(2, 192), ((0, 22), (0, 0)))
    grad = cotangent[0]
    mixed, act, actt, slope, unitt, context_grad, w, vec, table = front(
        inputs[0], grad, positions, packed, mix_weight, out_weight, up_weight, down_weight
    )
    late, table = lax.optimization_barrier((grad, table))
    grads = [grad] + [shift_x(late, k) for k in (1, 2, 3)]
    context, context_t, mix_grad = attention(mixed, table, context_grad)
    outputs, input_grad, g_out, g_mix, g_up, g_down, small = tail(
        context, context_t, mix_grad, act, actt, slope, unitt, w, vec, grads, inputs[0]
    )
    return (
        outputs.astype(BF)[None],
        input_grad.astype(BF)[None],
        small[0, :24],
        small[1, :24],
        small[2, :24],
        small[3, :24],
        g_mix,
        small[6:9, :24].T.reshape(72),
        g_out,
        small[4, :24],
        g_up,
        small[16:20, :24].reshape(96),
        g_down,
        small[4, :24],
    )


def solution(mesh):
    vec, mat, tok = P("shard"), P("shard", None), P("shard", "seq", None)
    return jax.shard_map(
        local,
        mesh=mesh,
        in_specs=(tok, P("shard", "seq"), vec, vec, vec, vec, mat, vec, mat, vec, mat, vec, mat, vec, tok),
        out_specs=(tok, tok, vec, vec, vec, vec, mat, vec, mat, vec, mat, vec, mat, vec),
        check_vma=False,
    )
```

```python
import jax
import jax.numpy as jnp
from jax import lax
from jax.experimental import pallas as pl
from jax.experimental.pallas import tpu as pltpu
from jax.sharding import PartitionSpec as P

HD = 64
ROT = 16
NX = 4
BF = jnp.bfloat16
F32 = jnp.float32
MESH = pl.DeviceIdType.MESH
NT = (((1,), (1,)), ((), ()))
VMEM_LIMIT = 56 * 1024 * 1024
WIDE = 1536
PAIR = 48


def dot(a, b):
    return jnp.dot(a, b, preferred_element_type=F32)


def dot_nt(a, b):
    return lax.dot_general(a, b, NT, preferred_element_type=F32)


def dot_tn(a, b):
    return lax.dot_general(a, b, (((0,), (0,)), ((), ())), preferred_element_type=F32)


def places():
    x = lax.axis_index("seq")
    s = lax.axis_index("shard")
    return x, s // 8, (s // 2) % 4, s % 2


def at(x, z, y, c):
    return (x, (z * 4 + y) * 2 + c)


ERFC = (0.254829592, -0.284496736, 1.421413741, -1.453152027, 1.061405429)


def gelu_and_slope(h):
    t = 1.0 / (1.0 + (0.3275911 * 2.0**-0.5) * jnp.abs(h))
    e = jnp.exp(h * h * -0.5)
    poly = t * (ERFC[0] + t * (ERFC[1] + t * (ERFC[2] + t * (ERFC[3] + t * ERFC[4]))))
    tail_part = 0.5 * poly * e
    cdf = jnp.where(h >= 0, 1.0 - tail_part, tail_part)
    return h * cdf, cdf + h * e * 0.3989422804014327


def iota(shape, dim):
    return lax.broadcasted_iota(jnp.int32, shape, dim)


def front_kernel(
    rows_ref, grad_ref, pos_ref, packed_ref, mix_ref, out_ref, up_ref, down_ref,
    mixed_o, act_o, actt_o, slope_o, unitt_o, cg_o, w_o, vec_o, table_o,
    rows_all, units, w, pos_all, grad, mixed, act, actt, slope, unitt, cg, cgs, vec, table, give, came, pair_ref,
    s1, r1, s2, r2, s3, r3, sx, rx, sf, rf, sp, rp, sc, rc, sg, rg, loc, wr,
):
    x, z, y, c = places()
    is0 = c == 0
    right, left, far = lax.rem(x + 1, 4), lax.rem(x + 3, 4), lax.rem(x + 2, 4)
    me = lax.axis_index("shard")
    mine, other = w.at[c], w.at[1 - c]

    def first(k):
        return at(x, jnp.where(is0, z, lax.rem(z + k, 4)), jnp.where(is0, lax.rem(y + k, 4), y), c)

    def second(k):
        return at(x, jnp.where(is0, lax.rem(z + k, 4), z), jnp.where(is0, y, lax.rem(y + k, 4)), c)

    def block(dz, dy):
        return lax.rem(z + dz, 4) * 4 + lax.rem(y + dy, 4)

    def held(a, b):
        da, db = (4 - a) % 4, (4 - b) % 4
        return jnp.where(is0, block(db, da), block(da, db))

    def rows_of(ref, b):
        return ref.at[pl.ds(pl.multiple_of(b * PAIR, 16), PAIR)]

    def quarter(who, q):
        return rows_all.at[pl.ds(pl.multiple_of(who * 512 + q * 128, 128), 128)]

    def remote(src, dst, ss, rs, dev):
        return pltpu.make_async_remote_copy(
            src_ref=src, dst_ref=dst, send_sem=ss, recv_sem=rs, device_id=dev, device_id_type=MESH
        )

    started = []

    def send(*args):
        cp = remote(*args)
        cp.start()
        started.append(cp)

    sibling = (x, me + 1 - 2 * c)

    def landed(dst, sem):
        remote(dst, dst, sem, sem, sibling).wait_recv()

    own_block = z * 4 + y
    own_pos = pos_all.at[x]
    local_copies = []
    for n, (src, dst) in enumerate(
        (
            (rows_ref, rows_all.at[pl.ds(pl.multiple_of(x * 512, 512), 512)]),
            (pos_ref, own_pos),
            (grad_ref, grad),
        )
    ):
        cp = pltpu.make_async_copy(src, dst, loc.at[n])
        cp.start()
        local_copies.append(cp)
    barrier = pltpu.get_barrier_semaphore()
    peers = [first(k) for k in (1, 2, 3)] + [second(k) for k in (1, 2, 3)]
    peers += [sibling, (right, me), (left, me), (far, me)]
    for peer in peers:
        pl.semaphore_signal(barrier, inc=1, device_id=peer, device_id_type=MESH)
    pl.semaphore_wait(barrier, len(peers))

    order = (1, 3, 2)
    own = [rows_ref.at[pl.ds(q * 128, 128)] for q in range(4)]
    for i in range(4):
        send(own[i], quarter(x, i), sx.at[0, i], rx.at[0, i], (right, me))
        send(own[3 - i], quarter(x, 3 - i), sx.at[1, 3 - i], rx.at[1, 3 - i], (left, me))
    for k in order:
        send(pos_ref, own_pos, sp.at[k - 1], rp.at[k - 1], (lax.rem(x + k, 4), me))

    def pick_x(parts):
        v = parts[0]
        for d in range(1, 4):
            v = jnp.where(x == d, parts[d], v)
        return v

    mix_part = pick_x([mix_ref[:, d * 576 : d * 576 + 576].astype(F32) for d in range(4)])
    half_a = jnp.concatenate([out_ref[...].astype(F32), mix_part, packed_ref[...].astype(F32)], axis=1)
    lane = iota((1, 384), 1)
    hot = iota((WIDE, 384), 0) == lax.div(lane, 24) * 96 + lax.rem(lane, 24) + 24 * x
    hot = hot.astype(F32).astype(BF)
    down_own = down_ref[...].astype(F32)
    half_b = jnp.concatenate(
        [dot(up_ref[:, 0:WIDE], hot), dot(up_ref[:, WIDE:], hot), pick_x([down_own[d * 24 : d * 24 + 24] for d in range(4)])],
        axis=1,
    )
    give[...] = jnp.concatenate([jnp.where(is0, half_b, half_a), jnp.zeros((8, WIDE), F32)], axis=0).astype(BF)
    send(give, came, sg.at[0], rg.at[0], sibling)
    for cp in local_copies:
        cp.wait()
    writes = []

    def write(src, dst):
        cp = pltpu.make_async_copy(src, dst, wr.at[len(writes)])
        cp.start()
        writes.append(cp)

    def norm(who):
        @pl.loop(0, 2)
        def _(i):
            r = pl.ds(pl.multiple_of(who * 512 + i * 256, 256), 256)
            v = rows_all[r].astype(F32)
            v = v - jnp.mean(v, axis=-1, keepdims=True)
            unit = v * lax.rsqrt(jnp.mean(v * v, axis=-1, keepdims=True) + 1e-05)
            units[r] = unit
            unitt[who, :, pl.ds(pl.multiple_of(i * 256, 256), 256)] = unit.astype(BF).T

        write(unitt.at[who], unitt_o.at[who])

    norm(x)
    landed(came, rg.at[0])
    theirs = came[...].astype(F32)[0:24]
    kept = jnp.where(is0, half_a, half_b)
    pair = jnp.concatenate([jnp.where(is0, kept, theirs), jnp.where(is0, theirs, kept)], axis=0).astype(BF)
    pair_ref[...] = pair
    w[c, pl.ds(pl.multiple_of(own_block * PAIR, 16), PAIR)] = pair
    for k in order:
        send(pair_ref, rows_of(mine, own_block), s1.at[k - 1], r1.at[k - 1], first(k))
    for k in order:
        send(pair_ref, rows_of(mine, own_block), s2.at[0, k - 1], r2.at[0, k - 1], second(k))
    send(pair_ref, rows_of(mine, own_block), s3.at[0, 0], r3.at[0, 0], sibling)

    for k in order:
        b = held(k, 0)
        landed(rows_of(mine, b), r1.at[k - 1])
        for j in order:
            send(rows_of(mine, b), rows_of(mine, b), s2.at[k, j - 1], r2.at[k, j - 1], second(j))
        send(rows_of(mine, b), rows_of(mine, b), s3.at[k, 0], r3.at[k, 0], sibling)

    for k in order:
        landed(pos_all.at[lax.rem(x + 4 - k, 4)], rp.at[k - 1])
    place = jnp.concatenate([pos_all[d] for d in range(4)], axis=1).astype(F32)
    freqs = jnp.ones((8, 2048), F32)
    for n in range(1, 8):
        freqs = jnp.where(iota((8, 2048), 0) == n, 10000.0 ** (-2.0 * n / ROT), freqs)
    angles = place * freqs
    cos8, sin8 = jnp.cos(angles), jnp.sin(angles)
    start = jnp.broadcast_to(iota((1, 2048), 1).astype(F32) - place, (8, 2048))
    table[...] = jnp.concatenate(
        [cos8, cos8, jnp.ones((48, 2048), F32), sin8, sin8, start, jnp.zeros((40, 2048), F32)], axis=0
    ).T

    for i in range(2):
        landed(quarter(left, i), rx.at[0, i])
        send(quarter(left, i), quarter(left, i), sf.at[0, i], rf.at[0, i], (right, me))
        landed(quarter(right, 3 - i), rx.at[1, 3 - i])
        send(quarter(right, 3 - i), quarter(right, 3 - i), sf.at[1, i], rf.at[1, i], (left, me))
    for j in order:
        for k in (0,) + order:
            b = held(k, j)
            landed(rows_of(mine, b), r2.at[k, j - 1])
            send(rows_of(mine, b), rows_of(mine, b), s3.at[k, j], r3.at[k, j], sibling)
    for i in range(2):
        landed(quarter(left, 2 + i), rx.at[0, 2 + i])
        landed(quarter(right, i), rx.at[1, i])
    norm(left)
    norm(right)
    for a in range(4):
        for b in range(4):
            da, db = (4 - a) % 4, (4 - b) % 4
            blk = jnp.where(is0, block(da, db), block(db, da))
            landed(rows_of(other, blk), r3.at[a, b])

    own_tok = pl.ds(pl.multiple_of(x * 512, 512), 512)
    for k in (2, 1, 3, 0):
        dev = lax.rem(x + k, 4)
        heads = w[0, pl.ds(pl.multiple_of(dev * 192, 64), 192), 0:768]

        @pl.loop(0, 2)
        def _(i):
            r = pl.ds(pl.multiple_of(i * 256, 256), 256)
            cgs[k, r] = dot_nt(grad[r], heads).astype(BF)

        if k:
            send(cgs.at[k], cg.at[own_tok], sc.at[k - 1], rc.at[k - 1], (dev, me))
        else:
            cg[own_tok] = cgs[0]

    packed = w[0, :, 1344:1536]
    pick = [dot((iota((32, 768), 1) == 24 * iota((32, 768), 0) + n).astype(BF), packed).astype(BF) for n in range(2)]

    def spread(src, width, base, group, shift):
        lane = iota((192, width), 1)
        one_hot = iota((192, width), 0) == lax.rem(lane, group) + base
        lane = iota((32, width), 1)
        keep = iota((32, width), 0) == lax.div(lane, group) + shift
        return jnp.sum(jnp.where(keep, dot(src, one_hot.astype(BF)), 0.0), axis=0, keepdims=True)

    g1, b1, g2, b2, out_b, down_b = (spread(pick[0], 768, 24 * n, 24, 0) for n in range(6))
    mix_b = spread(pick[1], 576, 0, 72, 8 * x)
    up_b = spread(pick[1], 768, 72 + 24 * x, 24, 0)
    vec[...] = jnp.concatenate([g1, b1, g2, b2, out_b + down_b, up_b, g1, g1], axis=0)

    write(w, w_o)
    write(vec, vec_o)
    write(table, table_o)

    def compute(who):
        @pl.loop(0, 2)
        def _(i):
            r = pl.ds(pl.multiple_of(who * 512 + i * 256, 256), 256)
            cols = pl.ds(pl.multiple_of(i * 256, 256), 256)
            unit = units[r]
            one = (unit * vec[0:1] + vec[1:2]).astype(BF)
            mixed[r] = (dot(one, w[0, :, 768:1344]) + mix_b).astype(BF)
            two = (unit * vec[2:3] + vec[3:4]).astype(BF)
            hidden = dot(two, w[1, :, 0:768]) + vec[5:6]
            a, s = gelu_and_slope(hidden)
            a = a.astype(BF)
            act[r] = a
            actt[who, :, cols] = a.T
            slope[r] = s.astype(BF)

        t = pl.ds(pl.multiple_of(who * 512, 512), 512)
        write(mixed.at[t], mixed_o.at[t])
        write(act.at[t], act_o.at[t])
        write(slope.at[t], slope_o.at[t])
        write(actt.at[who], actt_o.at[who])

    compute(x)
    compute(left)
    compute(right)
    for i in range(2):
        landed(quarter(far, i), rf.at[0, i])
        landed(quarter(far, 3 - i), rf.at[1, i])
    norm(far)
    compute(far)
    for k in (1, 3, 2):
        t = pl.ds(pl.multiple_of(lax.rem(x + 4 - k, 4) * 512, 512), 512)
        landed(cg.at[t], rc.at[k - 1])
    write(cg, cg_o)
    for cp in writes:
        cp.wait()
    for cp in started:
        cp.wait_send()


def front(rows, grad, pos, packed, mix, out, up, down):
    hbm = pl.BlockSpec(memory_space=pl.ANY)
    vm = pl.BlockSpec(memory_space=pltpu.VMEM)
    dma = pltpu.SemaphoreType.DMA
    outs = [
        ((2048, 576), BF), ((2048, 768), BF), ((4, 768, 512), BF), ((2048, 768), BF), ((4, 768, 512), BF),
        ((2048, 192), BF), ((2, 768, WIDE), BF), ((8, 768), F32), ((2048, 128), F32),
    ]
    return pl.pallas_call(
        front_kernel,
        out_shape=tuple(jax.ShapeDtypeStruct(s, t) for s, t in outs),
        in_specs=[hbm] * 2 + [vm] * 6,
        out_specs=[hbm] * 9,
        scratch_shapes=[
            pltpu.VMEM((2048, 768), BF),
            pltpu.VMEM((2048, 768), F32),
            pltpu.VMEM((2, 768, WIDE), BF),
            pltpu.VMEM((4, 1, 512), jnp.int32),
            pltpu.VMEM((512, 768), BF),
            pltpu.VMEM((2048, 576), BF),
            pltpu.VMEM((2048, 768), BF),
            pltpu.VMEM((4, 768, 512), BF),
            pltpu.VMEM((2048, 768), BF),
            pltpu.VMEM((4, 768, 512), BF),
            pltpu.VMEM((2048, 192), BF),
            pltpu.VMEM((4, 512, 192), BF),
            pltpu.VMEM((8, 768), F32),
            pltpu.VMEM((2048, 128), F32),
            pltpu.VMEM((32, WIDE), BF),
            pltpu.VMEM((32, WIDE), BF),
            pltpu.VMEM((PAIR, WIDE), BF),
            dma((3,)), dma((3,)), dma((4, 3)), dma((4, 3)), dma((4, 4)), dma((4, 4)),
            dma((2, 4)), dma((2, 4)), dma((2, 2)), dma((2, 2)), dma((3,)), dma((3,)), dma((3,)), dma((3,)),
            dma((1,)), dma((1,)), dma((3,)), dma((24,)),
        ],
        compiler_params=pltpu.CompilerParams(
            collective_id=0, has_side_effects=True, vmem_limit_bytes=VMEM_LIMIT
        ),
        name="front_all",
    )(rows, grad, pos, packed, mix, out, up, down)


BQ = 256
NB = 2048 // BQ


def attention_kernel(
    mixed_ref, table_ref, grad_ref, ctx_ref, ctxt_ref, out_ref,
    qs, ks, vs, qt, ea, eb, sa, sb, dkt, dvt, dqs, os, gs,
):
    row, lane = iota((64, 64), 0), iota((64, 64), 1)
    turn = jnp.where((lane == row + 8) & (row < 8), 1.0, jnp.where((row == lane + 8) & (lane < 8), -1.0, 0.0))
    turn = turn.astype(BF)
    scores, expd = (sa, sb), (ea, eb)

    def angles(r):
        t = table_ref[r]
        return t[:, 0:64], jnp.where(iota((512, 64), 1) < ROT, t[:, 64:128], 0.0)

    def with_lanes(v, first, second):
        lane = iota((v.shape[0], 128), 1)
        wide = jnp.concatenate([v, jnp.zeros((v.shape[0], 64), F32)], axis=1)
        return jnp.where(lane == 64, first, jnp.where(lane == 65, second, wide)).astype(BF)

    @pl.loop(0, 4)
    def _(i):
        r = pl.ds(pl.multiple_of(i * 512, 512), 512)
        cosine, sine = angles(r)
        for h in range(3):
            q = mixed_ref[r, h * 192 : h * 192 + 64]
            k = mixed_ref[r, h * 192 + 64 : h * 192 + 128]
            v = mixed_ref[r, h * 192 + 128 : h * 192 + 192]
            q = q.astype(F32) * cosine + dot(q, turn) * sine
            k = k.astype(F32) * cosine + dot(k, turn) * sine
            q = q.astype(BF) * 0.125
            qs[h, r] = q
            qt[h, :, r] = q.astype(F32).T.astype(BF)
            ks[h, r] = k.astype(BF)
            vs[h, r] = with_lanes(v.astype(F32), 1.0, 1.0)
            gs[h, r] = grad_ref[r, h * 64 : h * 64 + 64]

    @pl.loop(0, 3)
    def _(h):
        dkt[h] = jnp.zeros((64, 2048), F32)
        dvt[h] = jnp.zeros((64, 2048), F32)
        top, wide, grad_t = {}, {}, {}

        def score(i):
            r, n = pl.ds(i * BQ, BQ), (i + 1) * BQ
            s = dot_nt(qs[h, r], ks[h, 0:n])
            start = table_ref[r, 80:81].astype(jnp.int32)
            middle = 512 <= i * BQ < 1536
            parts = []
            for a in range(0, n, BQ):
                part = s[:, a : a + BQ]
                cols = iota((BQ, BQ), 1)
                keep = None if middle and a >= 512 else cols >= start - a
                if a + BQ == n:
                    causal = cols <= iota((BQ, BQ), 0)
                    keep = causal if keep is None else keep & causal
                parts.append(part if keep is None else jnp.where(keep, part, -1e30))
            s = jnp.concatenate(parts, axis=1)
            scores[i % 2][:, 0:n] = s
            m = s[:, 0:128]
            for t in range(128, n, 128):
                m = jnp.maximum(m, s[:, t : t + 128])
            top[i] = jnp.max(m, axis=-1, keepdims=True)

        def probs(i):
            r, n = pl.ds(i * BQ, BQ), (i + 1) * BQ
            e = jnp.exp(scores[i % 2][:, 0:n] - top[i]).astype(BF)
            expd[i % 2][:, 0:n] = e
            acc = dot(e, vs[h, 0:n])
            inverse = 1.0 / acc[:, 64:65]
            o = acc[:, :64] * inverse
            os[h, r] = o.astype(BF)
            g = gs[h, r].astype(F32) * inverse
            delta = -jnp.sum(g * o, axis=-1, keepdims=True)
            high = delta.astype(BF).astype(F32)
            wide[i] = with_lanes(g, high, delta - high)
            grad_t[i] = g.T.astype(BF)

        def back(i):
            r, n = pl.ds(i * BQ, BQ), (i + 1) * BQ
            dp = dot_nt(wide[i], vs[h, 0:n])
            e = expd[i % 2][:, 0:n]
            ds = e * dp.astype(BF)
            dqs[h, r] = dot(ds, ks[h, 0:n]) * 0.125
            dkt[h, :, 0:n] += dot(qt[h, :, r], ds)
            dvt[h, :, 0:n] += dot(grad_t[i], e)

        for step in range(NB + 2):
            if 1 <= step <= NB:
                probs(step - 1)
            if step < NB:
                score(step)
            if step >= 2:
                back(step - 2)

    @pl.loop(0, 4)
    def _(i):
        r = pl.ds(pl.multiple_of(i * 512, 512), 512)
        cosine, sine = angles(r)

        def unturn(g):
            return g * cosine + dot_nt((g * sine).astype(BF), turn)

        parts = []
        for h in range(3):
            parts.append(unturn(dqs[h, r]))
            parts.append(unturn(dkt[h, :, r].T))
            parts.append(dvt[h, :, r].T)
        out_ref[r] = jnp.concatenate(parts, axis=1).astype(BF)
        ctx = jnp.concatenate([os[h, r].astype(F32) for h in range(3)], axis=1)
        ctx_ref[r] = ctx.astype(BF)
        ctxt_ref[:, r] = ctx.T.astype(BF)


def attention(mixed, table, grads):
    vm = pl.BlockSpec(memory_space=pltpu.VMEM)
    return pl.pallas_call(
        attention_kernel,
        out_shape=(
            jax.ShapeDtypeStruct((2048, 192), BF),
            jax.ShapeDtypeStruct((192, 2048), BF),
            jax.ShapeDtypeStruct((2048, 576), BF),
        ),
        in_specs=[vm] * 3,
        out_specs=[vm] * 3,
        scratch_shapes=[
            pltpu.VMEM((3, 2048, 64), BF),
            pltpu.VMEM((3, 2048, 64), BF),
            pltpu.VMEM((3, 2048, 128), BF),
            pltpu.VMEM((3, 64, 2048), BF),
            pltpu.VMEM((BQ, 2048), BF),
            pltpu.VMEM((BQ, 2048), BF),
            pltpu.VMEM((BQ, 2048), F32),
            pltpu.VMEM((BQ, 2048), F32),
            pltpu.VMEM((3, 64, 2048), F32),
            pltpu.VMEM((3, 64, 2048), F32),
            pltpu.VMEM((3, 2048, 64), F32),
            pltpu.VMEM((3, 2048, 64), BF),
            pltpu.VMEM((3, 2048, 64), BF),
        ],
        compiler_params=pltpu.CompilerParams(vmem_limit_bytes=VMEM_LIMIT),
        cost_estimate=pl.CostEstimate(
            flops=30_000_000_000, bytes_accessed=10_000_000, transcendentals=8_000_000
        ),
        name="attention_both",
    )(mixed, table, grads)


def tail_kernel(
    ctx_h, ctxt_h, mg_h, act_h, actt_h, dg_h, unitt_h, w_h, vec_ref, ga_h, gb_h, gc_h, gd_h, rows_ref,
    out_ref, back_ref, wout_ref, wmix_ref, wup_ref, wdown_ref, small_ref,
    ctx, ctxt, mg, act, actt, hl, unitt, w, g, buf, passed, got, grads, first_in, second_in, part, third_in, fin_ref, col, mixcol,
    ld, sa, ra, sb, rb, s0, r0, s1, r1, s2, r2, s3, r3, s4, r4,
):
    x, z, y, c = places()
    is0 = c == 0
    me = lax.axis_index("shard")
    right, left = lax.rem(x + 1, 4), lax.rem(x + 3, 4)
    sibling = (x, me + 1 - 2 * c)

    def tok(k):
        return pl.ds(pl.multiple_of(lax.rem(x + 4 - k, 4) * 512, 512), 512)

    loads = []

    def load(src, dst):
        cp = pltpu.make_async_copy(src, dst, ld.at[len(loads)])
        cp.start()
        loads.append(cp)
        return cp

    l_ctx = load(ctx_h, ctx)
    l_w = load(w_h, w)
    l_act = load(act_h, act)

    def first(k):
        return at(x, jnp.where(is0, lax.rem(z + k, 4), z), jnp.where(is0, y, lax.rem(y + k, 4)), c)

    def second(k):
        return at(x, jnp.where(is0, z, lax.rem(z + k, 4)), jnp.where(is0, lax.rem(y + k, 4), y), c)

    here1 = jnp.where(is0, z, y)
    here2 = jnp.where(is0, y, z)

    def rows(a, b, flip):
        blk = jnp.where(is0 != flip, a * 4 + b, b * 4 + a)
        return pl.ds(pl.multiple_of(blk * PAIR, 16), PAIR)

    barrier = pltpu.get_barrier_semaphore()
    peers = [first(k) for k in (1, 2, 3)] + [second(k) for k in (1, 2, 3)] + [sibling]
    peers += [(lax.rem(x + k, 4), me) for k in (1, 2, 3)]
    for peer in peers:
        pl.semaphore_signal(barrier, inc=1, device_id=peer, device_id_type=MESH)
    pl.semaphore_wait(barrier, len(peers))
    started = []

    def remote(src, dst, ss, rs, dev):
        cp = pltpu.make_async_remote_copy(
            src_ref=src, dst_ref=dst, send_sem=ss, recv_sem=rs, device_id=dev, device_id_type=MESH
        )
        return cp

    def send(*args):
        cp = remote(*args)
        cp.start()
        started.append(cp)

    def landed(dst, sem):
        remote(dst, dst, sem, sem, sibling).wait_recv()

    half = [pl.ds(0, 256), pl.ds(256, 256)]
    dev_x = [(right, me), (left, me)]

    def far_send(n):
        for d in range(2):
            send(buf.at[n, 2, half[d]], passed.at[n, d], sa.at[n, d], ra.at[n, d], dev_x[d])

    def near_send(n, d, h):
        send(buf.at[n, 3 - 2 * d, half[h]], got.at[n, d, half[h]], sb.at[n, d, h], rb.at[n, d, h], dev_x[d])

    def pass_on(n):
        for d in range(2):
            landed(passed.at[n, d], ra.at[n, d])
            k = 3 - 2 * d
            buf[n, k, half[d]] = (buf[n, k, half[d]].astype(F32) + passed[n, d].astype(F32)).astype(BF)
            near_send(n, d, d)

    def total(n, h):
        for d in range(2):
            landed(got.at[n, d, half[h]], rb.at[n, d, h])
        return buf[n, 0, half[h]].astype(F32) + got[n, 0, half[h]].astype(F32) + got[n, 1, half[h]].astype(F32)

    out_rows = pl.ds(pl.multiple_of(x * 192, 64), 192)

    def outputs_of(k):
        base = lax.rem(x + 4 - k, 4) * 512

        @pl.loop(0, 2)
        def _(i):
            r = pl.ds(pl.multiple_of(base + i * 256, 256), 256)
            o = dot(ctx[r], w[0, out_rows, 0:768]) + dot(act[r], w[1, :, 768:])
            buf[0, k, pl.ds(pl.multiple_of(i * 256, 256), 256)] = o.astype(BF)

    def pulls_of(k):
        base = lax.rem(x + 4 - k, 4) * 512

        @pl.loop(0, 2)
        def _(i):
            r = pl.ds(pl.multiple_of(base + i * 256, 256), 256)
            ag = dot_nt(g[r], w[1, :, 768:])
            low = (ag * hl[r].astype(F32)).astype(BF)
            hl[r] = low
            s = dot_nt(low, w[1, :, 0:768]) * vec_ref[2:3] + dot_nt(mg[r], w[0, :, 768:1344]) * vec_ref[0:1]
            buf[1, k, pl.ds(pl.multiple_of(i * 256, 256), 256)] = s.astype(BF)

    l_ctx.wait()
    l_w.wait()
    l_act.wait()
    l_g = [load(s, g.at[tok(k)]) for k, s in enumerate((ga_h, gb_h, gc_h, gd_h))]
    l_dg = load(dg_h, hl)
    l_mg = load(mg_h, mg)
    l_unitt = load(unitt_h, unitt)
    l_actt = load(actt_h, actt)
    l_ctxt = load(ctxt_h, ctxt)
    for k in (2, 3, 1, 0):
        outputs_of(k)
        if k == 2:
            far_send(0)
        elif k == 3:
            near_send(0, 0, 1)
        elif k == 1:
            near_send(0, 1, 0)
    for cp in l_g:
        cp.wait()
    l_dg.wait()
    l_mg.wait()
    for k in (2, 3, 1, 0):
        pulls_of(k)
        if k == 2:
            far_send(1)
        elif k == 3:
            near_send(1, 0, 1)
        elif k == 1:
            near_send(1, 1, 0)
    pass_on(0)
    l_unitt.wait()
    l_actt.wait()
    l_ctxt.wait()
    ones = jnp.ones((16, 2048), BF)
    sum_mix = dot(ones, mg[...])[0:8]
    sum_up = dot(ones, hl[...])[0:8]
    sum_g = dot(ones, g[...])[0:8]
    gains = jnp.concatenate([vec_ref[...], sum_up, sum_g], axis=0)
    col[...] = jnp.concatenate([gains, jnp.zeros((104, 768), F32)], axis=0).T

    grads[0, :, 0:768] = jnp.zeros((768, 768), BF)
    grads[0, out_rows, 0:768] = dot(ctxt[...], g[...]).astype(BF)
    mixcol[...] = jnp.concatenate([sum_mix, jnp.zeros((120, 576), F32)], axis=0).T
    lane = iota((192, 192), 1)
    bias = jnp.zeros((192, 192), F32)
    for n in range(3):
        bias = jnp.where(lane == 6 + n, mixcol[pl.ds(n, 192, stride=3), 0:1], bias)

    def gradients_of(zone):
        r = pl.ds(pl.multiple_of(zone * 192, 64), 192)
        cols = col[r]

        def over_tokens(a, b):
            return sum(dot(a[n, r], b[n * 512 : n * 512 + 512]) for n in range(4))

        u1 = over_tokens(unitt, mg)
        wm = w[0, r, 768:1344].astype(F32)
        gain1 = jnp.sum(wm * u1, axis=-1, keepdims=True)
        shift1 = jnp.sum(wm * sum_mix[0:1], axis=-1, keepdims=True)
        dmix = u1 * cols[:, 0:1] + cols[:, 1:2] * sum_mix[0:1]
        u2 = over_tokens(unitt, hl)
        wu = w[1, r, 0:768].astype(F32)
        gain2 = jnp.sum(wu * u2, axis=-1, keepdims=True)
        shift2 = jnp.sum(wu * sum_up[0:1], axis=-1, keepdims=True)
        grads[1, r, 0:768] = (u2 * cols[:, 2:3] + cols[:, 3:4] * sum_up[0:1]).astype(BF)
        grads[1, r, 768:] = over_tokens(actt, g).astype(BF)
        small = jnp.where(zone == x, bias, 0.0)
        for n, v in enumerate((gain1, shift1, gain2, shift2, cols[:, 16:17], cols[:, 8:9])):
            small = jnp.where(lane == n, v, small)
        grads[0, r, 768:1536] = jnp.concatenate([dmix, small], axis=1).astype(BF)

    def block_rows(zone, b):
        return pl.ds(pl.multiple_of((zone * 4 + b) * PAIR, 16), PAIR)

    def add_sibling(zone):
        for b in range(4):
            r = block_rows(zone, b)
            landed(first_in.at[r], r0.at[zone, b])
            grads[c, r] = (grads[c, r].astype(F32) + first_in[r].astype(F32)).astype(BF)
            one, two = jnp.where(is0, zone, b), jnp.where(is0, b, zone)
            k = lax.rem(one + 4 - here1, 4)

            @pl.when(k != 0)
            def _():
                remote(
                    grads.at[c, r], second_in.at[k - 1, two], s1.at[k - 1, two], r1.at[k - 1, two], first(k)
                ).start()

    order = (1, 3, 2, 0)
    zones = [lax.rem(z + k, 4) for k in order]
    for n, zone in enumerate(zones):
        gradients_of(zone)
        for b in range(4):
            r = block_rows(zone, b)
            send(grads.at[1 - c, r], first_in.at[r], s0.at[zone, b], r0.at[zone, b], sibling)
        if n:
            add_sibling(zones[n - 1])
    add_sibling(zones[3])
    pass_on(1)
    lane = iota((1, WIDE), 1)
    group = lax.rem(lax.div(lane, 24), 4)
    source = lax.div(lane, 96) * 24 + lax.rem(lane, 24)
    for d in range(4):
        hot = iota((384, WIDE), 0) == jnp.where(group == d, source, -1)
        w[d // 2, (d % 2) * 384 : (d % 2) * 384 + 384] = hot.astype(F32).astype(BF)
    for j in order:
        b = lax.rem(here2 + j, 4)
        r = rows(here1, b, False)
        acc = grads[c, r].astype(F32)
        for k in (1, 3, 2):
            landed(second_in.at[k - 1, b], r1.at[k - 1, b])
            acc = acc + second_in[k - 1, b].astype(F32)
        part[j] = acc.astype(BF)
        if j:
            send(part.at[j], third_in.at[j - 1], s2.at[j - 1], r2.at[j - 1], second(j))
    for h in range(2):
        o = total(0, h) + rows_ref[half[h]].astype(F32) + vec_ref[4:5]
        out_ref[half[h]] = o
    acc = part[0].astype(F32)
    for j in (1, 3, 2):
        landed(third_in.at[j - 1], r2.at[j - 1])
        acc = acc + third_in[j - 1].astype(F32)
    fin_ref[c, x] = acc.astype(BF)
    for k in (1, 3, 2):
        slot = fin_ref.at[c, x]
        send(slot, slot, s3.at[k - 1], r3.at[k - 1], (lax.rem(x + k, 4), me))
    slot = fin_ref.at[c, x]
    send(slot, slot, s4.at[0], r4.at[0], sibling)
    for h in range(2):
        s = total(1, h)
        v = rows_ref[half[h]].astype(F32)
        v = v - jnp.mean(v, axis=-1, keepdims=True)
        inverse = lax.rsqrt(jnp.mean(v * v, axis=-1, keepdims=True) + 1e-05)
        unit = v * inverse
        s = s - jnp.mean(s, axis=-1, keepdims=True) - unit * jnp.mean(s * unit, axis=-1, keepdims=True)
        own = pl.ds(pl.multiple_of(x * 512 + h * 256, 256), 256)
        back_ref[half[h]] = g[own].astype(F32) + inverse * s
    for k in (1, 3, 2):
        slot = fin_ref.at[c, lax.rem(x + 4 - k, 4)]
        landed(slot, r3.at[k - 1])
        send(slot, slot, s4.at[k], r4.at[k], sibling)
    for k in range(4):
        landed(fin_ref.at[1 - c, lax.rem(x + 4 - k, 4)], r4.at[k])

    def mine(role, d, a, b):
        v = fin_ref[role, d, :, a:b].astype(F32)
        return jnp.where(is0, v[0:24], v[24:48])

    wout_ref[...] = sum(mine(0, d, 0, 768) for d in range(4))
    tails = [mine(0, d, 768, WIDE) for d in range(4)]
    wmix_ref[...] = jnp.concatenate([t[:, 0:576] for t in tails], axis=1)
    lane = iota((24, 128), 1)
    small = sum(t[:, 576:704] for t in tails)
    for d in range(4):
        small = jnp.where(lane == 16 + d, tails[d][:, 581:582], small)
    small = jnp.where(lane == 4, tails[0][:, 576:704], small)
    small_ref[...] = jnp.concatenate([small, jnp.zeros((104, 128), F32)], axis=0).T[0:24]
    ups = [mine(1, d, 0, 768).astype(BF) for d in range(4)]
    for n in range(2):
        wup_ref[:, n * WIDE : n * WIDE + WIDE] = sum(
            dot(ups[d][:, n * 384 : n * 384 + 384], w[d // 2, (d % 2) * 384 : (d % 2) * 384 + 384])
            for d in range(4)
        )
    for d in range(4):
        wdown_ref[d * 24 : d * 24 + 24] = mine(1, d, 768, WIDE)
    for cp in started:
        cp.wait_send()
    for k in range(3):
        for b in range(4):
            remote(second_in.at[k, b], second_in.at[k, b], s1.at[k, b], r1.at[k, b], sibling).wait_send()


def tail(ctx, ctxt, mg, act, actt, dg, unitt, w, vec, g, rows):
    vm = pl.BlockSpec(memory_space=pltpu.VMEM)
    hbm = pl.BlockSpec(memory_space=pl.ANY)
    dma = pltpu.SemaphoreType.DMA
    return pl.pallas_call(
        tail_kernel,
        out_shape=(
            jax.ShapeDtypeStruct((512, 768), F32),
            jax.ShapeDtypeStruct((512, 768), F32),
            jax.ShapeDtypeStruct((24, 768), F32),
            jax.ShapeDtypeStruct((24, 2304), F32),
            jax.ShapeDtypeStruct((24, 3072), F32),
            jax.ShapeDtypeStruct((96, 768), F32),
            jax.ShapeDtypeStruct((24, 128), F32),
        ),
        in_specs=[hbm] * 8 + [vm] + [hbm] * 4 + [vm],
        out_specs=[vm] * 7,
        scratch_shapes=[
            pltpu.VMEM((2048, 192), BF),
            pltpu.VMEM((192, 2048), BF),
            pltpu.VMEM((2048, 576), BF),
            pltpu.VMEM((2048, 768), BF),
            pltpu.VMEM((4, 768, 512), BF),
            pltpu.VMEM((2048, 768), BF),
            pltpu.VMEM((4, 768, 512), BF),
            pltpu.VMEM((2, 768, WIDE), BF),
            pltpu.VMEM((2048, 768), BF),
            pltpu.VMEM((2, 4, 512, 768), BF),
            pltpu.VMEM((2, 2, 256, 768), BF),
            pltpu.VMEM((2, 2, 512, 768), BF),
            pltpu.VMEM((2, 768, WIDE), BF),
            pltpu.VMEM((768, WIDE), BF),
            pltpu.VMEM((3, 4, PAIR, WIDE), BF),
            pltpu.VMEM((4, PAIR, WIDE), BF),
            pltpu.VMEM((3, PAIR, WIDE), BF),
            pltpu.VMEM((2, 4, PAIR, WIDE), BF),
            pltpu.VMEM((768, 128), F32),
            pltpu.VMEM((576, 128), F32),
            dma((12,)),
            dma((2, 2)), dma((2, 2)), dma((2, 2, 2)), dma((2, 2, 2)),
            dma((4, 4)), dma((4, 4)), dma((3, 4)), dma((3, 4)), dma((3,)), dma((3,)),
            dma((3,)), dma((3,)), dma((4,)), dma((4,)),
        ],
        compiler_params=pltpu.CompilerParams(
            collective_id=1, has_side_effects=True, vmem_limit_bytes=60 * 1024 * 1024
        ),
        name="tail_all",
    )(ctx, ctxt, mg, act, actt, dg, unitt, w, vec, *g, rows)


def shift_x(v, k):
    return lax.ppermute(v, "seq", [(i, (i + k) % NX) for i in range(NX)])


def local(
    inputs, positions, first_gain, first_shift, second_gain, second_shift, mix_weight, mix_bias,
    out_weight, out_bias, up_weight, up_bias, down_weight, down_bias, cotangent,
):
    flat = jnp.zeros((384,), BF)
    for place, v in (
        (0, first_gain), (24, first_shift), (48, second_gain), (72, second_shift), (96, out_bias),
        (120, down_bias), (192, mix_bias), (264, up_bias),
    ):
        flat = flat + jnp.pad(v, (place, 384 - place - v.shape[0]))
    packed = jnp.pad(flat.reshape(2, 192), ((0, 22), (0, 0)))
    grad = cotangent[0]
    mixed, act, actt, slope, unitt, context_grad, w, vec, table = front(
        inputs[0], grad, positions, packed, mix_weight, out_weight, up_weight, down_weight
    )
    late, table = lax.optimization_barrier((grad, table))
    grads = [grad] + [shift_x(late, k) for k in (1, 2, 3)]
    context, context_t, mix_grad = attention(mixed, table, context_grad)
    outputs, input_grad, g_out, g_mix, g_up, g_down, small = tail(
        context, context_t, mix_grad, act, actt, slope, unitt, w, vec, grads, inputs[0]
    )
    return (
        outputs.astype(BF)[None],
        input_grad.astype(BF)[None],
        small[0, :24],
        small[1, :24],
        small[2, :24],
        small[3, :24],
        g_mix,
        small[6:9, :24].T.reshape(72),
        g_out,
        small[4, :24],
        g_up,
        small[16:20, :24].reshape(96),
        g_down,
        small[4, :24],
    )


def solution(mesh):
    vec, mat, tok = P("shard"), P("shard", None), P("shard", "seq", None)
    return jax.shard_map(
        local,
        mesh=mesh,
        in_specs=(tok, P("shard", "seq"), vec, vec, vec, vec, mat, vec, mat, vec, mat, vec, mat, vec, tok),
        out_specs=(tok, tok, vec, vec, vec, vec, mat, vec, mat, vec, mat, vec, mat, vec),
        check_vma=False,
    )
```
